256 devices in a mesh: row: 16 (over z, core), col: 16 (over y, x).
Axes of the slice: x: 4, y: 4, z: 8, core: 2. Of those that a mesh axis runs over, the one named last changes fastest.
Arguments:
- points: bfloat16 [16384, 1024], P(('row', 'col')), may hold values from -6 to 6
- factor: float32 [16384, 256], P(('row', 'col')), may hold values from 0 to 1
Outputs:
- factor_out: float32 [16384, 256], P(('row', 'col'))
The draws below stay inside these ranges and needn't reach their ends.
All inputs are finite; a program needn't handle non-finite values.
Results may differ from the reference program's by a relative error of at most 0.002.
The reference program's roundings to bfloat16 on the way count: a program that leaves them out, or rounds other values in their place, can miss the bound.
Values may be sent and summed in bfloat16 or wider, within the bound.
No kernel may reach another device: no remote copies, remote signals or barrier semaphores. Data moves between devices by JAX's collectives and lax.ppermute only.
A program may use at most 64 MiB of HBM per device.

```python
import math
import jax
import jax.numpy as jnp
from jax import lax

EMBED_WIDTH = 1024
R = 256
ITERS = 2
NPTS = 16384


def level_of(key, shape, split, least, top_value):
    factor_of, own = 1.0, jax.random.fold_in(key, 6)
    for axis_at, blocks in split:
        steps = jnp.exp(jax.random.uniform(jax.random.fold_in(own, axis_at), (blocks,), jnp.float32, least / len(split), top_value / len(split)))
        factor_of = factor_of * jnp.repeat(steps, shape[axis_at] // blocks).reshape([-1 if axis == axis_at else 1 for axis in range(len(shape))])
    return factor_of


def gaussian(rng, dims, spread, reach, shards=(), kind=jnp.bfloat16):
    entries = jax.random.normal(rng, dims, jnp.float32) * spread
    if len(shards) > 0:
        entries = level_of(rng, dims, shards, -0.22, 0.18) * entries
    return jnp.clip(entries, min=-reach, max=reach).astype(kind)


def setup_inputs(seed: int = 0) -> dict:
    arg_keys = jax.random.split(jax.random.key(seed), 3)
    points = gaussian(arg_keys[0], (NPTS, EMBED_WIDTH), 1.0, 6.0, ((0, 256),))
    factor = jnp.clip(1.0 * jax.random.uniform(arg_keys[1], (NPTS, R), jnp.float32) ** level_of(arg_keys[1], (NPTS, R), ((0, 256),), -0.2, 0.2), 0.0, 1.0)
    return dict(points=points, factor=factor)


def reference(points, factor):
    data = points.astype(jnp.float32)
    total = data.shape[0]
    rank = factor.shape[1]
    block_slab = math.gcd(512, total)
    nblocks = total // block_slab
    squared_norms = lax.optimization_barrier(jnp.sum(data * data, axis=1))

    def kernel_row_slab(index):
        offset_begin = (index * block_slab).astype(jnp.int32)
        rows = lax.dynamic_slice_in_dim(data, offset_begin, block_slab, 0)
        row_squared_norm = lax.dynamic_slice_in_dim(squared_norms, offset_begin, block_slab, 0)
        gram_matrix = jnp.dot(rows, data.T, precision=lax.Precision.HIGHEST)
        return jnp.exp((2.0 * gram_matrix - row_squared_norm[:, None] - squared_norms[None, :]) * (0.5 / EMBED_WIDTH))
    indices = jnp.arange(nblocks, dtype=jnp.int32)
    rowsum = lax.map(lambda i: lax.optimization_barrier(jnp.sum(kernel_row_slab(i), axis=1)), indices).reshape(total)
    grand = jnp.sum(rowsum)
    means = rowsum / total

    def affinity_rows(index):
        offset_begin = (index * block_slab).astype(jnp.int32)
        kern = kernel_row_slab(index)
        mine = lax.dynamic_slice_in_dim(means, offset_begin, block_slab, 0)
        return (kern - mine[:, None] - means[None, :] + grand / (total * total)).astype(jnp.bfloat16)
    unit = 2.0 / math.sqrt(total * rank)
    h = factor * unit
    for step in range(ITERS):
        hb = lax.optimization_barrier(h.astype(jnp.bfloat16)).astype(jnp.float32)
        ah = lax.map(lambda i: jnp.dot(affinity_rows(i).astype(jnp.float32), hb, precision=lax.Precision.HIGHEST), indices).reshape(total, rank)
        hh = jnp.dot(h.T, h, precision=lax.Precision.HIGHEST)
        scale = 0.5 / jnp.sqrt(jnp.sum(hh * hh) + 1e-06)
        h = jnp.maximum(h - scale * (jnp.dot(h, hh, precision=lax.Precision.HIGHEST) - ah), 0.0)
    return h / unit
```

```python
import math

import jax
import jax.numpy as jnp
from jax import lax
from jax.sharding import Mesh
from jax.sharding import PartitionSpec as P

EMBED_WIDTH = 1024
ITERS = 2
Z, CORE, Y, X = "row_0", "row_1", "col_0", "col_1"
ROW = (Z, CORE)
COL = (Y, X)
ROW_COL = (Z, CORE, Y, X)


def from_ahead(value, axis, steps):
    length = lax.axis_size(axis)
    return lax.ppermute(value, axis, [((i + steps) % length, i) for i in range(length)])


def to_ahead(value, axis, steps):
    length = lax.axis_size(axis)
    return lax.ppermute(value, axis, [(i, (i + steps) % length) for i in range(length)])


def all_ahead(value, axis):
    length = lax.axis_size(axis)
    return jnp.stack([value] + [from_ahead(value, axis, s) for s in range(1, length)])


def sent_to_all(value, axes):
    length = math.prod(lax.axis_size(a) for a in axes)
    copies = jnp.broadcast_to(value, (length, *value.shape))
    return lax.all_to_all(copies, axes, split_axis=0, concat_axis=0, tiled=True)


def to_own_place(value, dim, axis):
    return jnp.roll(value, lax.axis_index(axis), dim)


def from_own_place(value, dim, axis):
    return jnp.roll(value, -lax.axis_index(axis), dim)


def column_order(value):
    half = value.shape[2] // 2
    first = value[:, :, :half]
    second = jnp.swapaxes(value[:, :, half:], 0, 1)
    rest = value.shape[3:]
    return jnp.concatenate([first.reshape(-1, *rest), second.reshape(-1, *rest)])


def shards(points, factor):
    nz, ncore, ny, nx = (lax.axis_size(a) for a in ROW_COL)
    nrow, ncol = nz * ncore, ny * nx
    pts, rank = factor.shape
    total = pts * nrow * ncol
    unit = 2.0 / math.sqrt(total * rank)
    h = factor * unit
    hb = h.astype(jnp.bfloat16)
    width = points.shape[1]
    half = pts // 2

    both = jnp.concatenate([points, hb], axis=1)
    by_x = all_ahead(both[:half], X)
    by_y = all_ahead(both[half:], Y)
    along_z = all_ahead(points, Z)
    cols = jnp.concatenate(
        [all_ahead(by_x, Y).reshape(-1, width + rank), all_ahead(by_y, X).reshape(-1, width + rank)]
    )
    other = from_ahead(along_z, CORE, 1)
    rows = jnp.stack([along_z, other]).reshape(-1, width)
    col_pts, hb_cols = cols[:, :width], cols[:, width:]

    gram_matrix = lax.dot_general(
        rows, col_pts, (((1,), (1,)), ((), ())), preferred_element_type=jnp.float32
    )
    row_sq = jnp.sum(jnp.square(rows.astype(jnp.float32)), axis=1)
    col_sq = jnp.sum(jnp.square(col_pts.astype(jnp.float32)), axis=1)
    kern = jnp.exp((2.0 * gram_matrix - row_sq[:, None] - col_sq[None, :]) * (0.5 / EMBED_WIDTH))

    own_col = lax.axis_index(COL)
    own_row = lax.axis_index(ROW)
    part = rank // ncol

    def gram_part(cols_b):
        whole = lax.dot_general(
            cols_b, cols_b, (((0,), (0,)), ((), ())), preferred_element_type=jnp.float32
        )
        return lax.dynamic_slice_in_dim(whole, own_col * part, part, 0)

    row_sum = jnp.sum(kern, axis=1).reshape(ncore, nz, pts)
    placed = jnp.swapaxes(to_own_place(to_own_place(row_sum, 0, CORE), 1, Z), 0, 1)
    message = jnp.concatenate([placed.reshape(-1, rank), gram_part(hb_cols)])
    summed = jnp.sum(sent_to_all(message, ROW), axis=0)
    lines = nrow * pts // rank
    mean_rows = summed[:lines].reshape(nz, ncore, pts) / total
    own_mean = lax.dynamic_slice_in_dim(mean_rows.reshape(nrow, pts), own_row, 1, 0)
    band = jnp.full((1, rank - pts), jnp.sum(mean_rows))
    message = jnp.concatenate([jnp.concatenate([own_mean, band], axis=1), summed[lines:]])
    gathered = sent_to_all(message, COL)
    hh = gathered[:, 1:].reshape(rank, rank)
    grand = jnp.sum(gathered[:, 0, pts]) / total
    mean_cols = gathered[:, 0, :pts].reshape(ny, nx, pts)
    mean_cols = column_order(from_own_place(from_own_place(mean_cols, 0, Y), 1, X))
    mean_rows = from_own_place(from_own_place(jnp.swapaxes(mean_rows, 0, 1), 0, CORE), 1, Z)
    affinity = (kern - mean_rows.reshape(-1)[:, None] - mean_cols[None, :] + grand).astype(
        jnp.bfloat16
    )

    def summed_rows(partial, extra):
        partial = partial.reshape(ncore, nz, pts, rank)
        if extra is None:
            mine = partial[0] + from_ahead(partial[1], CORE, 1)
            return mine[0] + sum(to_ahead(mine[s], Z, s) for s in range(1, nz)), None
        extras = jnp.concatenate([partial[1].reshape(-1, rank), extra])
        extras = from_ahead(extras, CORE, 1)
        mine = partial[0] + extras[: nz * pts].reshape(nz, pts, rank)
        extra = extra + extras[nz * pts :]
        own = jnp.concatenate([mine[0], extra])
        own = own + sum(
            to_ahead(jnp.concatenate([mine[s], extra]), Z, s) for s in range(1, nz)
        )
        return own[:pts], own[pts:]

    for step in range(ITERS):
        partial = jnp.dot(affinity, hb_cols, preferred_element_type=jnp.float32)
        if step == 0:
            ah, _ = summed_rows(partial, None)
        else:
            ah, own_part = summed_rows(partial, gram_part(hb_cols))
            hh = sent_to_all(own_part, COL).reshape(rank, rank)
        scale = 0.5 / jnp.sqrt(jnp.sum(hh * hh) + 1e-06)
        h = jnp.maximum(h - scale * (jnp.dot(h, hh, precision=lax.Precision.HIGHEST) - ah), 0.0)
        if step + 1 < ITERS:
            hb_cols = column_order(all_ahead(all_ahead(h.astype(jnp.bfloat16), X), Y))
    return h / unit


def solution(mesh):
    split = Mesh(mesh.devices.reshape(8, 2, 4, 4), ROW_COL)
    return jax.shard_map(
        shards,
        mesh=split,
        in_specs=(P(ROW_COL, None), P(ROW_COL, None)),
        out_specs=P(ROW_COL, None),
        check_vma=False,
    )
```

```python
import math

import jax
import jax.numpy as jnp
from jax import lax
from jax.sharding import Mesh
from jax.sharding import PartitionSpec as P

EMBED_WIDTH = 1024
ITERS = 2
Z, CORE, Y, X = "row_0", "row_1", "col_0", "col_1"
ROW = (Z, CORE)
COL = (Y, X)
ROW_COL = (Z, CORE, Y, X)


def from_ahead(value, axis, steps):
    length = lax.axis_size(axis)
    return lax.ppermute(value, axis, [((i + steps) % length, i) for i in range(length)])


def to_ahead(value, axis, steps):
    length = lax.axis_size(axis)
    return lax.ppermute(value, axis, [(i, (i + steps) % length) for i in range(length)])


def all_ahead(value, axis):
    length = lax.axis_size(axis)
    return jnp.stack([value] + [from_ahead(value, axis, s) for s in range(1, length)])


def sent_to_all(value, axes):
    length = math.prod(lax.axis_size(a) for a in axes)
    copies = jnp.broadcast_to(value, (length, *value.shape))
    return lax.all_to_all(copies, axes, split_axis=0, concat_axis=0, tiled=True)


def to_own_place(value, dim, axis):
    return jnp.roll(value, lax.axis_index(axis), dim)


def from_own_place(value, dim, axis):
    return jnp.roll(value, -lax.axis_index(axis), dim)


def column_order(value):
    half = value.shape[2] // 2
    first = value[:, :, :half]
    second = jnp.swapaxes(value[:, :, half:], 0, 1)
    rest = value.shape[3:]
    return jnp.concatenate([first.reshape(-1, *rest), second.reshape(-1, *rest)])


def shards(points, factor):
    nz, ncore, ny, nx = (lax.axis_size(a) for a in ROW_COL)
    nrow, ncol = nz * ncore, ny * nx
    pts, rank = factor.shape
    total = pts * nrow * ncol
    unit = 2.0 / math.sqrt(total * rank)
    h = factor * unit
    hb = h.astype(jnp.bfloat16)
    width = points.shape[1]
    half = pts // 2

    both = jnp.concatenate([points, hb], axis=1)
    first, second = both[:half], both[half:]
    by_x = [from_ahead(first, X, s) for s in (1, 3, 2)]
    by_y = [from_ahead(second, Y, s) for s in (1, 3, 2)]
    z1, z7 = from_ahead(points, Z, 1), from_ahead(points, Z, -1)
    by_x, by_y, z1, z7 = lax.optimization_barrier((by_x, by_y, z1, z7))
    by_x = jnp.stack([first, by_x[0], by_x[2], by_x[1]])
    by_y = jnp.stack([second, by_y[0], by_y[2], by_y[1]])
    z23 = from_ahead(jnp.stack([points, z1]), Z, 2)
    z65 = from_ahead(jnp.stack([points, z7]), Z, -2)
    z4 = from_ahead(z23[1], Z, 1)
    cols = [by_x] + [from_ahead(by_x, Y, s) for s in (1, 3, 2)]
    cols += [by_y] + [from_ahead(by_y, X, s) for s in (1, 3, 2)]
    cols = [cols[i].reshape(-1, width + rank) for i in (0, 1, 3, 2, 4, 5, 7, 6)]
    cols = jnp.concatenate(cols)
    along_z = jnp.stack([points, z1, z23[0], z23[1], z4, z65[1], z65[0], z7])
    along_z = to_own_place(along_z, 0, Z)
    other = from_ahead(along_z, CORE, 1)
    rows = jnp.stack([along_z, other]).reshape(-1, width)
    col_pts, hb_cols = cols[:, :width], cols[:, width:]

    gram_matrix = lax.dot_general(
        rows, col_pts, (((1,), (1,)), ((), ())), preferred_element_type=jnp.float32
    )
    row_sq = jnp.sum(jnp.square(rows.astype(jnp.float32)), axis=1)
    col_sq = jnp.sum(jnp.square(col_pts.astype(jnp.float32)), axis=1)
    kern = jnp.exp((2.0 * gram_matrix - row_sq[:, None] - col_sq[None, :]) * (0.5 / EMBED_WIDTH))

    own_col = lax.axis_index(COL)
    own_row = lax.axis_index(ROW)
    part = rank // ncol

    def gram_part(cols_b):
        whole = lax.dot_general(
            cols_b, cols_b, (((0,), (0,)), ((), ())), preferred_element_type=jnp.float32
        )
        return lax.dynamic_slice_in_dim(whole, own_col * part, part, 0)

    row_sum = jnp.sum(kern, axis=1).reshape(ncore, nz, pts)
    placed = jnp.swapaxes(to_own_place(row_sum, 0, CORE), 0, 1)
    message = jnp.concatenate([placed.reshape(-1, rank), gram_part(hb_cols)])
    summed = jnp.sum(sent_to_all(message, ROW), axis=0)
    lines = nrow * pts // rank
    mean_rows = summed[:lines].reshape(nz, ncore, pts) / total
    own_mean = lax.dynamic_slice_in_dim(mean_rows.reshape(nrow, pts), own_row, 1, 0)
    band = jnp.full((1, rank - pts), jnp.sum(mean_rows))
    message = jnp.concatenate([jnp.concatenate([own_mean, band], axis=1), summed[lines:]])
    gathered = sent_to_all(message, COL)
    hh = gathered[:, 1:].reshape(rank, rank)
    grand = jnp.sum(gathered[:, 0, pts]) / total
    mean_cols = gathered[:, 0, :pts].reshape(ny, nx, pts)
    mean_cols = column_order(from_own_place(from_own_place(mean_cols, 0, Y), 1, X))
    mean_rows = from_own_place(jnp.swapaxes(mean_rows, 0, 1), 0, CORE)
    affinity = (kern - mean_rows.reshape(-1)[:, None] - mean_cols[None, :] + grand).astype(
        jnp.bfloat16
    )

    def summed_rows(partial, extra):
        partial = partial.reshape(ncore, nz, pts, rank)
        if extra is None:
            mine = partial[0] + from_ahead(partial[1], CORE, 1)
        else:
            sent = jnp.concatenate([partial[1].reshape(-1, rank), extra])
            got = from_ahead(sent, CORE, 1)
            mine = partial[0] + got[: nz * pts].reshape(nz, pts, rank)
            extra = jnp.broadcast_to(extra + got[nz * pts :], (nz, *extra.shape))
            mine = jnp.concatenate([mine, extra], axis=1)
        own = jnp.sum(lax.all_to_all(mine, Z, 0, 0, tiled=True), axis=0)
        return own[:pts], own[pts:]

    for step in range(ITERS):
        partial = jnp.dot(affinity, hb_cols, preferred_element_type=jnp.float32)
        if step == 0:
            ah, _ = summed_rows(partial, None)
        else:
            ah, own_part = summed_rows(partial, gram_part(hb_cols))
            hh = sent_to_all(own_part, COL).reshape(rank, rank)
        scale = 0.5 / jnp.sqrt(jnp.sum(hh * hh) + 1e-06)
        h = jnp.maximum(h - scale * (jnp.dot(h, hh, precision=lax.Precision.HIGHEST) - ah), 0.0)
        if step + 1 < ITERS:
            hb_cols = column_order(all_ahead(all_ahead(h.astype(jnp.bfloat16), X), Y))
    return h / unit


def solution(mesh):
    split = Mesh(mesh.devices.reshape(8, 2, 4, 4), ROW_COL)
    return jax.shard_map(
        shards,
        mesh=split,
        in_specs=(P(ROW_COL, None), P(ROW_COL, None)),
        out_specs=P(ROW_COL, None),
        check_vma=False,
    )
```

```python
import functools
import math

import jax
import jax.numpy as jnp
from jax import lax
from jax.experimental import pallas as pl
from jax.experimental.pallas import tpu as pltpu
from jax.sharding import Mesh
from jax.sharding import PartitionSpec as P

EMBED_WIDTH = 1024
Z, CORE, Y, X = "row_0", "row_1", "col_0", "col_1"
ROW = (Z, CORE)
COL = (Y, X)
ROW_COL = (Z, CORE, Y, X)


def from_ahead(value, axis, steps):
    length = lax.axis_size(axis)
    return lax.ppermute(value, axis, [((i + steps) % length, i) for i in range(length)])


def sent_to_all(value, axes):
    length = math.prod(lax.axis_size(a) for a in axes)
    copies = jnp.broadcast_to(value, (length, *value.shape))
    return lax.all_to_all(copies, axes, split_axis=0, concat_axis=0, tiled=True)


F32, BF16 = jnp.float32, jnp.bfloat16
VMEM = pl.BlockSpec(memory_space=pltpu.VMEM)
LANES = 128


def call(kernel, outs, args, flops, scratch=(), vmem=24):
    size = sum(math.prod(a.shape) * a.dtype.itemsize for a in (*outs, *args))
    return pl.pallas_call(
        kernel,
        out_shape=outs,
        in_specs=[VMEM] * len(args),
        out_specs=[VMEM] * len(outs),
        scratch_shapes=list(scratch),
        compiler_params=pltpu.CompilerParams(vmem_limit_bytes=vmem << 20),
        cost_estimate=pl.CostEstimate(flops=flops, bytes_accessed=size, transcendentals=0),
    )(*args)


def rows_dot(a, b):
    return lax.dot_general(a, b, (((1,), (1,)), ((), ())), preferred_element_type=F32)


def squares(rows):
    wide = rows.astype(F32)
    groups = [wide[:, g : g + LANES] for g in range(0, rows.shape[1], LANES)]
    return sum(g * g for g in groups)


def columns_kernel(by_x, y1, y2, y3, by_y, x1, x2, x3, pts_ref, hb_ref, sq_ref, part_ref, gram_ref):
    ny, nx = lax.axis_size(Y), lax.axis_size(X)
    y, x = lax.axis_index(Y), lax.axis_index(X)
    half = by_x.shape[1]
    width = pts_ref.shape[1]
    for far, ref in enumerate((by_x, y1, y2, y3)):
        for near in range(nx):
            at = lax.rem(y + far, ny) * nx + lax.rem(x + near, nx)
            at = pl.multiple_of(at * 2 * half, half)
            pts_ref[pl.ds(at, half), :] = ref[near, :, :width]
            hb_ref[pl.ds(at, half), :] = ref[near, :, width:]
    for far, ref in enumerate((by_y, x1, x2, x3)):
        for near in range(ny):
            at = lax.rem(y + near, ny) * nx + lax.rem(x + far, nx)
            at = pl.multiple_of(at * 2 * half + half, half)
            pts_ref[pl.ds(at, half), :] = ref[near, :, :width]
            hb_ref[pl.ds(at, half), :] = ref[near, :, width:]
    for block in range(pts_ref.shape[0] // LANES):
        sums = squares(pts_ref[block * LANES : (block + 1) * LANES, :])
        sq_ref[block : block + 1, :] = jnp.sum(sums.T, axis=0, keepdims=True)
    gram_ref[...] = lax.dot_general(
        hb_ref[...], hb_ref[...], (((0,), (0,)), ((), ())), preferred_element_type=F32
    )
    part = part_ref.shape[0]
    at = pl.multiple_of((y * nx + x) * part, part)
    part_ref[...] = gram_ref[pl.ds(at, part), :]


def rows_kernel(
    p0, p1, p23, p4, p65, p7, o0, o1, o23, o4, o65, o7, cols, sq, kern, sums, held
):
    z, core = lax.axis_index(Z), lax.axis_index(CORE)
    nz, pts = lax.axis_size(Z), p0.shape[0]

    def put(which, steps, value):
        at = (which * nz + lax.rem(z + steps, nz)) * pts
        held[pl.ds(pl.multiple_of(at, pts), pts), :] = value

    for which, refs in ((core, (p0, p1, p23, p4, p65, p7)), (1 - core, (o0, o1, o23, o4, o65, o7))):
        put(which, 0, refs[0][...])
        put(which, 1, refs[1][...])
        put(which, 2, refs[2][0])
        put(which, 3, refs[2][1])
        put(which, 4, refs[3][...])
        put(which, 5, refs[4][1])
        put(which, 6, refs[4][0])
        put(which, 7, refs[5][...])
    col_sq = jnp.concatenate([sq[g : g + 1, :] for g in range(sq.shape[0])], axis=1)
    tall = 2 * LANES

    def block(i, _):
        at = pl.ds(pl.multiple_of(i * tall, tall), tall)
        rows = held[at, :]
        row_sq = jnp.sum(squares(rows), axis=1, keepdims=True)
        gram = rows_dot(rows, cols[...])
        values = jnp.exp((2.0 * gram - row_sq - col_sq) * (0.5 / EMBED_WIDTH))
        kern[at, :] = values
        total = sum(values[:, g : g + LANES] for g in range(0, values.shape[1], LANES))
        for j in range(2):
            line = jnp.sum(total[j * LANES : (j + 1) * LANES].T, axis=0, keepdims=True)
            sums[pl.ds(i * 2 + j, 1), :] = line
        return 0

    lax.fori_loop(0, held.shape[0] // tall, block, 0)


def means_kernel(got, mean_ref, out):
    z, core = lax.axis_index(Z), lax.axis_index(CORE)
    n = got.shape[0]
    lines = mean_ref.shape[0]
    total = lines * LANES * n
    even, odd = got[0], got[1]
    for i in range(2, n, 2):
        even, odd = even + got[i], odd + got[i + 1]
    sums = even + odd
    means = sums[:lines] / total
    mean_ref[...] = means
    own = mean_ref[pl.ds((core * lax.axis_size(Z) + z) // 2, 1), :]
    band = jnp.broadcast_to(jnp.sum(means, keepdims=True), (1, LANES))
    fill = jnp.zeros((lines - 2, LANES), F32)
    deep = (got.shape[1] - lines) // 2
    pieces = [own, band, fill]
    for at in (lines, lines + deep):
        pieces += [even[at : at + deep], odd[at : at + deep]]
    whole = jnp.concatenate(pieces, axis=0)
    for i in range(out.shape[0]):
        out[i] = whole


def centred_kernel(own, kern, mean_ref, got, hb, aff, partial, *hh):
    z, core = lax.axis_index(Z), lax.axis_index(CORE)
    n = got.shape[0]
    total = mean_ref.shape[0] * LANES * n
    which = core if own else 1 - core
    grand = got[0, 1:2, :]
    for i in range(1, n):
        grand = grand + got[i, 1:2, :]
    grand = grand / total
    lane = lax.broadcasted_iota(jnp.int32, (1, LANES), 1)
    odd = lax.rem(z, 2) == 1
    places = []
    for i in range(0, n, 2):
        pair = []
        for j in range(2):
            line = got[i + j, 0:1, :]
            swapped = pltpu.roll(line, LANES // 2, 1)
            pair.append(jnp.where(odd if j == 0 else jnp.logical_not(odd), swapped, line))
        places.append(jnp.where(lane < LANES // 2, pair[0], pair[1]))
    lines = mean_ref.shape[0] // 2
    rows = aff.shape[0]
    for i in range(lines):
        line = mean_ref[pl.ds(which * lines + i, 1), :]
        mine = jnp.broadcast_to(line, (LANES, LANES)).T
        at = pl.ds(pl.multiple_of(which * rows + i * LANES, LANES), LANES)
        for g, place in enumerate(places):
            values = kern[at, g * LANES : (g + 1) * LANES]
            values = values - mine - place + grand
            aff[i * LANES : (i + 1) * LANES, g * LANES : (g + 1) * LANES] = values.astype(BF16)
    partial[...] = jnp.dot(aff[...], hb[...], preferred_element_type=F32)
    if hh:
        deep = (got.shape[1] - 8) // 2
        for i in range(n):
            hh[0][i * deep : (i + 1) * deep, :LANES] = got[i, 8 : 8 + deep, :]
            hh[0][i * deep : (i + 1) * deep, LANES:] = got[i, 8 + deep :, :]


def shards(points, factor):
    nz, ncore, ny, nx = (lax.axis_size(a) for a in ROW_COL)
    nrow, ncol = nz * ncore, ny * nx
    pts, rank = factor.shape
    total = pts * nrow * ncol
    unit = 2.0 / math.sqrt(total * rank)
    h = factor * unit
    hb = h.astype(BF16)
    width = points.shape[1]
    half = pts // 2
    shape = jax.ShapeDtypeStruct

    both = jnp.concatenate([points, hb], axis=1)
    first, second = both[:half], both[half:]
    by_x = [from_ahead(first, X, s) for s in (1, 3, 2)]
    by_y = [from_ahead(second, Y, s) for s in (1, 3, 2)]
    z1, z7 = from_ahead(points, Z, 1), from_ahead(points, Z, -1)
    by_x, by_y, z1, z7 = lax.optimization_barrier((by_x, by_y, z1, z7))
    by_x = jnp.stack([first, by_x[0], by_x[2], by_x[1]])
    by_y = jnp.stack([second, by_y[0], by_y[2], by_y[1]])
    z23 = from_ahead(jnp.stack([points, z1]), Z, 2)
    z65 = from_ahead(jnp.stack([points, z7]), Z, -2)
    z4 = from_ahead(z23[1], Z, 1)
    cols = [by_x] + [from_ahead(by_x, Y, s) for s in (1, 2, 3)]
    cols += [by_y] + [from_ahead(by_y, X, s) for s in (1, 2, 3)]
    along_z = [points, z1, z23, z4, z65, z7]
    other = [from_ahead(v, CORE, 1) for v in along_z]

    part = rank // ncol
    group = nrow * pts
    col_pts, hb_cols, col_sq, own_part = call(
        columns_kernel,
        [
            shape((group, width), BF16),
            shape((group, rank), BF16),
            shape((group // LANES, LANES), F32),
            shape((part, rank), F32),
        ],
        cols,
        2 * group * rank * rank,
        [pltpu.VMEM((rank, rank), F32)],
    )
    own_part = own_part + from_ahead(own_part, CORE, 1)
    kern, row_sum = call(
        rows_kernel,
        [shape((group, group), F32), shape((group // LANES, LANES), F32)],
        [*along_z, *other, col_pts, col_sq],
        2 * group * group * width,
        [pltpu.VMEM((group, width), BF16)],
    )
    core_part = lax.dynamic_slice_in_dim(own_part, lax.axis_index(CORE) * (part // 2), part // 2, 0)
    message = jnp.concatenate([row_sum, core_part[:, :LANES], core_part[:, LANES:]])
    mean_rows, message = call(
        means_kernel,
        [shape(row_sum.shape, F32), shape((ncol, 8 + 2 * part, LANES), F32)],
        [sent_to_all(message, ROW)],
        1,
    )
    gathered = lax.all_to_all(message, COL, 0, 0, tiled=True)

    def centred(own):
        outs = [shape((group // 2, group), BF16), shape((group // 2, rank), F32)]
        if own:
            outs.append(shape((rank, rank), F32))
        return call(
            functools.partial(centred_kernel, own),
            outs,
            [kern, mean_rows, gathered, hb_cols],
            group * group * rank,
        )

    aff_other, partial_other = centred(False)
    got = from_ahead(partial_other, CORE, 1)
    aff_own, partial_own, hh = centred(True)

    def over_z(mine):
        return jnp.sum(lax.all_to_all(mine, Z, 0, 0, tiled=True), axis=0)

    def stepped(h, ah, hh):
        scale = 0.5 / jnp.sqrt(jnp.sum(hh * hh) + 1e-06)
        return jnp.maximum(h - scale * (jnp.dot(h, hh, precision=lax.Precision.HIGHEST) - ah), 0.0)

    ah = over_z((partial_own + got).reshape(nz, pts, rank))
    h = stepped(h, ah, hh)

    hb_cols = sent_to_all(h.astype(BF16), COL).reshape(group, rank)
    gram = lax.dot_general(hb_cols, hb_cols, (((0,), (0,)), ((), ())), preferred_element_type=F32)
    own_part = lax.dynamic_slice_in_dim(gram, lax.axis_index(COL) * part, part, 0)
    partial_other = jnp.dot(aff_other, hb_cols, preferred_element_type=F32)
    got = from_ahead(jnp.concatenate([partial_other, own_part]), CORE, 1)
    partial_own = jnp.dot(aff_own, hb_cols, preferred_element_type=F32)
    mine = (partial_own + got[: group // 2]).reshape(nz, pts, rank)
    extra = jnp.broadcast_to(own_part + got[group // 2 :], (nz, part, rank))
    own = over_z(jnp.concatenate([mine, extra], axis=1))
    hh = sent_to_all(own[pts:], COL).reshape(rank, rank)
    return stepped(h, own[:pts], hh) / unit


def solution(mesh):
    split = Mesh(mesh.devices.reshape(8, 2, 4, 4), ROW_COL)
    return jax.shard_map(
        shards,
        mesh=split,
        in_specs=(P(ROW_COL, None), P(ROW_COL, None)),
        out_specs=P(ROW_COL, None),
        check_vma=False,
    )
```

```python
import functools
import math

import jax
import jax.numpy as jnp
from jax import lax
from jax.experimental import pallas as pl
from jax.experimental.pallas import tpu as pltpu
from jax.sharding import Mesh
from jax.sharding import PartitionSpec as P

EMBED_WIDTH = 1024
Z, CORE, Y, X = "row_0", "row_1", "col_0", "col_1"
ROW = (Z, CORE)
COL = (Y, X)
ROW_COL = (Z, CORE, Y, X)


def from_ahead(value, axis, steps):
    length = lax.axis_size(axis)
    return lax.ppermute(value, axis, [((i + steps) % length, i) for i in range(length)])


def sent_to_all(value, axes):
    length = math.prod(lax.axis_size(a) for a in axes)
    copies = jnp.broadcast_to(value, (length, *value.shape))
    return lax.all_to_all(copies, axes, split_axis=0, concat_axis=0, tiled=True)


F32, BF16 = jnp.float32, jnp.bfloat16
VMEM = pl.BlockSpec(memory_space=pltpu.VMEM)
LANES = 128


def call(kernel, outs, args, flops, scratch=(), vmem=24):
    size = sum(math.prod(a.shape) * a.dtype.itemsize for a in (*outs, *args))
    return pl.pallas_call(
        kernel,
        out_shape=outs,
        in_specs=[VMEM] * len(args),
        out_specs=[VMEM] * len(outs),
        scratch_shapes=list(scratch),
        compiler_params=pltpu.CompilerParams(vmem_limit_bytes=vmem << 20),
        cost_estimate=pl.CostEstimate(flops=flops, bytes_accessed=size, transcendentals=0),
    )(*args)


def rows_dot(a, b):
    return lax.dot_general(a, b, (((1,), (1,)), ((), ())), preferred_element_type=F32)


def squares(rows):
    wide = rows.astype(F32)
    groups = [wide[:, g : g + LANES] for g in range(0, rows.shape[1], LANES)]
    return sum(g * g for g in groups)


def columns_kernel(by_x, y1, y2, y3, by_y, x1, x2, x3, pts_ref, hb_ref, sq_ref, part_ref, gram_ref):
    ny, nx = lax.axis_size(Y), lax.axis_size(X)
    y, x = lax.axis_index(Y), lax.axis_index(X)
    half = by_x.shape[1]
    width = pts_ref.shape[1]
    for far, ref in enumerate((by_x, y1, y2, y3)):
        for near in range(nx):
            at = lax.rem(y + far, ny) * nx + lax.rem(x + near, nx)
            at = pl.multiple_of(at * 2 * half, half)
            pts_ref[pl.ds(at, half), :] = ref[near, :, :width]
            hb_ref[pl.ds(at, half), :] = ref[near, :, width:]
    for far, ref in enumerate((by_y, x1, x2, x3)):
        for near in range(ny):
            at = lax.rem(y + near, ny) * nx + lax.rem(x + far, nx)
            at = pl.multiple_of(at * 2 * half + half, half)
            pts_ref[pl.ds(at, half), :] = ref[near, :, :width]
            hb_ref[pl.ds(at, half), :] = ref[near, :, width:]
    for block in range(pts_ref.shape[0] // LANES):
        sums = squares(pts_ref[block * LANES : (block + 1) * LANES, :])
        sq_ref[block : block + 1, :] = jnp.sum(sums.T, axis=0, keepdims=True)
    gram_ref[...] = lax.dot_general(
        hb_ref[...], hb_ref[...], (((0,), (0,)), ((), ())), preferred_element_type=F32
    )
    part = part_ref.shape[0]
    at = pl.multiple_of((y * nx + x) * part, part)
    part_ref[...] = gram_ref[pl.ds(at, part), :]


def rows_kernel(
    p0, p1, p23, p4, p65, p7, o0, o1, o23, o4, o65, o7, cols, sq, part, more, kern, out, held, sums
):
    z, core = lax.axis_index(Z), lax.axis_index(CORE)
    nz, pts = lax.axis_size(Z), p0.shape[0]

    def put(which, steps, value):
        at = (which * nz + lax.rem(z + steps, nz)) * pts
        held[pl.ds(pl.multiple_of(at, pts), pts), :] = value

    for which, refs in ((core, (p0, p1, p23, p4, p65, p7)), (1 - core, (o0, o1, o23, o4, o65, o7))):
        put(which, 0, refs[0][...])
        put(which, 1, refs[1][...])
        put(which, 2, refs[2][0])
        put(which, 3, refs[2][1])
        put(which, 4, refs[3][...])
        put(which, 5, refs[4][1])
        put(which, 6, refs[4][0])
        put(which, 7, refs[5][...])
    col_sq = jnp.concatenate([sq[g : g + 1, :] for g in range(sq.shape[0])], axis=1)
    tall = 2 * LANES

    def block(i, _):
        at = pl.ds(pl.multiple_of(i * tall, tall), tall)
        rows = held[at, :]
        row_sq = jnp.sum(squares(rows), axis=1, keepdims=True)
        gram = rows_dot(rows, cols[...])
        values = jnp.exp((2.0 * gram - row_sq - col_sq) * (0.5 / EMBED_WIDTH))
        kern[at, :] = values
        total = sum(values[:, g : g + LANES] for g in range(0, values.shape[1], LANES))
        for j in range(2):
            line = jnp.sum(total[j * LANES : (j + 1) * LANES].T, axis=0, keepdims=True)
            sums[pl.ds(i * 2 + j, 1), :] = line
        return 0

    lax.fori_loop(0, held.shape[0] // tall, block, 0)
    lines = sums.shape[0]
    deep = part.shape[0] // 2
    at = pl.ds(pl.multiple_of(core * deep, deep), deep)
    mine = part[at, :] + more[at, :]
    for i in range(out.shape[0]):
        out[i, :lines] = sums[...]
        out[i, lines : lines + deep] = mine[:, :LANES]
        out[i, lines + deep :] = mine[:, LANES:]


def means_kernel(got, mean_ref, out):
    z, core = lax.axis_index(Z), lax.axis_index(CORE)
    n = got.shape[0]
    lines = mean_ref.shape[0]
    total = lines * LANES * n
    even, odd = got[0], got[1]
    for i in range(2, n, 2):
        even, odd = even + got[i], odd + got[i + 1]
    sums = even + odd
    means = sums[:lines] / total
    mean_ref[...] = means
    own = mean_ref[pl.ds((core * lax.axis_size(Z) + z) // 2, 1), :]
    band = jnp.broadcast_to(jnp.sum(means, keepdims=True), (1, LANES))
    fill = jnp.zeros((lines - 2, LANES), F32)
    deep = (got.shape[1] - lines) // 2
    pieces = [own, band, fill]
    for at in (lines, lines + deep):
        pieces += [even[at : at + deep], odd[at : at + deep]]
    whole = jnp.concatenate(pieces, axis=0)
    for i in range(out.shape[0]):
        out[i] = whole


def centred_kernel(own, kern, mean_ref, got, hb, aff, partial, *hh):
    z, core = lax.axis_index(Z), lax.axis_index(CORE)
    n = got.shape[0]
    total = mean_ref.shape[0] * LANES * n
    which = core if own else 1 - core
    grand = got[0, 1:2, :]
    for i in range(1, n):
        grand = grand + got[i, 1:2, :]
    grand = grand / total
    lane = lax.broadcasted_iota(jnp.int32, (1, LANES), 1)
    odd = lax.rem(z, 2) == 1
    places = []
    for i in range(0, n, 2):
        pair = []
        for j in range(2):
            line = got[i + j, 0:1, :]
            swapped = pltpu.roll(line, LANES // 2, 1)
            pair.append(jnp.where(odd if j == 0 else jnp.logical_not(odd), swapped, line))
        places.append(jnp.where(lane < LANES // 2, pair[0], pair[1]))
    lines = mean_ref.shape[0] // 2
    rows = aff.shape[0]
    for i in range(lines):
        line = mean_ref[pl.ds(which * lines + i, 1), :]
        mine = jnp.broadcast_to(line, (LANES, LANES)).T
        at = pl.ds(pl.multiple_of(which * rows + i * LANES, LANES), LANES)
        for g, place in enumerate(places):
            values = kern[at, g * LANES : (g + 1) * LANES]
            values = values - mine - place + grand
            aff[i * LANES : (i + 1) * LANES, g * LANES : (g + 1) * LANES] = values.astype(BF16)
    partial[...] = jnp.dot(aff[...], hb[...], preferred_element_type=F32)
    if hh:
        deep = (got.shape[1] - 8) // 2
        for i in range(n):
            hh[0][i * deep : (i + 1) * deep, :LANES] = got[i, 8 : 8 + deep, :]
            hh[0][i * deep : (i + 1) * deep, LANES:] = got[i, 8 + deep :, :]


def start_kernel(unit, points, factor, first, second):
    half, width = first.shape[0], points.shape[1]
    hb = (factor[...] * unit).astype(BF16)
    first[:, :width] = points[:half, :]
    first[:, width:] = hb[:half]
    second[:, :width] = points[half:, :]
    second[:, width:] = hb[half:]


def step_kernel(before, after, got, hh_ref, h_ref, out, *copies):
    ah = got[0]
    for i in range(1, got.shape[0]):
        ah = ah + got[i]
    hh = hh_ref[...]
    h = h_ref[...] * before if before else h_ref[...]
    square = jnp.sum(jnp.sum(hh * hh, axis=0, keepdims=True), axis=1, keepdims=True)
    scale = 0.5 / jnp.sqrt(square + 1e-06)
    product = jnp.dot(h, hh, precision=lax.Precision.HIGHEST, preferred_element_type=F32)
    h = jnp.maximum(h - scale * (product - ah), 0.0)
    out[...] = h / after if after else h
    if copies:
        hb = h.astype(BF16)
        for i in range(copies[0].shape[0]):
            copies[0][i] = hb


def shards(points, factor):
    nz, ncore, ny, nx = (lax.axis_size(a) for a in ROW_COL)
    nrow, ncol = nz * ncore, ny * nx
    pts, rank = factor.shape
    total = pts * nrow * ncol
    unit = 2.0 / math.sqrt(total * rank)
    width = points.shape[1]
    half = pts // 2
    shape = jax.ShapeDtypeStruct

    first, second = call(
        functools.partial(start_kernel, unit),
        [shape((half, width + rank), BF16)] * 2,
        [points, factor],
        1,
    )
    tie = lax.optimization_barrier
    z1, z7 = from_ahead(points, Z, 1), from_ahead(points, Z, -1)
    x1, x3 = from_ahead(first, X, 1), from_ahead(first, X, -1)
    y1, y3 = from_ahead(second, Y, 1), from_ahead(second, Y, -1)
    z1, z7, first, second = tie((z1, z7, first, second))
    z23 = from_ahead(jnp.stack([points, z1]), Z, 2)
    z65 = from_ahead(jnp.stack([points, z7]), Z, -2)
    x2, y2 = from_ahead(first, X, 2), from_ahead(second, Y, 2)
    x1, x2, x3, y1, y2, y3 = tie((x1, x2, x3, y1, y2, y3))
    by_x = jnp.stack([first, x1, x2, x3])
    by_y = jnp.stack([second, y1, y2, y3])
    from_y = [from_ahead(by_x, Y, s) for s in (1, 2, 3)]
    from_x = [from_ahead(by_y, X, s) for s in (1, 2, 3)]
    from_y[0], z23, z65, z1, z7 = tie((from_y[0], z23, z65, z1, z7))
    z4 = from_ahead(z23[1], Z, 1)
    other_0, other_1, other_7 = (from_ahead(v, CORE, 1) for v in (points, z1, z7))
    along_z = [points, z1, z23, z4, z65, z7]
    cols = [by_x, *from_y, by_y, *from_x]
    other_23, other_65 = from_ahead(z23, CORE, 1), from_ahead(z65, CORE, 1)
    other = [other_0, other_1, other_23, other_65, other_7]
    cols, other = tie((cols, other))
    other.insert(3, from_ahead(z4, CORE, 1))

    part = rank // ncol
    group = nrow * pts
    col_pts, hb_cols, col_sq, own_part = call(
        columns_kernel,
        [
            shape((group, width), BF16),
            shape((group, rank), BF16),
            shape((group // LANES, LANES), F32),
            shape((part, rank), F32),
        ],
        cols,
        2 * group * rank * rank,
        [pltpu.VMEM((rank, rank), F32)],
    )
    more_part = from_ahead(own_part, CORE, 1)
    lines = group // LANES
    kern, message = call(
        rows_kernel,
        [shape((group, group), F32), shape((nrow, lines + part, LANES), F32)],
        [*along_z, *other, col_pts, col_sq, own_part, more_part],
        2 * group * group * width,
        [pltpu.VMEM((group, width), BF16), pltpu.VMEM((lines, LANES), F32)],
    )
    mean_rows, message = call(
        means_kernel,
        [shape((lines, LANES), F32), shape((ncol, 8 + 2 * part, LANES), F32)],
        [lax.all_to_all(message, ROW, 0, 0, tiled=True)],
        1,
    )
    gathered = lax.all_to_all(message, COL, 0, 0, tiled=True)

    def centred(own):
        outs = [shape((group // 2, group), BF16), shape((group // 2, rank), F32)]
        if own:
            outs.append(shape((rank, rank), F32))
        return call(
            functools.partial(centred_kernel, own),
            outs,
            [kern, mean_rows, gathered, hb_cols],
            group * group * rank,
        )

    aff_other, partial_other = centred(False)
    got = from_ahead(partial_other, CORE, 1)
    aff_own, partial_own, hh = centred(True)

    def over_z(mine):
        return lax.all_to_all(mine.reshape(nz, pts, rank), Z, 0, 0, tiled=True)

    def stepped(before, after, ah, hh, h, copies):
        outs = [shape((pts, rank), F32)] + [shape((ncol, pts, rank), BF16)] * copies
        flops = 12 * pts * rank * rank
        return call(functools.partial(step_kernel, before, after), outs, [ah, hh, h], flops)

    ah = over_z(partial_own + got)
    h, hb_cols = stepped(unit, None, ah, hh, factor, 1)

    hb_cols = lax.all_to_all(hb_cols, COL, 0, 0, tiled=True).reshape(group, rank)
    partial_other = jnp.dot(aff_other, hb_cols, preferred_element_type=F32)
    got = from_ahead(partial_other, CORE, 1)
    gram = lax.dot_general(hb_cols, hb_cols, (((0,), (0,)), ((), ())), preferred_element_type=F32)
    own_part = lax.dynamic_slice_in_dim(gram, lax.axis_index(COL) * part, part, 0)
    own_part = own_part + from_ahead(own_part, CORE, 1)
    partial_own = jnp.dot(aff_own, hb_cols, preferred_element_type=F32)
    ah = over_z(partial_own + got)
    for bit in (1, 2, 4):
        own_part = own_part + lax.ppermute(own_part, Z, [(i, i ^ bit) for i in range(nz)])
    ah, own_part = tie((ah, own_part))
    hh = sent_to_all(own_part, COL).reshape(rank, rank)
    return stepped(None, unit, ah, hh, h, 0)[0]


def solution(mesh):
    split = Mesh(mesh.devices.reshape(8, 2, 4, 4), ROW_COL)
    return jax.shard_map(
        shards,
        mesh=split,
        in_specs=(P(ROW_COL, None), P(ROW_COL, None)),
        out_specs=P(ROW_COL, None),
        check_vma=False,
    )
```

```python
import functools
import math

import jax
import jax.numpy as jnp
from jax import lax
from jax.experimental import pallas as pl
from jax.experimental.pallas import tpu as pltpu
from jax.sharding import Mesh
from jax.sharding import PartitionSpec as P

EMBED_WIDTH = 1024
Z, CORE, Y, X = "row_0", "row_1", "col_0", "col_1"
ROW = (Z, CORE)
COL = (Y, X)
ROW_COL = (Z, CORE, Y, X)


def from_ahead(value, axis, steps):
    length = lax.axis_size(axis)
    return lax.ppermute(value, axis, [((i + steps) % length, i) for i in range(length)])


def sent_to_all(value, axes):
    length = math.prod(lax.axis_size(a) for a in axes)
    copies = jnp.broadcast_to(value, (length, *value.shape))
    return lax.all_to_all(copies, axes, split_axis=0, concat_axis=0, tiled=True)


F32, BF16 = jnp.float32, jnp.bfloat16
VMEM = pl.BlockSpec(memory_space=pltpu.VMEM)
LANES = 128


def call(kernel, outs, args, flops, scratch=(), vmem=24):
    size = sum(math.prod(a.shape) * a.dtype.itemsize for a in (*outs, *args))
    return pl.pallas_call(
        kernel,
        out_shape=outs,
        in_specs=[VMEM] * len(args),
        out_specs=[VMEM] * len(outs),
        scratch_shapes=list(scratch),
        compiler_params=pltpu.CompilerParams(vmem_limit_bytes=vmem << 20),
        cost_estimate=pl.CostEstimate(flops=flops, bytes_accessed=size, transcendentals=0),
    )(*args)


def rows_dot(a, b):
    return lax.dot_general(a, b, (((1,), (1,)), ((), ())), preferred_element_type=F32)


def squares(rows):
    wide = rows.astype(F32)
    groups = [wide[:, g : g + LANES] for g in range(0, rows.shape[1], LANES)]
    return sum(g * g for g in groups)


def columns_kernel(by_x, y1, y2, y3, by_y, x1, x2, x3, pts_ref, hb_ref, sq_ref, part_ref, gram_ref):
    ny, nx = lax.axis_size(Y), lax.axis_size(X)
    y, x = lax.axis_index(Y), lax.axis_index(X)
    half = by_x.shape[1]
    width = pts_ref.shape[1]
    for far, ref in enumerate((by_x, y1, y2, y3)):
        for near in range(nx):
            at = lax.rem(y + far, ny) * nx + lax.rem(x + near, nx)
            at = pl.multiple_of(at * 2 * half, half)
            pts_ref[pl.ds(at, half), :] = ref[near, :, :width]
            hb_ref[pl.ds(at, half), :] = ref[near, :, width:]
    for far, ref in enumerate((by_y, x1, x2, x3)):
        for near in range(ny):
            at = lax.rem(y + near, ny) * nx + lax.rem(x + far, nx)
            at = pl.multiple_of(at * 2 * half + half, half)
            pts_ref[pl.ds(at, half), :] = ref[near, :, :width]
            hb_ref[pl.ds(at, half), :] = ref[near, :, width:]
    for block in range(pts_ref.shape[0] // LANES):
        sums = squares(pts_ref[block * LANES : (block + 1) * LANES, :])
        sq_ref[block : block + 1, :] = jnp.sum(sums.T, axis=0, keepdims=True)
    gram_ref[...] = lax.dot_general(
        hb_ref[...], hb_ref[...], (((0,), (0,)), ((), ())), preferred_element_type=F32
    )
    part = part_ref.shape[0]
    at = pl.multiple_of((y * nx + x) * part, part)
    part_ref[...] = gram_ref[pl.ds(at, part), :]


def rows_kernel(
    p0, p1, p23, p4, p65, p7, o0, o1, o23, o4, o65, o7, cols, sq, part, more, kern, out, held, sums
):
    z, core = lax.axis_index(Z), lax.axis_index(CORE)
    nz, pts = lax.axis_size(Z), p0.shape[0]

    def put(which, steps, value):
        at = (which * nz + lax.rem(z + steps, nz)) * pts
        held[pl.ds(pl.multiple_of(at, pts), pts), :] = value

    for which, refs in ((core, (p0, p1, p23, p4, p65, p7)), (1 - core, (o0, o1, o23, o4, o65, o7))):
        put(which, 0, refs[0][...])
        put(which, 1, refs[1][...])
        put(which, 2, refs[2][0])
        put(which, 3, refs[2][1])
        put(which, 4, refs[3][...])
        put(which, 5, refs[4][1])
        put(which, 6, refs[4][0])
        put(which, 7, refs[5][...])
    col_sq = jnp.concatenate([sq[g : g + 1, :] for g in range(sq.shape[0])], axis=1)
    tall = 2 * LANES

    def block(i, _):
        at = pl.ds(pl.multiple_of(i * tall, tall), tall)
        rows = held[at, :]
        row_sq = jnp.sum(squares(rows), axis=1, keepdims=True)
        gram = rows_dot(rows, cols[...])
        values = jnp.exp((2.0 * gram - row_sq - col_sq) * (0.5 / EMBED_WIDTH))
        kern[at, :] = values
        total = sum(values[:, g : g + LANES] for g in range(0, values.shape[1], LANES))
        for j in range(2):
            line = jnp.sum(total[j * LANES : (j + 1) * LANES].T, axis=0, keepdims=True)
            sums[pl.ds(i * 2 + j, 1), :] = line
        return 0

    lax.fori_loop(0, held.shape[0] // tall, block, 0)
    lines = sums.shape[0]
    deep = part.shape[0] // 2
    at = pl.ds(pl.multiple_of(core * deep, deep), deep)
    mine = part[at, :] + more[at, :]
    for i in range(out.shape[0]):
        out[i, :lines] = sums[...]
        out[i, lines : lines + deep] = mine[:, :LANES]
        out[i, lines + deep :] = mine[:, LANES:]


def means_kernel(got, mean_ref, out):
    z, core = lax.axis_index(Z), lax.axis_index(CORE)
    n = got.shape[0]
    lines = mean_ref.shape[0]
    total = lines * LANES * n
    even, odd = got[0], got[1]
    for i in range(2, n, 2):
        even, odd = even + got[i], odd + got[i + 1]
    sums = even + odd
    means = sums[:lines] / total
    mean_ref[...] = means
    own = mean_ref[pl.ds((core * lax.axis_size(Z) + z) // 2, 1), :]
    band = jnp.broadcast_to(jnp.sum(means, keepdims=True), (1, LANES))
    fill = jnp.zeros((lines - 2, LANES), F32)
    deep = (got.shape[1] - lines) // 2
    pieces = [own, band, fill]
    for at in (lines, lines + deep):
        pieces += [even[at : at + deep], odd[at : at + deep]]
    whole = jnp.concatenate(pieces, axis=0)
    for i in range(out.shape[0]):
        out[i] = whole


def centred_kernel(own, kern, mean_ref, got, hb, aff, partial, *more):
    z, core = lax.axis_index(Z), lax.axis_index(CORE)
    n = got.shape[0]
    total = mean_ref.shape[0] * LANES * n
    which = core if own else 1 - core
    grand = got[0, 1:2, :]
    for i in range(1, n):
        grand = grand + got[i, 1:2, :]
    grand = grand / total
    lane = lax.broadcasted_iota(jnp.int32, (1, LANES), 1)
    odd = lax.rem(z, 2) == 1
    places = []
    for i in range(0, n, 2):
        pair = []
        for j in range(2):
            line = got[i + j, 0:1, :]
            swapped = pltpu.roll(line, LANES // 2, 1)
            pair.append(jnp.where(odd if j == 0 else jnp.logical_not(odd), swapped, line))
        places.append(jnp.where(lane < LANES // 2, pair[0], pair[1]))
    lines = mean_ref.shape[0] // 2
    rows = aff.shape[0]
    for i in range(lines):
        line = mean_ref[pl.ds(which * lines + i, 1), :]
        mine = jnp.broadcast_to(line, (LANES, LANES)).T
        at = pl.ds(pl.multiple_of(which * rows + i * LANES, LANES), LANES)
        for g, place in enumerate(places):
            values = kern[at, g * LANES : (g + 1) * LANES]
            values = values - mine - place + grand
            aff[i * LANES : (i + 1) * LANES, g * LANES : (g + 1) * LANES] = values.astype(BF16)
    partial[...] = jnp.dot(aff[...], hb[...], preferred_element_type=F32)
    if more:
        hh_ref, scales = more
        deep = (got.shape[1] - 8) // 2
        for i in range(n):
            hh_ref[i * deep : (i + 1) * deep, :LANES] = got[i, 8 : 8 + deep, :]
            hh_ref[i * deep : (i + 1) * deep, LANES:] = got[i, 8 + deep :, :]
        hh = hh_ref[...]
        line = lax.broadcasted_iota(jnp.int32, hh.shape, 0)
        place = lax.broadcasted_iota(jnp.int32, hh.shape, 1)
        norm = jnp.sum(jnp.where(line == place, hh, 0.0), axis=0, keepdims=True)
        norm = jnp.sqrt(jnp.maximum(norm, 1e-30))
        grown = norm * (1.05 + 1.05 * total * step_size(hh))
        summed = grown * jnp.max(grown, axis=1, keepdims=True)
        for i, (value, top) in enumerate(((norm, 512.0), (grown, 512.0), (summed, 32768.0))):
            scales[2 * i : 2 * i + 1, :] = top / value
            scales[2 * i + 1 : 2 * i + 2, :] = value / top


def step_size(hh):
    square = jnp.sum(jnp.sum(hh * hh, axis=0, keepdims=True), axis=1, keepdims=True)
    return 0.5 / jnp.sqrt(square + 1e-06)


def start_kernel(unit, points, factor, first, second):
    half, width = first.shape[0], points.shape[1]
    hb = (factor[...] * unit).astype(BF16)
    first[:, :width] = points[:half, :]
    first[:, width:] = hb[:half]
    second[:, :width] = points[half:, :]
    second[:, width:] = hb[half:]


def step_kernel(before, after, ah_ref, hh_ref, h_ref, out, *copies):
    hh = hh_ref[...]
    h = h_ref[...] * before if before else h_ref[...]
    scale = step_size(hh)
    product = jnp.dot(h, hh, precision=lax.Precision.HIGHEST, preferred_element_type=F32)
    h = jnp.maximum(h - scale * (product - ah_ref[...]), 0.0)
    out[...] = h / after if after else h
    if copies:
        hb = h.astype(BF16)
        for i in range(copies[0].shape[0]):
            copies[0][i] = hb


def shards(points, factor):
    nz, ncore, ny, nx = (lax.axis_size(a) for a in ROW_COL)
    nrow, ncol = nz * ncore, ny * nx
    pts, rank = factor.shape
    total = pts * nrow * ncol
    unit = 2.0 / math.sqrt(total * rank)
    width = points.shape[1]
    half = pts // 2
    shape = jax.ShapeDtypeStruct

    first, second = call(
        functools.partial(start_kernel, unit),
        [shape((half, width + rank), BF16)] * 2,
        [points, factor],
        1,
    )
    tie = lax.optimization_barrier
    z1, z7 = from_ahead(points, Z, 1), from_ahead(points, Z, -1)
    x1, x3 = from_ahead(first, X, 1), from_ahead(first, X, -1)
    y1, y3 = from_ahead(second, Y, 1), from_ahead(second, Y, -1)
    z1, z7, first, second = tie((z1, z7, first, second))
    z23 = from_ahead(jnp.stack([points, z1]), Z, 2)
    z65 = from_ahead(jnp.stack([points, z7]), Z, -2)
    x2, y2 = from_ahead(first, X, 2), from_ahead(second, Y, 2)
    x1, x2, x3, y1, y2, y3 = tie((x1, x2, x3, y1, y2, y3))
    by_x = jnp.stack([first, x1, x2, x3])
    by_y = jnp.stack([second, y1, y2, y3])
    from_y = [from_ahead(by_x, Y, s) for s in (1, 2, 3)]
    from_x = [from_ahead(by_y, X, s) for s in (1, 2, 3)]
    from_y[0], z23, z65, z1, z7 = tie((from_y[0], z23, z65, z1, z7))
    z4 = from_ahead(z23[1], Z, 1)
    other_0, other_1, other_7 = (from_ahead(v, CORE, 1) for v in (points, z1, z7))
    along_z = [points, z1, z23, z4, z65, z7]
    cols = [by_x, *from_y, by_y, *from_x]
    other_23, other_65 = from_ahead(z23, CORE, 1), from_ahead(z65, CORE, 1)
    other = [other_0, other_1, other_23, other_65, other_7]
    cols, other = tie((cols, other))
    other.insert(3, from_ahead(z4, CORE, 1))

    part = rank // ncol
    group = nrow * pts
    col_pts, hb_cols, col_sq, own_part = call(
        columns_kernel,
        [
            shape((group, width), BF16),
            shape((group, rank), BF16),
            shape((group // LANES, LANES), F32),
            shape((part, rank), F32),
        ],
        cols,
        2 * group * rank * rank,
        [pltpu.VMEM((rank, rank), F32)],
    )
    more_part = from_ahead(own_part, CORE, 1)
    lines = group // LANES
    kern, message = call(
        rows_kernel,
        [shape((group, group), F32), shape((nrow, lines + part, LANES), F32)],
        [*along_z, *other, col_pts, col_sq, own_part, more_part],
        2 * group * group * width,
        [pltpu.VMEM((group, width), BF16), pltpu.VMEM((lines, LANES), F32)],
    )
    mean_rows, message = call(
        means_kernel,
        [shape((lines, LANES), F32), shape((ncol, 8 + 2 * part, LANES), F32)],
        [lax.all_to_all(message, ROW, 0, 0, tiled=True)],
        1,
    )
    gathered = lax.all_to_all(message, COL, 0, 0, tiled=True)

    def centred(own):
        outs = [shape((group // 2, group), BF16), shape((group // 2, rank), F32)]
        if own:
            outs += [shape((rank, rank), F32), shape((8, rank), F32)]
        return call(
            functools.partial(centred_kernel, own),
            outs,
            [kern, mean_rows, gathered, hb_cols],
            group * group * rank,
        )

    aff_other, partial_other = centred(False)
    got = from_ahead(partial_other, CORE, 1)
    aff_own, partial_own, hh, scales = centred(True)

    def over_z(mine):
        mine = lax.all_to_all(mine.astype(jnp.float16), Z, 0, 0, tiled=True)
        return jnp.sum(mine.astype(F32), axis=0)

    def stepped(before, after, ah, hh, h, copies):
        outs = [shape((pts, rank), F32)] + [shape((ncol, pts, rank), BF16)] * copies
        flops = 12 * pts * rank * rank
        return call(functools.partial(step_kernel, before, after), outs, [ah, hh, h], flops)

    mine = (partial_own + got) * scales[0]
    ah = over_z(mine.reshape(nz, pts, rank)) * scales[1]
    h, hb_cols = stepped(unit, None, ah, hh, factor, 1)

    hb_cols = lax.all_to_all(hb_cols, COL, 0, 0, tiled=True).reshape(group, rank)
    gram = lax.dot_general(hb_cols, hb_cols, (((0,), (0,)), ((), ())), preferred_element_type=F32)
    own_part = lax.dynamic_slice_in_dim(gram, lax.axis_index(COL) * part, part, 0)
    partial_other = jnp.dot(aff_other, hb_cols, preferred_element_type=F32)
    got = from_ahead(jnp.concatenate([partial_other, own_part]), CORE, 1)
    partial_own = jnp.dot(aff_own, hb_cols, preferred_element_type=F32)
    mine = ((partial_own + got[: group // 2]) * scales[2]).reshape(nz, pts, rank)
    extra = (own_part + got[group // 2 :]) * scales[4]
    extra = jnp.broadcast_to(extra, (nz, part, rank))
    own = over_z(jnp.concatenate([mine, extra], axis=1))
    hh = sent_to_all(own[pts:] * scales[5], COL).reshape(rank, rank)
    ah = own[:pts] * scales[3]
    return stepped(None, unit, ah, hh, h, 0)[0]


def solution(mesh):
    split = Mesh(mesh.devices.reshape(8, 2, 4, 4), ROW_COL)
    return jax.shard_map(
        shards,
        mesh=split,
        in_specs=(P(ROW_COL, None), P(ROW_COL, None)),
        out_specs=P(ROW_COL, None),
        check_vma=False,
    )
```

```python
import functools
import math

import jax
import jax.numpy as jnp
from jax import lax
from jax.experimental import pallas as pl
from jax.experimental.pallas import tpu as pltpu
from jax.sharding import Mesh
from jax.sharding import PartitionSpec as P

EMBED_WIDTH = 1024
Z, CORE, Y, X = "row_0", "row_1", "col_0", "col_1"
ROW = (Z, CORE)
COL = (Y, X)
ROW_COL = (Z, CORE, Y, X)


def from_ahead(value, axis, steps):
    length = lax.axis_size(axis)
    return lax.ppermute(value, axis, [((i + steps) % length, i) for i in range(length)])


def sent_to_all(value, axes):
    length = math.prod(lax.axis_size(a) for a in axes)
    copies = jnp.broadcast_to(value, (length, *value.shape))
    return lax.all_to_all(copies, axes, split_axis=0, concat_axis=0, tiled=True)


F32, BF16 = jnp.float32, jnp.bfloat16
VMEM = pl.BlockSpec(memory_space=pltpu.VMEM)
LANES = 128


def call(kernel, outs, args, flops, scratch=(), vmem=24):
    size = sum(math.prod(a.shape) * a.dtype.itemsize for a in (*outs, *args))
    return pl.pallas_call(
        kernel,
        out_shape=outs,
        in_specs=[VMEM] * len(args),
        out_specs=[VMEM] * len(outs),
        scratch_shapes=list(scratch),
        compiler_params=pltpu.CompilerParams(vmem_limit_bytes=vmem << 20),
        cost_estimate=pl.CostEstimate(flops=flops, bytes_accessed=size, transcendentals=0),
    )(*args)


def rows_dot(a, b):
    return lax.dot_general(a, b, (((1,), (1,)), ((), ())), preferred_element_type=F32)


def squares(rows):
    wide = rows.astype(F32)
    groups = [wide[:, g : g + LANES] for g in range(0, rows.shape[1], LANES)]
    return sum(g * g for g in groups)


def columns_kernel(by_x, y1, y2, y3, by_y, x1, x2, x3, pts_ref, hb_ref, sq_ref, part_ref, gram_ref):
    ny, nx = lax.axis_size(Y), lax.axis_size(X)
    y, x = lax.axis_index(Y), lax.axis_index(X)
    half = by_x.shape[1]
    width = pts_ref.shape[1]
    for far, ref in enumerate((by_x, y1, y2, y3)):
        for near in range(nx):
            at = lax.rem(y + far, ny) * nx + lax.rem(x + near, nx)
            at = pl.multiple_of(at * 2 * half, half)
            pts_ref[pl.ds(at, half), :] = ref[near, :, :width]
            hb_ref[pl.ds(at, half), :] = ref[near, :, width:]
    for far, ref in enumerate((by_y, x1, x2, x3)):
        for near in range(ny):
            at = lax.rem(y + near, ny) * nx + lax.rem(x + far, nx)
            at = pl.multiple_of(at * 2 * half + half, half)
            pts_ref[pl.ds(at, half), :] = ref[near, :, :width]
            hb_ref[pl.ds(at, half), :] = ref[near, :, width:]
    for block in range(pts_ref.shape[0] // LANES):
        sums = squares(pts_ref[block * LANES : (block + 1) * LANES, :])
        sq_ref[block : block + 1, :] = jnp.sum(sums.T, axis=0, keepdims=True)
    gram_ref[...] = lax.dot_general(
        hb_ref[...], hb_ref[...], (((0,), (0,)), ((), ())), preferred_element_type=F32
    )
    part = part_ref.shape[0]
    at = pl.multiple_of((y * nx + x) * part, part)
    part_ref[...] = gram_ref[pl.ds(at, part), :]


def rows_kernel(own, other, cols, sq, part, more, kern, out, sums):
    core = lax.axis_index(CORE)
    col_sq = jnp.concatenate([sq[g : g + 1, :] for g in range(sq.shape[0])], axis=1)
    tall = 2 * LANES

    def block(ref, first, i):
        rows = ref[pl.ds(pl.multiple_of(i * tall, tall), tall), :]
        at = first * ref.shape[0] // tall + i
        row_sq = jnp.sum(squares(rows), axis=1, keepdims=True)
        gram = rows_dot(rows, cols[...])
        values = jnp.exp((2.0 * gram - row_sq - col_sq) * (0.5 / EMBED_WIDTH))
        kern[pl.ds(pl.multiple_of(at * tall, tall), tall), :] = values
        total = sum(values[:, g : g + LANES] for g in range(0, values.shape[1], LANES))
        for j in range(2):
            line = jnp.sum(total[j * LANES : (j + 1) * LANES].T, axis=0, keepdims=True)
            sums[pl.ds(at * 2 + j, 1), :] = line

    for ref, first in ((own, core), (other, 1 - core)):

        def body(i, _, ref=ref, first=first):
            block(ref, first, i)
            return 0

        lax.fori_loop(0, ref.shape[0] // tall, body, 0)
    lines = sums.shape[0]
    deep = part.shape[0] // 2
    at = pl.ds(pl.multiple_of(core * deep, deep), deep)
    mine = part[at, :] + more[at, :]
    for i in range(out.shape[0]):
        out[i, :lines] = sums[...]
        out[i, lines : lines + deep] = mine[:, :LANES]
        out[i, lines + deep :] = mine[:, LANES:]


def means_kernel(got, mean_ref, out):
    z, core = lax.axis_index(Z), lax.axis_index(CORE)
    n = got.shape[0]
    lines = mean_ref.shape[0]
    total = lines * LANES * n
    even, odd = got[0], got[1]
    for i in range(2, n, 2):
        even, odd = even + got[i], odd + got[i + 1]
    sums = even + odd
    means = sums[:lines] / total
    mean_ref[...] = means
    own = mean_ref[pl.ds((core * lax.axis_size(Z) + z) // 2, 1), :]
    band = jnp.broadcast_to(jnp.sum(means, keepdims=True), (1, LANES))
    fill = jnp.zeros((lines - 2, LANES), F32)
    deep = (got.shape[1] - lines) // 2
    pieces = [own, band, fill]
    for at in (lines, lines + deep):
        pieces += [even[at : at + deep], odd[at : at + deep]]
    whole = jnp.concatenate(pieces, axis=0)
    for i in range(out.shape[0]):
        out[i] = whole


def centred_kernel(own, kern, mean_ref, got, hb, aff, partial, *more):
    z, core = lax.axis_index(Z), lax.axis_index(CORE)
    n = got.shape[0]
    total = mean_ref.shape[0] * LANES * n
    which = core if own else 1 - core
    grand = got[0, 1:2, :]
    for i in range(1, n):
        grand = grand + got[i, 1:2, :]
    grand = grand / total
    lane = lax.broadcasted_iota(jnp.int32, (1, LANES), 1)
    odd = lax.rem(z, 2) == 1
    places = []
    for i in range(0, n, 2):
        pair = []
        for j in range(2):
            line = got[i + j, 0:1, :]
            swapped = pltpu.roll(line, LANES // 2, 1)
            pair.append(jnp.where(odd if j == 0 else jnp.logical_not(odd), swapped, line))
        places.append(jnp.where(lane < LANES // 2, pair[0], pair[1]))
    lines = mean_ref.shape[0] // 2
    rows = aff.shape[0]
    for i in range(lines):
        line = mean_ref[pl.ds(which * lines + i, 1), :]
        mine = jnp.broadcast_to(line, (LANES, LANES)).T
        at = pl.ds(pl.multiple_of(which * rows + i * LANES, LANES), LANES)
        for g, place in enumerate(places):
            values = kern[at, g * LANES : (g + 1) * LANES]
            values = values - mine - place + grand
            aff[i * LANES : (i + 1) * LANES, g * LANES : (g + 1) * LANES] = values.astype(BF16)
    partial[...] = jnp.dot(aff[...], hb[...], preferred_element_type=F32)
    if more:
        hh_ref, scales = more
        deep = (got.shape[1] - 8) // 2
        for i in range(n):
            hh_ref[i * deep : (i + 1) * deep, :LANES] = got[i, 8 : 8 + deep, :]
            hh_ref[i * deep : (i + 1) * deep, LANES:] = got[i, 8 + deep :, :]
        hh = hh_ref[...]
        line = lax.broadcasted_iota(jnp.int32, hh.shape, 0)
        place = lax.broadcasted_iota(jnp.int32, hh.shape, 1)
        norm = jnp.sum(jnp.where(line == place, hh, 0.0), axis=0, keepdims=True)
        norm = jnp.sqrt(jnp.maximum(norm, 1e-30))
        grown = norm * (1.05 + 1.05 * total * step_size(hh))
        summed = grown * jnp.max(grown, axis=1, keepdims=True)
        for i, (value, top) in enumerate(((norm, 512.0), (grown, 512.0), (summed, 32768.0))):
            scales[2 * i : 2 * i + 1, :] = top / value
            scales[2 * i + 1 : 2 * i + 2, :] = value / top


def step_size(hh):
    square = jnp.sum(jnp.sum(hh * hh, axis=0, keepdims=True), axis=1, keepdims=True)
    return 0.5 / jnp.sqrt(square + 1e-06)


def start_kernel(unit, points, factor, first, second, copies):
    half, width = first.shape[0], points.shape[1]
    hb = (factor[...] * unit).astype(BF16)
    first[:, :width] = points[:half, :]
    first[:, width:] = hb[:half]
    second[:, :width] = points[half:, :]
    second[:, width:] = hb[half:]
    for i in range(copies.shape[0]):
        copies[i] = points[...]


def step_kernel(before, after, ah_ref, hh_ref, h_ref, out, *copies):
    hh = hh_ref[...]
    h = h_ref[...] * before if before else h_ref[...]
    scale = step_size(hh)
    product = jnp.dot(h, hh, precision=lax.Precision.HIGHEST, preferred_element_type=F32)
    h = jnp.maximum(h - scale * (product - ah_ref[...]), 0.0)
    out[...] = h / after if after else h
    if copies:
        hb = h.astype(BF16)
        for i in range(copies[0].shape[0]):
            copies[0][i] = hb


def shards(points, factor):
    nz, ncore, ny, nx = (lax.axis_size(a) for a in ROW_COL)
    nrow, ncol = nz * ncore, ny * nx
    pts, rank = factor.shape
    total = pts * nrow * ncol
    unit = 2.0 / math.sqrt(total * rank)
    width = points.shape[1]
    half = pts // 2
    shape = jax.ShapeDtypeStruct

    first, second, copies = call(
        functools.partial(start_kernel, unit),
        [*[shape((half, width + rank), BF16)] * 2, shape((nz, pts, width), BF16)],
        [points, factor],
        1,
    )
    tie = lax.optimization_barrier
    along_z = lax.all_to_all(copies, Z, 0, 0, tiled=True)
    x1, x3 = from_ahead(first, X, 1), from_ahead(first, X, -1)
    y1, y3 = from_ahead(second, Y, 1), from_ahead(second, Y, -1)
    x2, y2 = from_ahead(first, X, 2), from_ahead(second, Y, 2)
    x1, x2, x3, y1, y2, y3 = tie((x1, x2, x3, y1, y2, y3))
    by_x = jnp.stack([first, x1, x2, x3])
    by_y = jnp.stack([second, y1, y2, y3])
    from_y = [from_ahead(by_x, Y, s) for s in (1, 2, 3)]
    from_x = [from_ahead(by_y, X, s) for s in (1, 2, 3)]
    from_y, from_x, along_z = tie((from_y, from_x, along_z.reshape(-1, width)))
    cols = [by_x, *from_y, by_y, *from_x]
    other = from_ahead(along_z, CORE, 1)

    part = rank // ncol
    group = nrow * pts
    col_pts, hb_cols, col_sq, own_part = call(
        columns_kernel,
        [
            shape((group, width), BF16),
            shape((group, rank), BF16),
            shape((group // LANES, LANES), F32),
            shape((part, rank), F32),
        ],
        cols,
        2 * group * rank * rank,
        [pltpu.VMEM((rank, rank), F32)],
    )
    more_part = from_ahead(own_part, CORE, 1)
    lines = group // LANES
    kern, message = call(
        rows_kernel,
        [shape((group, group), F32), shape((nrow, lines + part, LANES), F32)],
        [along_z, other, col_pts, col_sq, own_part, more_part],
        2 * group * group * width,
        [pltpu.VMEM((lines, LANES), F32)],
    )
    mean_rows, message = call(
        means_kernel,
        [shape((lines, LANES), F32), shape((ncol, 8 + 2 * part, LANES), F32)],
        [lax.all_to_all(message, ROW, 0, 0, tiled=True)],
        1,
    )
    gathered = lax.all_to_all(message, COL, 0, 0, tiled=True)

    def centred(own):
        outs = [shape((group // 2, group), BF16), shape((group // 2, rank), F32)]
        if own:
            outs += [shape((rank, rank), F32), shape((8, rank), F32)]
        return call(
            functools.partial(centred_kernel, own),
            outs,
            [kern, mean_rows, gathered, hb_cols],
            group * group * rank,
        )

    aff_other, partial_other = centred(False)
    got = from_ahead(partial_other, CORE, 1)
    aff_own, partial_own, hh, scales = centred(True)

    def over_z(mine):
        mine = lax.all_to_all(mine.astype(jnp.float16), Z, 0, 0, tiled=True)
        return jnp.sum(mine.astype(F32), axis=0)

    def stepped(before, after, ah, hh, h, copies):
        outs = [shape((pts, rank), F32)] + [shape((ncol, pts, rank), BF16)] * copies
        flops = 12 * pts * rank * rank
        return call(functools.partial(step_kernel, before, after), outs, [ah, hh, h], flops)

    mine = (partial_own + got) * scales[0]
    ah = over_z(mine.reshape(nz, pts, rank)) * scales[1]
    h, hb_cols = stepped(unit, None, ah, hh, factor, 1)

    hb_cols = lax.all_to_all(hb_cols, COL, 0, 0, tiled=True).reshape(group, rank)
    gram = lax.dot_general(hb_cols, hb_cols, (((0,), (0,)), ((), ())), preferred_element_type=F32)
    own_part = lax.dynamic_slice_in_dim(gram, lax.axis_index(COL) * part, part, 0)
    partial_other = jnp.dot(aff_other, hb_cols, preferred_element_type=F32)
    got = from_ahead(jnp.concatenate([partial_other, own_part]), CORE, 1)
    partial_own = jnp.dot(aff_own, hb_cols, preferred_element_type=F32)
    mine = ((partial_own + got[: group // 2]) * scales[2]).reshape(nz, pts, rank)
    extra = (own_part + got[group // 2 :]) * scales[4]
    extra = jnp.broadcast_to(extra, (nz, part, rank))
    own = over_z(jnp.concatenate([mine, extra], axis=1))
    hh = sent_to_all(own[pts:] * scales[5], COL).reshape(rank, rank)
    ah = own[:pts] * scales[3]
    return stepped(None, unit, ah, hh, h, 0)[0]


def solution(mesh):
    split = Mesh(mesh.devices.reshape(8, 2, 4, 4), ROW_COL)
    return jax.shard_map(
        shards,
        mesh=split,
        in_specs=(P(ROW_COL, None), P(ROW_COL, None)),
        out_specs=P(ROW_COL, None),
        check_vma=False,
    )
```

```python
import functools
import math

import jax
import jax.numpy as jnp
from jax import lax
from jax.experimental import pallas as pl
from jax.experimental.pallas import tpu as pltpu
from jax.sharding import Mesh
from jax.sharding import PartitionSpec as P

EMBED_WIDTH = 1024
Z, CORE, Y, X = "row_0", "row_1", "col_0", "col_1"
ROW = (Z, CORE)
COL = (Y, X)
ROW_COL = (Z, CORE, Y, X)


def from_ahead(value, axis, steps):
    length = lax.axis_size(axis)
    return lax.ppermute(value, axis, [((i + steps) % length, i) for i in range(length)])


def sent_to_all(value, axes):
    length = math.prod(lax.axis_size(a) for a in axes)
    copies = jnp.broadcast_to(value, (length, *value.shape))
    return lax.all_to_all(copies, axes, split_axis=0, concat_axis=0, tiled=True)


F32, BF16 = jnp.float32, jnp.bfloat16
VMEM = pl.BlockSpec(memory_space=pltpu.VMEM)
LANES = 128


def call(kernel, outs, args, flops, scratch=(), vmem=10, place=pltpu.VMEM):
    size = sum(math.prod(a.shape) * a.dtype.itemsize for a in (*outs, *args))
    return pl.pallas_call(
        kernel,
        out_shape=outs,
        in_specs=[pl.BlockSpec(memory_space=place)] * len(args),
        out_specs=[VMEM] * len(outs),
        scratch_shapes=list(scratch),
        compiler_params=pltpu.CompilerParams(vmem_limit_bytes=vmem << 20),
        cost_estimate=pl.CostEstimate(flops=flops, bytes_accessed=size, transcendentals=0),
    )(*args)


def rows_dot(a, b):
    return lax.dot_general(a, b, (((1,), (1,)), ((), ())), preferred_element_type=F32)


def squares(rows):
    wide = rows.astype(F32)
    groups = [wide[:, g : g + LANES] for g in range(0, rows.shape[1], LANES)]
    return sum(g * g for g in groups)


def columns_kernel(
    ax0, ax1, ax2, ax3, y1, y2, y3, by0, by1, by2, by3, x1, x2, x3, pts_ref, hb_ref, sq_ref, part_ref, gram_ref
):
    ny, nx = lax.axis_size(Y), lax.axis_size(X)
    y, x = lax.axis_index(Y), lax.axis_index(X)
    half = ax0.shape[0]
    width = pts_ref.shape[1]

    def put(far, near, lower, value):
        at = (lax.rem(y + far, ny) * nx + lax.rem(x + near, nx)) * 2 * half + lower
        at = pl.ds(pl.multiple_of(at, half), half)
        pts_ref[at, :] = value[:, :width]
        hb_ref[at, :] = value[:, width:]

    for near, ref in enumerate((ax0, ax1, ax2, ax3)):
        put(0, near, 0, ref[...])
    for far, ref in enumerate((by0, by1, by2, by3)):
        put(far, 0, half, ref[...])
    for far, ref in enumerate((y1, y2, y3)):
        for near in range(nx):
            put(far + 1, near, 0, ref[near])
    for near, ref in enumerate((x1, x2, x3)):
        for far in range(ny):
            put(far, near + 1, half, ref[far])
    for block in range(pts_ref.shape[0] // LANES):
        sums = squares(pts_ref[block * LANES : (block + 1) * LANES, :])
        sq_ref[block : block + 1, :] = jnp.sum(sums.T, axis=0, keepdims=True)
    gram_ref[...] = lax.dot_general(
        hb_ref[...], hb_ref[...], (((0,), (0,)), ((), ())), preferred_element_type=F32
    )
    part = part_ref.shape[0]
    at = pl.multiple_of((y * nx + x) * part, part)
    part_ref[...] = gram_ref[pl.ds(at, part), :]


def rows_kernel(rows_ref, cols, sq, kern, sums):
    col_sq = jnp.concatenate([sq[g : g + 1, :] for g in range(sq.shape[0])], axis=1)
    tall = 2 * LANES

    def block(i, _):
        at = pl.ds(pl.multiple_of(i * tall, tall), tall)
        rows = rows_ref[at, :]
        row_sq = jnp.sum(squares(rows), axis=1, keepdims=True)
        gram = rows_dot(rows, cols[...])
        values = jnp.exp((2.0 * gram - row_sq - col_sq) * (0.5 / EMBED_WIDTH))
        kern[at, :] = values
        total = sum(values[:, g : g + LANES] for g in range(0, values.shape[1], LANES))
        for j in range(2):
            line = jnp.sum(total[j * LANES : (j + 1) * LANES].T, axis=0, keepdims=True)
            sums[pl.ds(i * 2 + j, 1), :] = line
        return 0

    lax.fori_loop(0, rows_ref.shape[0] // tall, block, 0)


def last_rows_kernel(rows_ref, cols, sq, own_sums, part, more, kern, out, sums):
    rows_kernel(rows_ref, cols, sq, kern, sums)
    core = lax.axis_index(CORE)
    mine = own_sums[...]
    theirs = sums[...]
    lines = 2 * mine.shape[0]
    deep = part.shape[0] // 2
    at = pl.ds(pl.multiple_of(core * deep, deep), deep)
    gram = part[at, :] + more[at, :]
    swap = core == 1
    both = jnp.concatenate(
        [jnp.where(swap, theirs, mine), jnp.where(swap, mine, theirs)], axis=0
    )
    for i in range(out.shape[0]):
        out[i, :lines] = both
        out[i, lines : lines + deep] = gram[:, :LANES]
        out[i, lines + deep :] = gram[:, LANES:]


def means_kernel(got, mean_ref, out):
    z, core = lax.axis_index(Z), lax.axis_index(CORE)
    n = got.shape[0]
    lines = mean_ref.shape[0]
    total = lines * LANES * n
    even, odd = got[0], got[1]
    for i in range(2, n, 2):
        even, odd = even + got[i], odd + got[i + 1]
    sums = even + odd
    means = sums[:lines] / total
    mean_ref[...] = means
    own = mean_ref[pl.ds((core * lax.axis_size(Z) + z) // 2, 1), :]
    band = jnp.broadcast_to(jnp.sum(means, keepdims=True), (1, LANES))
    fill = jnp.zeros((lines - 2, LANES), F32)
    deep = (got.shape[1] - lines) // 2
    pieces = [own, band, fill]
    for at in (lines, lines + deep):
        pieces += [even[at : at + deep], odd[at : at + deep]]
    whole = jnp.concatenate(pieces, axis=0)
    for i in range(out.shape[0]):
        out[i] = whole


def centred_kernel(own, kern, mean_ref, got, hb, aff, partial, *more):
    z, core = lax.axis_index(Z), lax.axis_index(CORE)
    n = got.shape[0]
    total = mean_ref.shape[0] * LANES * n
    which = core if own else 1 - core
    grand = got[0, 1:2, :]
    for i in range(1, n):
        grand = grand + got[i, 1:2, :]
    grand = grand / total
    lane = lax.broadcasted_iota(jnp.int32, (1, LANES), 1)
    odd = lax.rem(z, 2) == 1
    places = []
    for i in range(0, n, 2):
        pair = []
        for j in range(2):
            line = got[i + j, 0:1, :]
            swapped = pltpu.roll(line, LANES // 2, 1)
            pair.append(jnp.where(odd if j == 0 else jnp.logical_not(odd), swapped, line))
        places.append(jnp.where(lane < LANES // 2, pair[0], pair[1]))
    lines = mean_ref.shape[0] // 2
    for i in range(lines):
        line = mean_ref[pl.ds(which * lines + i, 1), :]
        mine = jnp.broadcast_to(line, (LANES, LANES)).T
        at = slice(i * LANES, (i + 1) * LANES)
        for g, place in enumerate(places):
            values = kern[at, g * LANES : (g + 1) * LANES]
            values = values - mine - place + grand
            aff[at, g * LANES : (g + 1) * LANES] = values.astype(BF16)
    partial[...] = jnp.dot(aff[...], hb[...], preferred_element_type=F32)
    if more:
        hh_ref, scales = more
        deep = (got.shape[1] - 8) // 2
        for i in range(n):
            hh_ref[i * deep : (i + 1) * deep, :LANES] = got[i, 8 : 8 + deep, :]
            hh_ref[i * deep : (i + 1) * deep, LANES:] = got[i, 8 + deep :, :]
        hh = hh_ref[...]
        line = lax.broadcasted_iota(jnp.int32, hh.shape, 0)
        place = lax.broadcasted_iota(jnp.int32, hh.shape, 1)
        norm = jnp.sum(jnp.where(line == place, hh, 0.0), axis=0, keepdims=True)
        norm = jnp.sqrt(jnp.maximum(norm, 1e-30))
        grown = norm * (1.05 + 1.05 * total * step_size(hh))
        summed = grown * jnp.max(grown, axis=1, keepdims=True)
        for i, (value, top) in enumerate(((norm, 512.0), (grown, 512.0), (summed, 32768.0))):
            scales[2 * i : 2 * i + 1, :] = top / value
            scales[2 * i + 1 : 2 * i + 2, :] = value / top


def step_size(hh):
    square = jnp.sum(jnp.sum(hh * hh, axis=0, keepdims=True), axis=1, keepdims=True)
    return 0.5 / jnp.sqrt(square + 1e-06)


def start_kernel(unit, points, factor, first, second, copies, wide, done):
    half, width = first.shape[0], points.shape[1]
    fetches = [
        pltpu.make_async_copy(points, copies.at[0], done.at[0]),
        pltpu.make_async_copy(factor, wide, done.at[1]),
    ]
    for fetch in fetches:
        fetch.start()
    for fetch in fetches:
        fetch.wait()
    value = copies[0]
    hb = (wide[...] * unit).astype(BF16)
    first[:, :width] = value[:half]
    first[:, width:] = hb[:half]
    second[:, :width] = value[half:]
    second[:, width:] = hb[half:]
    for i in range(1, copies.shape[0]):
        copies[i] = value


def step_kernel(before, after, ah_ref, hh_ref, h_ref, out, *copies):
    hh = hh_ref[...]
    h = h_ref[...] * before if before else h_ref[...]
    scale = step_size(hh)
    product = jnp.dot(h, hh, precision=lax.Precision.HIGHEST, preferred_element_type=F32)
    h = jnp.maximum(h - scale * (product - ah_ref[...]), 0.0)
    out[...] = h / after if after else h
    if copies:
        hb = h.astype(BF16)
        for i in range(copies[0].shape[0]):
            copies[0][i] = hb


def shards(points, factor):
    nz, ncore, ny, nx = (lax.axis_size(a) for a in ROW_COL)
    nrow, ncol = nz * ncore, ny * nx
    pts, rank = factor.shape
    total = pts * nrow * ncol
    unit = 2.0 / math.sqrt(total * rank)
    width = points.shape[1]
    half = pts // 2
    shape = jax.ShapeDtypeStruct

    first, second, copies = call(
        functools.partial(start_kernel, unit),
        [*[shape((half, width + rank), BF16)] * 2, shape((nz, pts, width), BF16)],
        [points, factor],
        1,
        [pltpu.VMEM((pts, rank), F32), pltpu.SemaphoreType.DMA((2,))],
        vmem=60,
        place=pl.ANY,
    )
    tie = lax.optimization_barrier
    along_z = lax.all_to_all(copies, Z, 0, 0, tiled=True)
    x1, x3 = from_ahead(first, X, 1), from_ahead(first, X, -1)
    y1, y3 = from_ahead(second, Y, 1), from_ahead(second, Y, -1)
    x2, y2 = from_ahead(first, X, 2), from_ahead(second, Y, 2)
    x1, x2, x3, y1, y2, y3 = tie((x1, x2, x3, y1, y2, y3))
    by_x = jnp.stack([first, x1, x2, x3])
    by_y = jnp.stack([second, y1, y2, y3])
    from_y = [from_ahead(by_x, Y, s) for s in (1, 2, 3)]
    from_x = [from_ahead(by_y, X, s) for s in (1, 2, 3)]
    cols = [first, x1, x2, x3, *from_y, second, y1, y2, y3, *from_x]

    part = rank // ncol
    group = nrow * pts
    col_pts, hb_cols, col_sq, own_part = call(
        columns_kernel,
        [
            shape((group, width), BF16),
            shape((group, rank), BF16),
            shape((group // LANES, LANES), F32),
            shape((part, rank), F32),
        ],
        cols,
        2 * group * rank * rank,
        [pltpu.VMEM((rank, rank), F32)],
    )
    own_part, along_z = tie((own_part, along_z.reshape(-1, width)))
    other = from_ahead(along_z, CORE, 1)
    more_part = from_ahead(own_part, CORE, 1)
    lines = group // LANES
    own_kern, own_sums = call(
        rows_kernel,
        [shape((group // 2, group), F32), shape((lines // 2, LANES), F32)],
        [along_z, col_pts, col_sq],
        group * group * width,
    )
    other_kern, message = call(
        last_rows_kernel,
        [shape((group // 2, group), F32), shape((nrow, lines + part, LANES), F32)],
        [other, col_pts, col_sq, own_sums, own_part, more_part],
        group * group * width,
        [pltpu.VMEM((lines // 2, LANES), F32)],
    )
    mean_rows, message = call(
        means_kernel,
        [shape((lines, LANES), F32), shape((ncol, 8 + 2 * part, LANES), F32)],
        [lax.all_to_all(message, ROW, 0, 0, tiled=True)],
        1,
    )
    gathered = lax.all_to_all(message, COL, 0, 0, tiled=True)

    def centred(own):
        outs = [shape((group // 2, group), BF16), shape((group // 2, rank), F32)]
        if own:
            outs += [shape((rank, rank), F32), shape((8, rank), F32)]
        return call(
            functools.partial(centred_kernel, own),
            outs,
            [own_kern if own else other_kern, mean_rows, gathered, hb_cols],
            group * group * rank,
        )

    aff_other, partial_other = centred(False)
    got = from_ahead(partial_other, CORE, 1)
    aff_own, partial_own, hh, scales = centred(True)

    def over_z(mine):
        mine = lax.all_to_all(mine.astype(jnp.float16), Z, 0, 0, tiled=True)
        return jnp.sum(mine.astype(F32), axis=0)

    def stepped(before, after, ah, hh, h, copies):
        outs = [shape((pts, rank), F32)] + [shape((ncol, pts, rank), BF16)] * copies
        flops = 12 * pts * rank * rank
        return call(functools.partial(step_kernel, before, after), outs, [ah, hh, h], flops)

    mine = (partial_own + got) * scales[0]
    ah = over_z(mine.reshape(nz, pts, rank)) * scales[1]
    h, hb_cols = stepped(unit, None, ah, hh, factor, 1)

    hb_cols = lax.all_to_all(hb_cols, COL, 0, 0, tiled=True).reshape(group, rank)
    gram = lax.dot_general(hb_cols, hb_cols, (((0,), (0,)), ((), ())), preferred_element_type=F32)
    own_part = lax.dynamic_slice_in_dim(gram, lax.axis_index(COL) * part, part, 0)
    partial_other = jnp.dot(aff_other, hb_cols, preferred_element_type=F32)
    got = from_ahead(jnp.concatenate([partial_other, own_part]), CORE, 1)
    partial_own = jnp.dot(aff_own, hb_cols, preferred_element_type=F32)
    mine = ((partial_own + got[: group // 2]) * scales[2]).reshape(nz, pts, rank)
    extra = (own_part + got[group // 2 :]) * scales[4]
    extra = jnp.broadcast_to(extra, (nz, part, rank))
    own = over_z(jnp.concatenate([mine, extra], axis=1))
    hh = sent_to_all(own[pts:] * scales[5], COL).reshape(rank, rank)
    ah = own[:pts] * scales[3]
    return stepped(None, unit, ah, hh, h, 0)[0]


def solution(mesh):
    split = Mesh(mesh.devices.reshape(8, 2, 4, 4), ROW_COL)
    return jax.shard_map(
        shards,
        mesh=split,
        in_specs=(P(ROW_COL, None), P(ROW_COL, None)),
        out_specs=P(ROW_COL, None),
        check_vma=False,
    )
```

```python
import functools
import math

import jax
import jax.numpy as jnp
from jax import lax
from jax.experimental import pallas as pl
from jax.experimental.pallas import tpu as pltpu
from jax.sharding import Mesh
from jax.sharding import PartitionSpec as P

EMBED_WIDTH = 1024
Z, CORE, Y, X = "row_0", "row_1", "col_0", "col_1"
ROW = (Z, CORE)
COL = (Y, X)
ROW_COL = (Z, CORE, Y, X)


def from_ahead(value, axis, steps):
    length = lax.axis_size(axis)
    return lax.ppermute(value, axis, [((i + steps) % length, i) for i in range(length)])


def sent_to_all(value, axes):
    length = math.prod(lax.axis_size(a) for a in axes)
    copies = jnp.broadcast_to(value, (length, *value.shape))
    return lax.all_to_all(copies, axes, split_axis=0, concat_axis=0, tiled=True)


F32, BF16 = jnp.float32, jnp.bfloat16
VMEM = pl.BlockSpec(memory_space=pltpu.VMEM)
LANES = 128


def call(kernel, outs, args, flops, scratch=(), vmem=10, place=pltpu.VMEM):
    size = sum(math.prod(a.shape) * a.dtype.itemsize for a in (*outs, *args))
    return pl.pallas_call(
        kernel,
        out_shape=outs,
        in_specs=[pl.BlockSpec(memory_space=place)] * len(args),
        out_specs=[VMEM] * len(outs),
        scratch_shapes=list(scratch),
        compiler_params=pltpu.CompilerParams(vmem_limit_bytes=vmem << 20),
        cost_estimate=pl.CostEstimate(flops=flops, bytes_accessed=size, transcendentals=0),
    )(*args)


def rows_dot(a, b):
    return lax.dot_general(a, b, (((1,), (1,)), ((), ())), preferred_element_type=F32)


def squares(rows):
    wide = rows.astype(F32)
    groups = [wide[:, g : g + LANES] for g in range(0, rows.shape[1], LANES)]
    return sum(g * g for g in groups)


def columns_kernel(
    y2, x2, y1, x1, y3, x3, ax0, ax1, ax2, ax3, by0, by1, by2, by3, pts_ref, hb_ref, sq_ref, part_ref, gram_ref
):
    ny, nx = lax.axis_size(Y), lax.axis_size(X)
    y, x = lax.axis_index(Y), lax.axis_index(X)
    half = ax0.shape[0]
    width = pts_ref.shape[1]

    def put(far, near, lower, value):
        at = (lax.rem(y + far, ny) * nx + lax.rem(x + near, nx)) * 2 * half + lower
        at = pl.ds(pl.multiple_of(at, half), half)
        pts_ref[at, :] = value[:, :width]
        hb_ref[at, :] = value[:, width:]

    for near, ref in enumerate((ax0, ax1, ax2, ax3)):
        put(0, near, 0, ref[...])
    for far, ref in enumerate((by0, by1, by2, by3)):
        put(far, 0, half, ref[...])
    for far, ref in enumerate((y1, y2, y3)):
        for near in range(nx):
            put(far + 1, near, 0, ref[near])
    for near, ref in enumerate((x1, x2, x3)):
        for far in range(ny):
            put(far, near + 1, half, ref[far])
    for block in range(pts_ref.shape[0] // LANES):
        sums = squares(pts_ref[block * LANES : (block + 1) * LANES, :])
        sq_ref[block : block + 1, :] = jnp.sum(sums.T, axis=0, keepdims=True)
    gram_ref[...] = lax.dot_general(
        hb_ref[...], hb_ref[...], (((0,), (0,)), ((), ())), preferred_element_type=F32
    )
    part = part_ref.shape[0]
    at = pl.multiple_of((y * nx + x) * part, part)
    part_ref[...] = gram_ref[pl.ds(at, part), :]


def rows_kernel(rows_ref, cols, sq, kern, sums):
    col_sq = jnp.concatenate([sq[g : g + 1, :] for g in range(sq.shape[0])], axis=1)
    tall = 2 * LANES

    def block(i, _):
        at = pl.ds(pl.multiple_of(i * tall, tall), tall)
        rows = rows_ref[at, :]
        row_sq = jnp.sum(squares(rows), axis=1, keepdims=True)
        gram = rows_dot(rows, cols[...])
        values = jnp.exp((2.0 * gram - row_sq - col_sq) * (0.5 / EMBED_WIDTH))
        kern[at, :] = values
        total = sum(values[:, g : g + LANES] for g in range(0, values.shape[1], LANES))
        for j in range(2):
            line = jnp.sum(total[j * LANES : (j + 1) * LANES].T, axis=0, keepdims=True)
            sums[pl.ds(i * 2 + j, 1), :] = line
        return 0

    lax.fori_loop(0, rows_ref.shape[0] // tall, block, 0)


def last_rows_kernel(rows_ref, cols, sq, own_sums, part, more, kern, out, sums):
    rows_kernel(rows_ref, cols, sq, kern, sums)
    core = lax.axis_index(CORE)
    mine = own_sums[...]
    theirs = sums[...]
    lines = 2 * mine.shape[0]
    deep = part.shape[0] // 2
    at = pl.ds(pl.multiple_of(core * deep, deep), deep)
    gram = part[at, :] + more[at, :]
    swap = core == 1
    both = jnp.concatenate(
        [jnp.where(swap, theirs, mine), jnp.where(swap, mine, theirs)], axis=0
    )
    for i in range(out.shape[0]):
        out[i, :lines] = both
        out[i, lines : lines + deep] = gram[:, :LANES]
        out[i, lines + deep :] = gram[:, LANES:]


def means_kernel(got, mean_ref, out):
    z, core = lax.axis_index(Z), lax.axis_index(CORE)
    n = got.shape[0]
    lines = mean_ref.shape[0]
    total = lines * LANES * n
    even, odd = got[0], got[1]
    for i in range(2, n, 2):
        even, odd = even + got[i], odd + got[i + 1]
    sums = even + odd
    means = sums[:lines] / total
    mean_ref[...] = means
    own = mean_ref[pl.ds((core * lax.axis_size(Z) + z) // 2, 1), :]
    band = jnp.broadcast_to(jnp.sum(means, keepdims=True), (1, LANES))
    fill = jnp.zeros((lines - 2, LANES), F32)
    deep = (got.shape[1] - lines) // 2
    pieces = [own, band, fill]
    for at in (lines, lines + deep):
        pieces += [even[at : at + deep], odd[at : at + deep]]
    whole = jnp.concatenate(pieces, axis=0)
    for i in range(out.shape[0]):
        out[i] = whole


def centred_kernel(own, kern, mean_ref, got, hb, aff, partial, *more):
    z, core = lax.axis_index(Z), lax.axis_index(CORE)
    n = got.shape[0]
    total = mean_ref.shape[0] * LANES * n
    which = core if own else 1 - core
    grand = got[0, 1:2, :]
    for i in range(1, n):
        grand = grand + got[i, 1:2, :]
    grand = grand / total
    lane = lax.broadcasted_iota(jnp.int32, (1, LANES), 1)
    odd = lax.rem(z, 2) == 1
    places = []
    for i in range(0, n, 2):
        pair = []
        for j in range(2):
            line = got[i + j, 0:1, :]
            swapped = pltpu.roll(line, LANES // 2, 1)
            pair.append(jnp.where(odd if j == 0 else jnp.logical_not(odd), swapped, line))
        places.append(jnp.where(lane < LANES // 2, pair[0], pair[1]))
    lines = mean_ref.shape[0] // 2
    for i in range(lines):
        line = mean_ref[pl.ds(which * lines + i, 1), :]
        mine = jnp.broadcast_to(line, (LANES, LANES)).T
        at = slice(i * LANES, (i + 1) * LANES)
        for g, place in enumerate(places):
            values = kern[at, g * LANES : (g + 1) * LANES]
            values = values - mine - place + grand
            aff[at, g * LANES : (g + 1) * LANES] = values.astype(BF16)
    partial[...] = jnp.dot(aff[...], hb[...], preferred_element_type=F32)
    if more:
        hh_ref, scales = more
        deep = (got.shape[1] - 8) // 2
        for i in range(n):
            hh_ref[i * deep : (i + 1) * deep, :LANES] = got[i, 8 : 8 + deep, :]
            hh_ref[i * deep : (i + 1) * deep, LANES:] = got[i, 8 + deep :, :]
        hh = hh_ref[...]
        line = lax.broadcasted_iota(jnp.int32, hh.shape, 0)
        place = lax.broadcasted_iota(jnp.int32, hh.shape, 1)
        norm = jnp.sum(jnp.where(line == place, hh, 0.0), axis=0, keepdims=True)
        norm = jnp.sqrt(jnp.maximum(norm, 1e-30))
        grown = norm * (1.05 + 1.05 * total * step_size(hh))
        summed = grown * jnp.max(grown, axis=1, keepdims=True)
        for i, (value, top) in enumerate(((norm, 512.0), (grown, 512.0), (summed, 32768.0))):
            scales[2 * i : 2 * i + 1, :] = top / value
            scales[2 * i + 1 : 2 * i + 2, :] = value / top


def step_size(hh):
    square = jnp.sum(jnp.sum(hh * hh, axis=0, keepdims=True), axis=1, keepdims=True)
    return 0.5 / jnp.sqrt(square + 1e-06)


def start_kernel(unit, points, factor, first, second, copies, wide, done):
    half, width = first.shape[0], points.shape[1]
    fetches = [
        pltpu.make_async_copy(points, copies.at[0], done.at[0]),
        pltpu.make_async_copy(factor, wide, done.at[1]),
    ]
    for fetch in fetches:
        fetch.start()
    for fetch in fetches:
        fetch.wait()
    value = copies[0]
    hb = (wide[...] * unit).astype(BF16)
    first[:, :width] = value[:half]
    first[:, width:] = hb[:half]
    second[:, :width] = value[half:]
    second[:, width:] = hb[half:]
    for i in range(1, copies.shape[0]):
        copies[i] = value


def step_kernel(before, after, ah_ref, hh_ref, h_ref, out, *copies):
    hh = hh_ref[...]
    h = h_ref[...] * before if before else h_ref[...]
    scale = step_size(hh)
    product = jnp.dot(h, hh, precision=lax.Precision.HIGHEST, preferred_element_type=F32)
    h = jnp.maximum(h - scale * (product - ah_ref[...]), 0.0)
    out[...] = h / after if after else h
    if copies:
        hb = h.astype(BF16)
        for i in range(copies[0].shape[0]):
            copies[0][i] = hb


def shards(points, factor):
    nz, ncore, ny, nx = (lax.axis_size(a) for a in ROW_COL)
    nrow, ncol = nz * ncore, ny * nx
    pts, rank = factor.shape
    total = pts * nrow * ncol
    unit = 2.0 / math.sqrt(total * rank)
    width = points.shape[1]
    half = pts // 2
    shape = jax.ShapeDtypeStruct

    first, second, copies = call(
        functools.partial(start_kernel, unit),
        [*[shape((half, width + rank), BF16)] * 2, shape((nz, pts, width), BF16)],
        [points, factor],
        1,
        [pltpu.VMEM((pts, rank), F32), pltpu.SemaphoreType.DMA((2,))],
        vmem=60,
        place=pl.ANY,
    )
    tie = lax.optimization_barrier
    along_z = lax.all_to_all(copies, Z, 0, 0, tiled=True)
    x1, x3 = from_ahead(first, X, 1), from_ahead(first, X, -1)
    y1, y3 = from_ahead(second, Y, 1), from_ahead(second, Y, -1)
    x2, y2 = from_ahead(first, X, 2), from_ahead(second, Y, 2)
    x1, x2, x3, y1, y2, y3 = tie((x1, x2, x3, y1, y2, y3))
    by_x = jnp.stack([first, x1, x2, x3])
    by_y = jnp.stack([second, y1, y2, y3])
    y_two, x_two = from_ahead(by_x, Y, 2), from_ahead(by_y, X, 2)
    y_one, x_one = from_ahead(by_x, Y, 1), from_ahead(by_y, X, 1)
    y_three, x_three = from_ahead(by_x, Y, 3), from_ahead(by_y, X, 3)
    far = [y_two, x_two, y_one, x_one, y_three, x_three]
    far, along_z = tie((far, along_z.reshape(-1, width)))
    other = from_ahead(along_z, CORE, 1)
    cols = [*far, first, x1, x2, x3, second, y1, y2, y3]

    part = rank // ncol
    group = nrow * pts
    col_pts, hb_cols, col_sq, own_part = call(
        columns_kernel,
        [
            shape((group, width), BF16),
            shape((group, rank), BF16),
            shape((group // LANES, LANES), F32),
            shape((part, rank), F32),
        ],
        cols,
        2 * group * rank * rank,
        [pltpu.VMEM((rank, rank), F32)],
    )
    more_part = from_ahead(own_part, CORE, 1)
    lines = group // LANES
    own_kern, own_sums = call(
        rows_kernel,
        [shape((group // 2, group), F32), shape((lines // 2, LANES), F32)],
        [along_z, col_pts, col_sq],
        group * group * width,
    )
    other_kern, message = call(
        last_rows_kernel,
        [shape((group // 2, group), F32), shape((nrow, lines + part, LANES), F32)],
        [other, col_pts, col_sq, own_sums, own_part, more_part],
        group * group * width,
        [pltpu.VMEM((lines // 2, LANES), F32)],
    )
    mean_rows, message = call(
        means_kernel,
        [shape((lines, LANES), F32), shape((ncol, 8 + 2 * part, LANES), F32)],
        [lax.all_to_all(message, ROW, 0, 0, tiled=True)],
        1,
    )
    gathered = lax.all_to_all(message, COL, 0, 0, tiled=True)

    def centred(own):
        outs = [shape((group // 2, group), BF16), shape((group // 2, rank), F32)]
        if own:
            outs += [shape((rank, rank), F32), shape((8, rank), F32)]
        return call(
            functools.partial(centred_kernel, own),
            outs,
            [own_kern if own else other_kern, mean_rows, gathered, hb_cols],
            group * group * rank,
        )

    aff_other, partial_other = centred(False)
    got = from_ahead(partial_other, CORE, 1)
    aff_own, partial_own, hh, scales = centred(True)

    def over_z(mine):
        mine = lax.all_to_all(mine.astype(jnp.float16), Z, 0, 0, tiled=True)
        return jnp.sum(mine.astype(F32), axis=0)

    def stepped(before, after, ah, hh, h, copies):
        outs = [shape((pts, rank), F32)] + [shape((ncol, pts, rank), BF16)] * copies
        flops = 12 * pts * rank * rank
        return call(functools.partial(step_kernel, before, after), outs, [ah, hh, h], flops)

    mine = (partial_own + got) * scales[0]
    ah = over_z(mine.reshape(nz, pts, rank)) * scales[1]
    h, hb_cols = stepped(unit, None, ah, hh, factor, 1)

    hb_cols = lax.all_to_all(hb_cols, COL, 0, 0, tiled=True).reshape(group, rank)
    partial_other = jnp.dot(aff_other, hb_cols, preferred_element_type=F32)
    got = from_ahead(partial_other, CORE, 1)
    gram = lax.dot_general(hb_cols, hb_cols, (((0,), (0,)), ((), ())), preferred_element_type=F32)
    own_part = lax.dynamic_slice_in_dim(gram, lax.axis_index(COL) * part, part, 0)
    more_part = from_ahead(own_part, CORE, 1)
    partial_own = jnp.dot(aff_own, hb_cols, preferred_element_type=F32)
    mine = ((partial_own + got) * scales[2]).reshape(nz, pts, rank)
    extra = jnp.broadcast_to((own_part + more_part) * scales[4], (nz, part, rank))
    own = over_z(jnp.concatenate([mine, extra], axis=1))
    hh = sent_to_all(own[pts:] * scales[5], COL).reshape(rank, rank)
    ah = own[:pts] * scales[3]
    return stepped(None, unit, ah, hh, h, 0)[0]


def solution(mesh):
    split = Mesh(mesh.devices.reshape(8, 2, 4, 4), ROW_COL)
    return jax.shard_map(
        shards,
        mesh=split,
        in_specs=(P(ROW_COL, None), P(ROW_COL, None)),
        out_specs=P(ROW_COL, None),
        check_vma=False,
    )
```

```python
import functools
import math

import jax
import jax.numpy as jnp
from jax import lax
from jax.experimental import pallas as pl
from jax.experimental.pallas import tpu as pltpu
from jax.sharding import Mesh
from jax.sharding import PartitionSpec as P

EMBED_WIDTH = 1024
Z, CORE, Y, X = "row_0", "row_1", "col_0", "col_1"
ROW = (Z, CORE)
COL = (Y, X)
ROW_COL = (Z, CORE, Y, X)


def from_ahead(value, axis, steps):
    length = lax.axis_size(axis)
    return lax.ppermute(value, axis, [((i + steps) % length, i) for i in range(length)])


def sent_to_all(value, axes):
    length = math.prod(lax.axis_size(a) for a in axes)
    copies = jnp.broadcast_to(value, (length, *value.shape))
    return lax.all_to_all(copies, axes, split_axis=0, concat_axis=0, tiled=True)


F32, BF16 = jnp.float32, jnp.bfloat16
VMEM = pl.BlockSpec(memory_space=pltpu.VMEM)
LANES = 128


def call(kernel, outs, args, flops, scratch=(), vmem=10, place=pltpu.VMEM, last=pltpu.VMEM):
    size = sum(math.prod(a.shape) * a.dtype.itemsize for a in (*outs, *args))
    return pl.pallas_call(
        kernel,
        out_shape=outs,
        in_specs=[pl.BlockSpec(memory_space=place)] * len(args),
        out_specs=[VMEM] * (len(outs) - 1) + [pl.BlockSpec(memory_space=last)],
        scratch_shapes=list(scratch),
        compiler_params=pltpu.CompilerParams(vmem_limit_bytes=vmem << 20),
        cost_estimate=pl.CostEstimate(flops=flops, bytes_accessed=size, transcendentals=0),
    )(*args)


def rows_dot(a, b):
    return lax.dot_general(a, b, (((1,), (1,)), ((), ())), preferred_element_type=F32)


def squares(rows):
    wide = rows.astype(F32)
    groups = [wide[:, g : g + LANES] for g in range(0, rows.shape[1], LANES)]
    return sum(g * g for g in groups)


def columns_kernel(
    y2, x2, y1, x1, y3, x3, ax0, ax1, ax2, ax3, by0, by1, by2, by3, pts_ref, hb_ref, sq_ref, part_ref, gram_ref
):
    ny, nx = lax.axis_size(Y), lax.axis_size(X)
    y, x = lax.axis_index(Y), lax.axis_index(X)
    half = ax0.shape[0]
    width = pts_ref.shape[1]

    def put(far, near, lower, value):
        at = (lax.rem(y + far, ny) * nx + lax.rem(x + near, nx)) * 2 * half + lower
        at = pl.ds(pl.multiple_of(at, half), half)
        pts_ref[at, :] = value[:, :width]
        hb_ref[at, :] = value[:, width:]

    for near, ref in enumerate((ax0, ax1, ax2, ax3)):
        put(0, near, 0, ref[...])
    for far, ref in enumerate((by0, by1, by2, by3)):
        put(far, 0, half, ref[...])
    for far, ref in enumerate((y1, y2, y3)):
        for near in range(nx):
            put(far + 1, near, 0, ref[near])
    for near, ref in enumerate((x1, x2, x3)):
        for far in range(ny):
            put(far, near + 1, half, ref[far])
    for block in range(pts_ref.shape[0] // LANES):
        sums = squares(pts_ref[block * LANES : (block + 1) * LANES, :])
        sq_ref[block : block + 1, :] = jnp.sum(sums.T, axis=0, keepdims=True)
    gram_ref[...] = lax.dot_general(
        hb_ref[...], hb_ref[...], (((0,), (0,)), ((), ())), preferred_element_type=F32
    )
    part = part_ref.shape[0]
    at = pl.multiple_of((y * nx + x) * part, part)
    part_ref[...] = gram_ref[pl.ds(at, part), :]


def rows_kernel(rows_ref, cols, sq, kern, sums):
    col_sq = jnp.concatenate([sq[g : g + 1, :] for g in range(sq.shape[0])], axis=1)
    tall = 2 * LANES

    def block(i, _):
        at = pl.ds(pl.multiple_of(i * tall, tall), tall)
        rows = rows_ref[at, :]
        row_sq = jnp.sum(squares(rows), axis=1, keepdims=True)
        gram = rows_dot(rows, cols[...])
        values = jnp.exp((2.0 * gram - row_sq - col_sq) * (0.5 / EMBED_WIDTH))
        kern[at, :] = values
        total = sum(values[:, g : g + LANES] for g in range(0, values.shape[1], LANES))
        for j in range(2):
            line = jnp.sum(total[j * LANES : (j + 1) * LANES].T, axis=0, keepdims=True)
            sums[pl.ds(i * 2 + j, 1), :] = line
        return 0

    lax.fori_loop(0, rows_ref.shape[0] // tall, block, 0)


def last_rows_kernel(rows_ref, cols, sq, own_sums, part, more, kern, out, sums):
    rows_kernel(rows_ref, cols, sq, kern, sums)
    core = lax.axis_index(CORE)
    mine = own_sums[...]
    theirs = sums[...]
    lines = 2 * mine.shape[0]
    deep = part.shape[0] // 2
    at = pl.ds(pl.multiple_of(core * deep, deep), deep)
    gram = part[at, :] + more[at, :]
    swap = core == 1
    both = jnp.concatenate(
        [jnp.where(swap, theirs, mine), jnp.where(swap, mine, theirs)], axis=0
    )
    for i in range(out.shape[0]):
        out[i, :lines] = both
        out[i, lines : lines + deep] = gram[:, :LANES]
        out[i, lines + deep :] = gram[:, LANES:]


def means_kernel(got, mean_ref, out):
    z, core = lax.axis_index(Z), lax.axis_index(CORE)
    n = got.shape[0]
    lines = mean_ref.shape[0]
    total = lines * LANES * n
    even, odd = got[0], got[1]
    for i in range(2, n, 2):
        even, odd = even + got[i], odd + got[i + 1]
    sums = even + odd
    means = sums[:lines] / total
    mean_ref[...] = means
    own = mean_ref[pl.ds((core * lax.axis_size(Z) + z) // 2, 1), :]
    band = jnp.broadcast_to(jnp.sum(means, keepdims=True), (1, LANES))
    fill = jnp.zeros((lines - 2, LANES), F32)
    deep = (got.shape[1] - lines) // 2
    pieces = [own, band, fill]
    for at in (lines, lines + deep):
        pieces += [even[at : at + deep], odd[at : at + deep]]
    whole = jnp.concatenate(pieces, axis=0)
    for i in range(out.shape[0]):
        out[i] = whole


def centred_kernel(own, kern, mean_ref, got, hb, aff, partial, *more):
    z, core = lax.axis_index(Z), lax.axis_index(CORE)
    n = got.shape[0]
    total = mean_ref.shape[0] * LANES * n
    which = core if own else 1 - core
    grand = got[0, 1:2, :]
    for i in range(1, n):
        grand = grand + got[i, 1:2, :]
    grand = grand / total
    lane = lax.broadcasted_iota(jnp.int32, (1, LANES), 1)
    odd = lax.rem(z, 2) == 1
    places = []
    for i in range(0, n, 2):
        pair = []
        for j in range(2):
            line = got[i + j, 0:1, :]
            swapped = pltpu.roll(line, LANES // 2, 1)
            pair.append(jnp.where(odd if j == 0 else jnp.logical_not(odd), swapped, line))
        places.append(jnp.where(lane < LANES // 2, pair[0], pair[1]))
    lines = mean_ref.shape[0] // 2
    for i in range(lines):
        line = mean_ref[pl.ds(which * lines + i, 1), :]
        mine = jnp.broadcast_to(line, (LANES, LANES)).T
        at = slice(i * LANES, (i + 1) * LANES)
        for g, place in enumerate(places):
            values = kern[at, g * LANES : (g + 1) * LANES]
            values = values - mine - place + grand
            aff[at, g * LANES : (g + 1) * LANES] = values.astype(BF16)
    partial[...] = jnp.dot(aff[...], hb[...], preferred_element_type=F32)
    if more:
        hh_ref, scales = more
        deep = (got.shape[1] - 8) // 2
        for i in range(n):
            hh_ref[i * deep : (i + 1) * deep, :LANES] = got[i, 8 : 8 + deep, :]
            hh_ref[i * deep : (i + 1) * deep, LANES:] = got[i, 8 + deep :, :]
        hh = hh_ref[...]
        line = lax.broadcasted_iota(jnp.int32, hh.shape, 0)
        place = lax.broadcasted_iota(jnp.int32, hh.shape, 1)
        norm = jnp.sum(jnp.where(line == place, hh, 0.0), axis=0, keepdims=True)
        norm = jnp.sqrt(jnp.maximum(norm, 1e-30))
        grown = norm * (1.05 + 1.05 * total * step_size(hh))
        summed = grown * jnp.max(grown, axis=1, keepdims=True)
        for i, (value, top) in enumerate(((norm, 512.0), (grown, 512.0), (summed, 32768.0))):
            scales[2 * i : 2 * i + 1, :] = top / value
            scales[2 * i + 1 : 2 * i + 2, :] = value / top


def step_size(hh):
    square = jnp.sum(jnp.sum(hh * hh, axis=0, keepdims=True), axis=1, keepdims=True)
    return 0.5 / jnp.sqrt(square + 1e-06)


def start_kernel(unit, points, factor, first, second, copies, value, wide, done):
    half, width = first.shape[0], points.shape[1]
    fetches = [
        pltpu.make_async_copy(points, value, done.at[0]),
        pltpu.make_async_copy(factor, wide, done.at[1]),
    ]
    fetches += [
        pltpu.make_async_copy(points, copies.at[i], done.at[2 + i]) for i in range(copies.shape[0])
    ]
    for fetch in fetches:
        fetch.start()
    fetches[0].wait()
    first[:, :width] = value[:half, :]
    second[:, :width] = value[half:, :]
    fetches[1].wait()
    hb = (wide[...] * unit).astype(BF16)
    first[:, width:] = hb[:half]
    second[:, width:] = hb[half:]
    for fetch in fetches[2:]:
        fetch.wait()


def step_kernel(before, after, ah_ref, hh_ref, h_ref, out, *copies):
    hh = hh_ref[...]
    h = h_ref[...] * before if before else h_ref[...]
    scale = step_size(hh)
    product = jnp.dot(h, hh, precision=lax.Precision.HIGHEST, preferred_element_type=F32)
    h = jnp.maximum(h - scale * (product - ah_ref[...]), 0.0)
    out[...] = h / after if after else h
    if copies:
        hb = h.astype(BF16)
        for i in range(copies[0].shape[0]):
            copies[0][i] = hb


def shards(points, factor):
    nz, ncore, ny, nx = (lax.axis_size(a) for a in ROW_COL)
    nrow, ncol = nz * ncore, ny * nx
    pts, rank = factor.shape
    total = pts * nrow * ncol
    unit = 2.0 / math.sqrt(total * rank)
    width = points.shape[1]
    half = pts // 2
    shape = jax.ShapeDtypeStruct

    first, second, copies = call(
        functools.partial(start_kernel, unit),
        [*[shape((half, width + rank), BF16)] * 2, shape((nz, pts, width), BF16)],
        [points, factor],
        1,
        [
            pltpu.VMEM((pts, width), BF16),
            pltpu.VMEM((pts, rank), F32),
            pltpu.SemaphoreType.DMA((2 + nz,)),
        ],
        vmem=60,
        place=pl.ANY,
        last=pl.ANY,
    )
    tie = lax.optimization_barrier
    along_z = lax.all_to_all(copies, Z, 0, 0, tiled=True)
    x1, x3 = from_ahead(first, X, 1), from_ahead(first, X, -1)
    y1, y3 = from_ahead(second, Y, 1), from_ahead(second, Y, -1)
    x2, y2 = from_ahead(first, X, 2), from_ahead(second, Y, 2)
    x1, x2, x3, y1, y2, y3 = tie((x1, x2, x3, y1, y2, y3))
    by_x = jnp.stack([first, x1, x2, x3])
    by_y = jnp.stack([second, y1, y2, y3])
    y_two, x_two = from_ahead(by_x, Y, 2), from_ahead(by_y, X, 2)
    y_one, x_one = from_ahead(by_x, Y, 1), from_ahead(by_y, X, 1)
    y_three, x_three = from_ahead(by_x, Y, 3), from_ahead(by_y, X, 3)
    far = [y_two, x_two, y_one, x_one, y_three, x_three]
    far, along_z = tie((far, along_z.reshape(-1, width)))
    other = from_ahead(along_z, CORE, 1)
    cols = [*far, first, x1, x2, x3, second, y1, y2, y3]

    part = rank // ncol
    group = nrow * pts
    col_pts, hb_cols, col_sq, own_part = call(
        columns_kernel,
        [
            shape((group, width), BF16),
            shape((group, rank), BF16),
            shape((group // LANES, LANES), F32),
            shape((part, rank), F32),
        ],
        cols,
        2 * group * rank * rank,
        [pltpu.VMEM((rank, rank), F32)],
    )
    more_part = from_ahead(own_part, CORE, 1)
    lines = group // LANES
    own_kern, own_sums = call(
        rows_kernel,
        [shape((group // 2, group), F32), shape((lines // 2, LANES), F32)],
        [along_z, col_pts, col_sq],
        group * group * width,
    )
    other_kern, message = call(
        last_rows_kernel,
        [shape((group // 2, group), F32), shape((nrow, lines + part, LANES), F32)],
        [other, col_pts, col_sq, own_sums, own_part, more_part],
        group * group * width,
        [pltpu.VMEM((lines // 2, LANES), F32)],
    )
    mean_rows, message = call(
        means_kernel,
        [shape((lines, LANES), F32), shape((ncol, 8 + 2 * part, LANES), F32)],
        [lax.all_to_all(message, ROW, 0, 0, tiled=True)],
        1,
    )
    gathered = lax.all_to_all(message, COL, 0, 0, tiled=True)

    def centred(own):
        outs = [shape((group // 2, group), BF16), shape((group // 2, rank), F32)]
        if own:
            outs += [shape((rank, rank), F32), shape((8, rank), F32)]
        return call(
            functools.partial(centred_kernel, own),
            outs,
            [own_kern if own else other_kern, mean_rows, gathered, hb_cols],
            group * group * rank,
        )

    aff_other, partial_other = centred(False)
    got = from_ahead(partial_other, CORE, 1)
    aff_own, partial_own, hh, scales = centred(True)

    def over_z(mine):
        mine = lax.all_to_all(mine.astype(jnp.float16), Z, 0, 0, tiled=True)
        return jnp.sum(mine.astype(F32), axis=0)

    def stepped(before, after, ah, hh, h, copies):
        outs = [shape((pts, rank), F32)] + [shape((ncol, pts, rank), BF16)] * copies
        flops = 12 * pts * rank * rank
        return call(functools.partial(step_kernel, before, after), outs, [ah, hh, h], flops)

    mine = (partial_own + got) * scales[0]
    ah = over_z(mine.reshape(nz, pts, rank)) * scales[1]
    h, hb_cols = stepped(unit, None, ah, hh, factor, 1)

    hb_cols = lax.all_to_all(hb_cols, COL, 0, 0, tiled=True).reshape(group, rank)
    partial_other = jnp.dot(aff_other, hb_cols, preferred_element_type=F32)
    got = from_ahead(partial_other, CORE, 1)
    gram = lax.dot_general(hb_cols, hb_cols, (((0,), (0,)), ((), ())), preferred_element_type=F32)
    own_part = lax.dynamic_slice_in_dim(gram, lax.axis_index(COL) * part, part, 0)
    more_part = from_ahead(own_part, CORE, 1)
    partial_own = jnp.dot(aff_own, hb_cols, preferred_element_type=F32)
    mine = ((partial_own + got) * scales[2]).reshape(nz, pts, rank)
    extra = jnp.broadcast_to((own_part + more_part) * scales[4], (nz, part, rank))
    own = over_z(jnp.concatenate([mine, extra], axis=1))
    hh = sent_to_all(own[pts:] * scales[5], COL).reshape(rank, rank)
    ah = own[:pts] * scales[3]
    return stepped(None, unit, ah, hh, h, 0)[0]


def solution(mesh):
    split = Mesh(mesh.devices.reshape(8, 2, 4, 4), ROW_COL)
    return jax.shard_map(
        shards,
        mesh=split,
        in_specs=(P(ROW_COL, None), P(ROW_COL, None)),
        out_specs=P(ROW_COL, None),
        check_vma=False,
    )
```

```python
import functools
import math

import jax
import jax.numpy as jnp
from jax import lax
from jax.experimental import pallas as pl
from jax.experimental.pallas import tpu as pltpu
from jax.sharding import Mesh
from jax.sharding import PartitionSpec as P

EMBED_WIDTH = 1024
Z, CORE, Y, X = "row_0", "row_1", "col_0", "col_1"
ROW = (Z, CORE)
COL = (Y, X)
ROW_COL = (Z, CORE, Y, X)


def from_ahead(value, axis, steps):
    length = lax.axis_size(axis)
    return lax.ppermute(value, axis, [((i + steps) % length, i) for i in range(length)])


def sent_to_all(value, axes):
    length = math.prod(lax.axis_size(a) for a in axes)
    copies = jnp.broadcast_to(value, (length, *value.shape))
    return lax.all_to_all(copies, axes, split_axis=0, concat_axis=0, tiled=True)


F32, BF16 = jnp.float32, jnp.bfloat16
VMEM = pl.BlockSpec(memory_space=pltpu.VMEM)
LANES = 128


def call(kernel, outs, args, flops, scratch=(), vmem=10, place=pltpu.VMEM, last=pltpu.VMEM):
    size = sum(math.prod(a.shape) * a.dtype.itemsize for a in (*outs, *args))
    return pl.pallas_call(
        kernel,
        out_shape=outs,
        in_specs=[pl.BlockSpec(memory_space=place)] * len(args),
        out_specs=[VMEM] * (len(outs) - 1) + [pl.BlockSpec(memory_space=last)],
        scratch_shapes=list(scratch),
        compiler_params=pltpu.CompilerParams(vmem_limit_bytes=vmem << 20),
        cost_estimate=pl.CostEstimate(flops=flops, bytes_accessed=size, transcendentals=0),
    )(*args)


def rows_dot(a, b):
    return lax.dot_general(a, b, (((1,), (1,)), ((), ())), preferred_element_type=F32)


def squares(rows):
    wide = rows.astype(F32)
    groups = [wide[:, g : g + LANES] for g in range(0, rows.shape[1], LANES)]
    return sum(g * g for g in groups)


def columns_kernel(
    y2, x2, y1, x1, y3, x3, ax0, ax1, ax2, ax3, by0, by1, by2, by3, pts_ref, hb_ref, sq_ref, part_ref, gram_ref
):
    ny, nx = lax.axis_size(Y), lax.axis_size(X)
    y, x = lax.axis_index(Y), lax.axis_index(X)
    half = ax0.shape[0]
    width = pts_ref.shape[1]

    def put(far, near, lower, value):
        at = (lax.rem(y + far, ny) * nx + lax.rem(x + near, nx)) * 2 * half + lower
        at = pl.ds(pl.multiple_of(at, half), half)
        pts_ref[at, :] = value[:, :width]
        hb_ref[at, :] = value[:, width:]

    for near, ref in enumerate((ax0, ax1, ax2, ax3)):
        put(0, near, 0, ref[...])
    for far, ref in enumerate((by0, by1, by2, by3)):
        put(far, 0, half, ref[...])
    for far, ref in enumerate((y1, y2, y3)):
        for near in range(nx):
            put(far + 1, near, 0, ref[near])
    for near, ref in enumerate((x1, x2, x3)):
        for far in range(ny):
            put(far, near + 1, half, ref[far])
    for block in range(pts_ref.shape[0] // LANES):
        sums = squares(pts_ref[block * LANES : (block + 1) * LANES, :])
        sq_ref[block : block + 1, :] = jnp.sum(sums.T, axis=0, keepdims=True)
    gram_ref[...] = lax.dot_general(
        hb_ref[...], hb_ref[...], (((0,), (0,)), ((), ())), preferred_element_type=F32
    )
    part = part_ref.shape[0]
    at = pl.multiple_of((y * nx + x) * part, part)
    part_ref[...] = gram_ref[pl.ds(at, part), :]


def rows_kernel(rows_ref, cols, sq, kern, sums):
    col_sq = jnp.concatenate([sq[g : g + 1, :] for g in range(sq.shape[0])], axis=1)
    tall = 2 * LANES

    def block(i, _):
        at = pl.ds(pl.multiple_of(i * tall, tall), tall)
        rows = rows_ref[at, :]
        row_sq = jnp.sum(squares(rows), axis=1, keepdims=True)
        gram = rows_dot(rows, cols[...])
        values = jnp.exp((2.0 * gram - row_sq - col_sq) * (0.5 / EMBED_WIDTH))
        kern[at, :] = values
        total = sum(values[:, g : g + LANES] for g in range(0, values.shape[1], LANES))
        for j in range(2):
            line = jnp.sum(total[j * LANES : (j + 1) * LANES].T, axis=0, keepdims=True)
            sums[pl.ds(i * 2 + j, 1), :] = line
        return 0

    lax.fori_loop(0, rows_ref.shape[0] // tall, block, 0)


def last_rows_kernel(rows_ref, cols, sq, own_sums, part, more, kern, out, sums):
    rows_kernel(rows_ref, cols, sq, kern, sums)
    core = lax.axis_index(CORE)
    mine = own_sums[...]
    theirs = sums[...]
    lines = 2 * mine.shape[0]
    deep = part.shape[0] // 2
    at = pl.ds(pl.multiple_of(core * deep, deep), deep)
    gram = part[at, :] + more[at, :]
    swap = core == 1
    both = jnp.concatenate(
        [jnp.where(swap, theirs, mine), jnp.where(swap, mine, theirs)], axis=0
    )
    for i in range(out.shape[0]):
        out[i, :lines] = both
        out[i, lines : lines + deep] = gram[:, :LANES]
        out[i, lines + deep :] = gram[:, LANES:]


def means_kernel(got, mean_ref, out):
    z, core = lax.axis_index(Z), lax.axis_index(CORE)
    n = got.shape[0]
    lines = mean_ref.shape[0]
    total = lines * LANES * n
    even, odd = got[0], got[1]
    for i in range(2, n, 2):
        even, odd = even + got[i], odd + got[i + 1]
    sums = even + odd
    means = sums[:lines] / total
    mean_ref[...] = means
    own = mean_ref[pl.ds((core * lax.axis_size(Z) + z) // 2, 1), :]
    band = jnp.broadcast_to(jnp.sum(means, keepdims=True), (1, LANES))
    fill = jnp.zeros((lines - 2, LANES), F32)
    deep = (got.shape[1] - lines) // 2
    pieces = [own, band, fill]
    for at in (lines, lines + deep):
        pieces += [even[at : at + deep], odd[at : at + deep]]
    whole = jnp.concatenate(pieces, axis=0)
    for i in range(out.shape[0]):
        out[i] = whole


def centred_kernel(own, kern, mean_ref, got, hb, aff, partial, *more):
    z, core = lax.axis_index(Z), lax.axis_index(CORE)
    n = got.shape[0]
    total = mean_ref.shape[0] * LANES * n
    which = core if own else 1 - core
    grand = got[0, 1:2, :]
    for i in range(1, n):
        grand = grand + got[i, 1:2, :]
    grand = grand / total
    lane = lax.broadcasted_iota(jnp.int32, (1, LANES), 1)
    odd = lax.rem(z, 2) == 1
    places = []
    for i in range(0, n, 2):
        pair = []
        for j in range(2):
            line = got[i + j, 0:1, :]
            swapped = pltpu.roll(line, LANES // 2, 1)
            pair.append(jnp.where(odd if j == 0 else jnp.logical_not(odd), swapped, line))
        places.append(jnp.where(lane < LANES // 2, pair[0], pair[1]))
    lines = mean_ref.shape[0] // 2
    for i in range(lines):
        line = mean_ref[pl.ds(which * lines + i, 1), :]
        mine = jnp.broadcast_to(line, (LANES, LANES)).T
        at = slice(i * LANES, (i + 1) * LANES)
        for g, place in enumerate(places):
            values = kern[at, g * LANES : (g + 1) * LANES]
            values = values - mine - place + grand
            aff[at, g * LANES : (g + 1) * LANES] = values.astype(BF16)
    partial[...] = jnp.dot(aff[...], hb[...], preferred_element_type=F32)
    if more:
        hh_ref, scales = more
        deep = (got.shape[1] - 8) // 2
        for i in range(n):
            hh_ref[i * deep : (i + 1) * deep, :LANES] = got[i, 8 : 8 + deep, :]
            hh_ref[i * deep : (i + 1) * deep, LANES:] = got[i, 8 + deep :, :]
        hh = hh_ref[...]
        line = lax.broadcasted_iota(jnp.int32, hh.shape, 0)
        place = lax.broadcasted_iota(jnp.int32, hh.shape, 1)
        norm = jnp.sum(jnp.where(line == place, hh, 0.0), axis=0, keepdims=True)
        norm = jnp.sqrt(jnp.maximum(norm, 1e-30))
        grown = norm * (1.05 + 1.05 * total * step_size(hh))
        summed = grown * jnp.max(grown, axis=1, keepdims=True)
        for i, (value, top) in enumerate(((norm, 512.0), (grown, 512.0), (summed, 32768.0))):
            scales[2 * i : 2 * i + 1, :] = top / value
            scales[2 * i + 1 : 2 * i + 2, :] = value / top


def step_size(hh):
    square = jnp.sum(jnp.sum(hh * hh, axis=0, keepdims=True), axis=1, keepdims=True)
    return 0.5 / jnp.sqrt(square + 1e-06)


def start_kernel(unit, points, factor, first, second, copies, value, wide, done):
    half, width = first.shape[0], points.shape[1]
    fetches = [
        pltpu.make_async_copy(points, value, done.at[0]),
        pltpu.make_async_copy(factor, wide, done.at[1]),
    ]
    for fetch in fetches:
        fetch.start()
    fetches[0].wait()
    stores = [
        pltpu.make_async_copy(value, copies.at[i], done.at[2 + i]) for i in range(copies.shape[0])
    ]
    for store in stores:
        store.start()
    first[:, :width] = value[:half, :]
    second[:, :width] = value[half:, :]
    fetches[1].wait()
    hb = (wide[...] * unit).astype(BF16)
    first[:, width:] = hb[:half]
    second[:, width:] = hb[half:]
    for store in stores:
        store.wait()


def step_kernel(before, after, ah_ref, hh_ref, h_ref, out, *copies):
    hh = hh_ref[...]
    h = h_ref[...] * before if before else h_ref[...]
    scale = step_size(hh)
    product = jnp.dot(h, hh, precision=lax.Precision.HIGHEST, preferred_element_type=F32)
    h = jnp.maximum(h - scale * (product - ah_ref[...]), 0.0)
    out[...] = h / after if after else h
    if copies:
        hb = h.astype(BF16)
        for i in range(copies[0].shape[0]):
            copies[0][i] = hb


def shards(points, factor):
    nz, ncore, ny, nx = (lax.axis_size(a) for a in ROW_COL)
    nrow, ncol = nz * ncore, ny * nx
    pts, rank = factor.shape
    total = pts * nrow * ncol
    unit = 2.0 / math.sqrt(total * rank)
    width = points.shape[1]
    half = pts // 2
    shape = jax.ShapeDtypeStruct

    first, second, copies = call(
        functools.partial(start_kernel, unit),
        [*[shape((half, width + rank), BF16)] * 2, shape((nz, pts, width), BF16)],
        [points, factor],
        1,
        [
            pltpu.VMEM((pts, width), BF16),
            pltpu.VMEM((pts, rank), F32),
            pltpu.SemaphoreType.DMA((2 + nz,)),
        ],
        vmem=60,
        place=pl.ANY,
        last=pl.ANY,
    )
    tie = lax.optimization_barrier
    along_z = lax.all_to_all(copies, Z, 0, 0, tiled=True)
    x1, x3 = from_ahead(first, X, 1), from_ahead(first, X, -1)
    y1, y3 = from_ahead(second, Y, 1), from_ahead(second, Y, -1)
    x2, y2 = from_ahead(first, X, 2), from_ahead(second, Y, 2)
    x1, x2, x3, y1, y2, y3 = tie((x1, x2, x3, y1, y2, y3))
    by_x = jnp.stack([first, x1, x2, x3])
    by_y = jnp.stack([second, y1, y2, y3])
    y_two, x_two = from_ahead(by_x, Y, 2), from_ahead(by_y, X, 2)
    y_one, x_one = from_ahead(by_x, Y, 1), from_ahead(by_y, X, 1)
    y_three, x_three = from_ahead(by_x, Y, 3), from_ahead(by_y, X, 3)
    far = [y_two, x_two, y_one, x_one, y_three, x_three]
    far, along_z = tie((far, along_z.reshape(-1, width)))
    other = from_ahead(along_z, CORE, 1)
    cols = [*far, first, x1, x2, x3, second, y1, y2, y3]

    part = rank // ncol
    group = nrow * pts
    col_pts, hb_cols, col_sq, own_part = call(
        columns_kernel,
        [
            shape((group, width), BF16),
            shape((group, rank), BF16),
            shape((group // LANES, LANES), F32),
            shape((part, rank), F32),
        ],
        cols,
        2 * group * rank * rank,
        [pltpu.VMEM((rank, rank), F32)],
    )
    more_part = from_ahead(own_part, CORE, 1)
    lines = group // LANES
    own_kern, own_sums = call(
        rows_kernel,
        [shape((group // 2, group), F32), shape((lines // 2, LANES), F32)],
        [along_z, col_pts, col_sq],
        group * group * width,
    )
    other_kern, message = call(
        last_rows_kernel,
        [shape((group // 2, group), F32), shape((nrow, lines + part, LANES), F32)],
        [other, col_pts, col_sq, own_sums, own_part, more_part],
        group * group * width,
        [pltpu.VMEM((lines // 2, LANES), F32)],
    )
    mean_rows, message = call(
        means_kernel,
        [shape((lines, LANES), F32), shape((ncol, 8 + 2 * part, LANES), F32)],
        [lax.all_to_all(message, ROW, 0, 0, tiled=True)],
        1,
    )
    gathered = lax.all_to_all(message, COL, 0, 0, tiled=True)

    def centred(own):
        outs = [shape((group // 2, group), BF16), shape((group // 2, rank), F32)]
        if own:
            outs += [shape((rank, rank), F32), shape((8, rank), F32)]
        return call(
            functools.partial(centred_kernel, own),
            outs,
            [own_kern if own else other_kern, mean_rows, gathered, hb_cols],
            group * group * rank,
        )

    aff_other, partial_other = centred(False)
    got = from_ahead(partial_other, CORE, 1)
    aff_own, partial_own, hh, scales = centred(True)

    def over_z(mine):
        mine = lax.all_to_all(mine.astype(jnp.float16), Z, 0, 0, tiled=True)
        return jnp.sum(mine.astype(F32), axis=0)

    def stepped(before, after, ah, hh, h, copies):
        outs = [shape((pts, rank), F32)] + [shape((ncol, pts, rank), BF16)] * copies
        flops = 12 * pts * rank * rank
        return call(functools.partial(step_kernel, before, after), outs, [ah, hh, h], flops)

    mine = (partial_own + got) * scales[0]
    ah = over_z(mine.reshape(nz, pts, rank)) * scales[1]
    h, hb_cols = stepped(unit, None, ah, hh, factor, 1)

    hb_cols = lax.all_to_all(hb_cols, COL, 0, 0, tiled=True).reshape(group, rank)
    partial_other = jnp.dot(aff_other, hb_cols, preferred_element_type=F32)
    got = from_ahead(partial_other, CORE, 1)
    gram = lax.dot_general(hb_cols, hb_cols, (((0,), (0,)), ((), ())), preferred_element_type=F32)
    own_part = lax.dynamic_slice_in_dim(gram, lax.axis_index(COL) * part, part, 0)
    more_part = from_ahead(own_part, CORE, 1)
    partial_own = jnp.dot(aff_own, hb_cols, preferred_element_type=F32)
    mine = ((partial_own + got) * scales[2]).reshape(nz, pts, rank)
    extra = jnp.broadcast_to((own_part + more_part) * scales[4], (nz, part, rank))
    own = over_z(jnp.concatenate([mine, extra], axis=1))
    hh = sent_to_all(own[pts:] * scales[5], COL).reshape(rank, rank)
    ah = own[:pts] * scales[3]
    return stepped(None, unit, ah, hh, h, 0)[0]


def solution(mesh):
    split = Mesh(mesh.devices.reshape(8, 2, 4, 4), ROW_COL)
    return jax.shard_map(
        shards,
        mesh=split,
        in_specs=(P(ROW_COL, None), P(ROW_COL, None)),
        out_specs=P(ROW_COL, None),
        check_vma=False,
    )
```

```python
import functools
import math

import jax
import jax.numpy as jnp
from jax import lax
from jax.experimental import pallas as pl
from jax.experimental.pallas import tpu as pltpu
from jax.sharding import Mesh
from jax.sharding import PartitionSpec as P

EMBED_WIDTH = 1024
Z, CORE, Y, X = "row_0", "row_1", "col_0", "col_1"
ROW = (Z, CORE)
COL = (Y, X)
ROW_COL = (Z, CORE, Y, X)


def from_ahead(value, axis, steps):
    length = lax.axis_size(axis)
    return lax.ppermute(value, axis, [((i + steps) % length, i) for i in range(length)])


def sent_to_all(value, axes):
    length = math.prod(lax.axis_size(a) for a in axes)
    copies = jnp.broadcast_to(value, (length, *value.shape))
    return lax.all_to_all(copies, axes, split_axis=0, concat_axis=0, tiled=True)


F32, BF16 = jnp.float32, jnp.bfloat16
VMEM = pl.BlockSpec(memory_space=pltpu.VMEM)
LANES = 128


def call(kernel, outs, args, flops, scratch=(), vmem=10, place=pltpu.VMEM):
    size = sum(math.prod(a.shape) * a.dtype.itemsize for a in (*outs, *args))
    return pl.pallas_call(
        kernel,
        out_shape=outs,
        in_specs=[pl.BlockSpec(memory_space=place)] * len(args),
        out_specs=[VMEM] * len(outs),
        scratch_shapes=list(scratch),
        compiler_params=pltpu.CompilerParams(vmem_limit_bytes=vmem << 20),
        cost_estimate=pl.CostEstimate(flops=flops, bytes_accessed=size, transcendentals=0),
    )(*args)


def rows_dot(a, b):
    return lax.dot_general(a, b, (((1,), (1,)), ((), ())), preferred_element_type=F32)


def squares(rows):
    wide = rows.astype(F32)
    groups = [wide[:, g : g + LANES] for g in range(0, rows.shape[1], LANES)]
    return sum(g * g for g in groups)


def columns_kernel(
    y2, x2, y1, x1, y3, x3, ax0, ax1, ax2, ax3, by0, by1, by2, by3, pts_ref, hb_ref, sq_ref, part_ref, gram_ref
):
    ny, nx = lax.axis_size(Y), lax.axis_size(X)
    y, x = lax.axis_index(Y), lax.axis_index(X)
    half = ax0.shape[0]
    width = pts_ref.shape[1]

    def put(far, near, lower, value):
        at = (lax.rem(y + far, ny) * nx + lax.rem(x + near, nx)) * 2 * half + lower
        at = pl.ds(pl.multiple_of(at, half), half)
        pts_ref[at, :] = value[:, :width]
        hb_ref[at, :] = value[:, width:]

    for near, ref in enumerate((ax0, ax1, ax2, ax3)):
        put(0, near, 0, ref[...])
    for far, ref in enumerate((by0, by1, by2, by3)):
        put(far, 0, half, ref[...])
    for far, ref in enumerate((y1, y2, y3)):
        for near in range(nx):
            put(far + 1, near, 0, ref[near])
    for near, ref in enumerate((x1, x2, x3)):
        for far in range(ny):
            put(far, near + 1, half, ref[far])
    for block in range(pts_ref.shape[0] // LANES):
        sums = squares(pts_ref[block * LANES : (block + 1) * LANES, :])
        sq_ref[block : block + 1, :] = jnp.sum(sums.T, axis=0, keepdims=True)
    gram_ref[...] = lax.dot_general(
        hb_ref[...], hb_ref[...], (((0,), (0,)), ((), ())), preferred_element_type=F32
    )
    part = part_ref.shape[0]
    at = pl.multiple_of((y * nx + x) * part, part)
    part_ref[...] = gram_ref[pl.ds(at, part), :]


def rows_kernel(rows_ref, cols, sq, kern, sums):
    col_sq = jnp.concatenate([sq[g : g + 1, :] for g in range(sq.shape[0])], axis=1)
    tall = 2 * LANES

    def block(i, _):
        at = pl.ds(pl.multiple_of(i * tall, tall), tall)
        rows = rows_ref[at, :]
        row_sq = jnp.sum(squares(rows), axis=1, keepdims=True)
        gram = rows_dot(rows, cols[...])
        values = jnp.exp((2.0 * gram - row_sq - col_sq) * (0.5 / EMBED_WIDTH))
        kern[at, :] = values
        total = sum(values[:, g : g + LANES] for g in range(0, values.shape[1], LANES))
        for j in range(2):
            line = jnp.sum(total[j * LANES : (j + 1) * LANES].T, axis=0, keepdims=True)
            sums[pl.ds(i * 2 + j, 1), :] = line
        return 0

    lax.fori_loop(0, rows_ref.shape[0] // tall, block, 0, unroll=True)


def last_rows_kernel(rows_ref, cols, sq, own_sums, part, more, kern, out, sums):
    rows_kernel(rows_ref, cols, sq, kern, sums)
    core = lax.axis_index(CORE)
    mine = own_sums[...]
    theirs = sums[...]
    lines = 2 * mine.shape[0]
    deep = part.shape[0] // 2
    at = pl.ds(pl.multiple_of(core * deep, deep), deep)
    gram = part[at, :] + more[at, :]
    swap = core == 1
    both = jnp.concatenate(
        [jnp.where(swap, theirs, mine), jnp.where(swap, mine, theirs)], axis=0
    )
    for i in range(out.shape[0]):
        out[i, :lines] = both
        out[i, lines : lines + deep] = gram[:, :LANES]
        out[i, lines + deep :] = gram[:, LANES:]


def means_kernel(got, mean_ref, out):
    z, core = lax.axis_index(Z), lax.axis_index(CORE)
    n = got.shape[0]
    lines = mean_ref.shape[0]
    total = lines * LANES * n
    even, odd = got[0], got[1]
    for i in range(2, n, 2):
        even, odd = even + got[i], odd + got[i + 1]
    sums = even + odd
    means = sums[:lines] / total
    mean_ref[...] = means
    own = mean_ref[pl.ds((core * lax.axis_size(Z) + z) // 2, 1), :]
    band = jnp.broadcast_to(jnp.sum(means, keepdims=True), (1, LANES))
    fill = jnp.zeros((lines - 2, LANES), F32)
    deep = (got.shape[1] - lines) // 2
    pieces = [own, band, fill]
    for at in (lines, lines + deep):
        pieces += [even[at : at + deep], odd[at : at + deep]]
    whole = jnp.concatenate(pieces, axis=0)
    for i in range(out.shape[0]):
        out[i] = whole


def centred_kernel(own, kern, mean_ref, got, hb, aff, partial, *more):
    z, core = lax.axis_index(Z), lax.axis_index(CORE)
    n = got.shape[0]
    total = mean_ref.shape[0] * LANES * n
    which = core if own else 1 - core
    grand = got[0, 1:2, :]
    for i in range(1, n):
        grand = grand + got[i, 1:2, :]
    grand = grand / total
    lane = lax.broadcasted_iota(jnp.int32, (1, LANES), 1)
    odd = lax.rem(z, 2) == 1
    places = []
    for i in range(0, n, 2):
        pair = []
        for j in range(2):
            line = got[i + j, 0:1, :]
            swapped = pltpu.roll(line, LANES // 2, 1)
            pair.append(jnp.where(odd if j == 0 else jnp.logical_not(odd), swapped, line))
        places.append(jnp.where(lane < LANES // 2, pair[0], pair[1]))
    lines = mean_ref.shape[0] // 2
    for i in range(lines):
        line = mean_ref[pl.ds(which * lines + i, 1), :]
        mine = jnp.broadcast_to(line, (LANES, LANES)).T
        at = slice(i * LANES, (i + 1) * LANES)
        for g, place in enumerate(places):
            values = kern[at, g * LANES : (g + 1) * LANES]
            values = values - mine - place + grand
            aff[at, g * LANES : (g + 1) * LANES] = values.astype(BF16)
    partial[...] = jnp.dot(aff[...], hb[...], preferred_element_type=F32)
    if more:
        hh_ref, scales = more
        deep = (got.shape[1] - 8) // 2
        for i in range(n):
            hh_ref[i * deep : (i + 1) * deep, :LANES] = got[i, 8 : 8 + deep, :]
            hh_ref[i * deep : (i + 1) * deep, LANES:] = got[i, 8 + deep :, :]
        hh = hh_ref[...]
        line = lax.broadcasted_iota(jnp.int32, hh.shape, 0)
        place = lax.broadcasted_iota(jnp.int32, hh.shape, 1)
        norm = jnp.sum(jnp.where(line == place, hh, 0.0), axis=0, keepdims=True)
        norm = jnp.sqrt(jnp.maximum(norm, 1e-30))
        grown = norm * (1.05 + 1.05 * total * step_size(hh))
        summed = grown * jnp.max(grown, axis=1, keepdims=True)
        for i, (value, top) in enumerate(((norm, 512.0), (grown, 512.0), (summed, 32768.0))):
            scales[2 * i : 2 * i + 1, :] = top / value
            scales[2 * i + 1 : 2 * i + 2, :] = value / top


def step_size(hh):
    square = jnp.sum(jnp.sum(hh * hh, axis=0, keepdims=True), axis=1, keepdims=True)
    return 0.5 / jnp.sqrt(square + 1e-06)


def start_kernel(unit, points, factor, first, second, copies, wide, done):
    half, width = first.shape[0], points.shape[1]
    fetches = [
        pltpu.make_async_copy(points, copies.at[0], done.at[0]),
        pltpu.make_async_copy(factor, wide, done.at[1]),
    ]
    for fetch in fetches:
        fetch.start()
    for fetch in fetches:
        fetch.wait()
    value = copies[0]
    hb = (wide[...] * unit).astype(BF16)
    first[:, :width] = value[:half]
    first[:, width:] = hb[:half]
    second[:, :width] = value[half:]
    second[:, width:] = hb[half:]
    for i in range(1, copies.shape[0]):
        copies[i] = value


def step_kernel(before, after, ah_ref, hh_ref, h_ref, out, *copies):
    hh = hh_ref[...]
    h = h_ref[...] * before if before else h_ref[...]
    scale = step_size(hh)
    product = jnp.dot(h, hh, precision=lax.Precision.HIGHEST, preferred_element_type=F32)
    h = jnp.maximum(h - scale * (product - ah_ref[...]), 0.0)
    out[...] = h / after if after else h
    if copies:
        hb = h.astype(BF16)
        for i in range(copies[0].shape[0]):
            copies[0][i] = hb


def shards(points, factor):
    nz, ncore, ny, nx = (lax.axis_size(a) for a in ROW_COL)
    nrow, ncol = nz * ncore, ny * nx
    pts, rank = factor.shape
    total = pts * nrow * ncol
    unit = 2.0 / math.sqrt(total * rank)
    width = points.shape[1]
    half = pts // 2
    shape = jax.ShapeDtypeStruct

    first, second, copies = call(
        functools.partial(start_kernel, unit),
        [*[shape((half, width + rank), BF16)] * 2, shape((nz, pts, width), BF16)],
        [points, factor],
        1,
        [pltpu.VMEM((pts, rank), F32), pltpu.SemaphoreType.DMA((2,))],
        vmem=60,
        place=pl.ANY,
    )
    tie = lax.optimization_barrier
    along_z = lax.all_to_all(copies, Z, 0, 0, tiled=True)
    x1, x3 = from_ahead(first, X, 1), from_ahead(first, X, -1)
    y1, y3 = from_ahead(second, Y, 1), from_ahead(second, Y, -1)
    x2, y2 = from_ahead(first, X, 2), from_ahead(second, Y, 2)
    x1, x2, x3, y1, y2, y3 = tie((x1, x2, x3, y1, y2, y3))
    by_x = jnp.stack([first, x1, x2, x3])
    by_y = jnp.stack([second, y1, y2, y3])
    y_two, x_two = from_ahead(by_x, Y, 2), from_ahead(by_y, X, 2)
    y_one, x_one = from_ahead(by_x, Y, 1), from_ahead(by_y, X, 1)
    y_three, x_three = from_ahead(by_x, Y, 3), from_ahead(by_y, X, 3)
    far = [y_two, x_two, y_one, x_one, y_three, x_three]
    far, along_z = tie((far, along_z.reshape(-1, width)))
    other = from_ahead(along_z, CORE, 1)
    cols = [*far, first, x1, x2, x3, second, y1, y2, y3]

    part = rank // ncol
    group = nrow * pts
    col_pts, hb_cols, col_sq, own_part = call(
        columns_kernel,
        [
            shape((group, width), BF16),
            shape((group, rank), BF16),
            shape((group // LANES, LANES), F32),
            shape((part, rank), F32),
        ],
        cols,
        2 * group * rank * rank,
        [pltpu.VMEM((rank, rank), F32)],
    )
    more_part = from_ahead(own_part, CORE, 1)
    lines = group // LANES
    own_kern, own_sums = call(
        rows_kernel,
        [shape((group // 2, group), F32), shape((lines // 2, LANES), F32)],
        [along_z, col_pts, col_sq],
        group * group * width,
    )
    other_kern, message = call(
        last_rows_kernel,
        [shape((group // 2, group), F32), shape((nrow, lines + part, LANES), F32)],
        [other, col_pts, col_sq, own_sums, own_part, more_part],
        group * group * width,
        [pltpu.VMEM((lines // 2, LANES), F32)],
    )
    mean_rows, message = call(
        means_kernel,
        [shape((lines, LANES), F32), shape((ncol, 8 + 2 * part, LANES), F32)],
        [lax.all_to_all(message, ROW, 0, 0, tiled=True)],
        1,
    )
    gathered = lax.all_to_all(message, COL, 0, 0, tiled=True)

    def centred(own):
        outs = [shape((group // 2, group), BF16), shape((group // 2, rank), F32)]
        if own:
            outs += [shape((rank, rank), F32), shape((8, rank), F32)]
        return call(
            functools.partial(centred_kernel, own),
            outs,
            [own_kern if own else other_kern, mean_rows, gathered, hb_cols],
            group * group * rank,
        )

    aff_other, partial_other = centred(False)
    got = from_ahead(partial_other, CORE, 1)
    aff_own, partial_own, hh, scales = centred(True)

    def over_z(mine):
        mine = lax.all_to_all(mine.astype(jnp.float16), Z, 0, 0, tiled=True)
        return jnp.sum(mine.astype(F32), axis=0)

    def stepped(before, after, ah, hh, h, copies):
        outs = [shape((pts, rank), F32)] + [shape((ncol, pts, rank), BF16)] * copies
        flops = 12 * pts * rank * rank
        return call(functools.partial(step_kernel, before, after), outs, [ah, hh, h], flops)

    mine = (partial_own + got) * scales[0]
    ah = over_z(mine.reshape(nz, pts, rank)) * scales[1]
    h, hb_cols = stepped(unit, None, ah, hh, factor, 1)

    hb_cols = lax.all_to_all(hb_cols, COL, 0, 0, tiled=True).reshape(group, rank)
    partial_other = jnp.dot(aff_other, hb_cols, preferred_element_type=F32)
    got = from_ahead(partial_other, CORE, 1)
    gram = lax.dot_general(hb_cols, hb_cols, (((0,), (0,)), ((), ())), preferred_element_type=F32)
    own_part = lax.dynamic_slice_in_dim(gram, lax.axis_index(COL) * part, part, 0)
    more_part = from_ahead(own_part, CORE, 1)
    partial_own = jnp.dot(aff_own, hb_cols, preferred_element_type=F32)
    mine = ((partial_own + got) * scales[2]).reshape(nz, pts, rank)
    extra = jnp.broadcast_to((own_part + more_part) * scales[4], (nz, part, rank))
    own = over_z(jnp.concatenate([mine, extra], axis=1))
    hh = sent_to_all(own[pts:] * scales[5], COL).reshape(rank, rank)
    ah = own[:pts] * scales[3]
    return stepped(None, unit, ah, hh, h, 0)[0]


def solution(mesh):
    split = Mesh(mesh.devices.reshape(8, 2, 4, 4), ROW_COL)
    return jax.shard_map(
        shards,
        mesh=split,
        in_specs=(P(ROW_COL, None), P(ROW_COL, None)),
        out_specs=P(ROW_COL, None),
        check_vma=False,
    )
```

```python
import functools
import math

import jax
import jax.numpy as jnp
from jax import lax
from jax.experimental import pallas as pl
from jax.experimental.pallas import tpu as pltpu
from jax.sharding import Mesh
from jax.sharding import PartitionSpec as P

EMBED_WIDTH = 1024
Z, CORE, Y, X = "row_0", "row_1", "col_0", "col_1"
ROW = (Z, CORE)
COL = (Y, X)
ROW_COL = (Z, CORE, Y, X)


def from_ahead(value, axis, steps):
    length = lax.axis_size(axis)
    return lax.ppermute(value, axis, [((i + steps) % length, i) for i in range(length)])


def sent_to_all(value, axes):
    length = math.prod(lax.axis_size(a) for a in axes)
    copies = jnp.broadcast_to(value, (length, *value.shape))
    return lax.all_to_all(copies, axes, split_axis=0, concat_axis=0, tiled=True)


F32, BF16 = jnp.float32, jnp.bfloat16
VMEM = pl.BlockSpec(memory_space=pltpu.VMEM)
LANES = 128


def call(kernel, outs, args, flops, scratch=(), vmem=10, place=pltpu.VMEM):
    size = sum(math.prod(a.shape) * a.dtype.itemsize for a in (*outs, *args))
    return pl.pallas_call(
        kernel,
        out_shape=outs,
        in_specs=[pl.BlockSpec(memory_space=place)] * len(args),
        out_specs=[VMEM] * len(outs),
        scratch_shapes=list(scratch),
        compiler_params=pltpu.CompilerParams(vmem_limit_bytes=vmem << 20),
        cost_estimate=pl.CostEstimate(flops=flops, bytes_accessed=size, transcendentals=0),
    )(*args)


def rows_dot(a, b):
    return lax.dot_general(a, b, (((1,), (1,)), ((), ())), preferred_element_type=F32)


def squares(rows):
    wide = rows.astype(F32)
    groups = [wide[:, g : g + LANES] for g in range(0, rows.shape[1], LANES)]
    return sum(g * g for g in groups)


def columns_kernel(
    x3, y3, x1, y1, x2, y2, ax0, ax1, ax2, ax3, by0, by1, by2, by3, pts_ref, hb_ref, sq_ref, part_ref, gram_ref
):
    ny, nx = lax.axis_size(Y), lax.axis_size(X)
    y, x = lax.axis_index(Y), lax.axis_index(X)
    half = ax0.shape[0]
    width = pts_ref.shape[1]

    def put(far, near, lower, value):
        at = (lax.rem(y + far, ny) * nx + lax.rem(x + near, nx)) * 2 * half + lower
        at = pl.ds(pl.multiple_of(at, half), half)
        pts_ref[at, :] = value[:, :width]
        hb_ref[at, :] = value[:, width:]

    for near, ref in enumerate((ax0, ax1, ax2, ax3)):
        put(0, near, 0, ref[...])
    for far, ref in enumerate((by0, by1, by2, by3)):
        put(far, 0, half, ref[...])
    for far, ref in enumerate((y1, y2, y3)):
        for near in range(nx):
            put(far + 1, near, 0, ref[near])
    for near, ref in enumerate((x1, x2, x3)):
        for far in range(ny):
            put(far, near + 1, half, ref[far])
    for block in range(pts_ref.shape[0] // LANES):
        sums = squares(pts_ref[block * LANES : (block + 1) * LANES, :])
        sq_ref[block : block + 1, :] = jnp.sum(sums.T, axis=0, keepdims=True)
    gram_ref[...] = lax.dot_general(
        hb_ref[...], hb_ref[...], (((0,), (0,)), ((), ())), preferred_element_type=F32
    )
    part = part_ref.shape[0]
    at = pl.multiple_of((y * nx + x) * part, part)
    part_ref[...] = gram_ref[pl.ds(at, part), :]


def rows_kernel(rows_ref, cols, sq, kern, sums):
    col_sq = jnp.concatenate([sq[g : g + 1, :] for g in range(sq.shape[0])], axis=1)
    tall = 2 * LANES

    def block(i, _):
        at = pl.ds(pl.multiple_of(i * tall, tall), tall)
        rows = rows_ref[at, :]
        row_sq = jnp.sum(squares(rows), axis=1, keepdims=True)
        gram = rows_dot(rows, cols[...])
        values = jnp.exp((2.0 * gram - row_sq - col_sq) * (0.5 / EMBED_WIDTH))
        kern[at, :] = values
        total = sum(values[:, g : g + LANES] for g in range(0, values.shape[1], LANES))
        for j in range(2):
            line = jnp.sum(total[j * LANES : (j + 1) * LANES].T, axis=0, keepdims=True)
            sums[pl.ds(i * 2 + j, 1), :] = line
        return 0

    lax.fori_loop(0, rows_ref.shape[0] // tall, block, 0, unroll=True)


def last_rows_kernel(rows_ref, cols, sq, own_sums, part, more, kern, out, sums):
    rows_kernel(rows_ref, cols, sq, kern, sums)
    core = lax.axis_index(CORE)
    mine = own_sums[...]
    theirs = sums[...]
    lines = 2 * mine.shape[0]
    deep = part.shape[0] // 2
    at = pl.ds(pl.multiple_of(core * deep, deep), deep)
    gram = part[at, :] + more[at, :]
    swap = core == 1
    both = jnp.concatenate(
        [jnp.where(swap, theirs, mine), jnp.where(swap, mine, theirs)], axis=0
    )
    for i in range(out.shape[0]):
        out[i, :lines] = both
        out[i, lines : lines + deep] = gram[:, :LANES]
        out[i, lines + deep :] = gram[:, LANES:]


def means_kernel(got, mean_ref, out):
    z, core = lax.axis_index(Z), lax.axis_index(CORE)
    n = got.shape[0]
    lines = mean_ref.shape[0]
    total = lines * LANES * n
    even, odd = got[0], got[1]
    for i in range(2, n, 2):
        even, odd = even + got[i], odd + got[i + 1]
    sums = even + odd
    means = sums[:lines] / total
    mean_ref[...] = means
    own = mean_ref[pl.ds((core * lax.axis_size(Z) + z) // 2, 1), :]
    band = jnp.broadcast_to(jnp.sum(means, keepdims=True), (1, LANES))
    fill = jnp.zeros((lines - 2, LANES), F32)
    deep = (got.shape[1] - lines) // 2
    pieces = [own, band, fill]
    for at in (lines, lines + deep):
        pieces += [even[at : at + deep], odd[at : at + deep]]
    whole = jnp.concatenate(pieces, axis=0)
    for i in range(out.shape[0]):
        out[i] = whole


def centred_kernel(own, kern, mean_ref, got, hb, aff, partial, *more):
    z, core = lax.axis_index(Z), lax.axis_index(CORE)
    n = got.shape[0]
    total = mean_ref.shape[0] * LANES * n
    which = core if own else 1 - core
    grand = got[0, 1:2, :]
    for i in range(1, n):
        grand = grand + got[i, 1:2, :]
    grand = grand / total
    lane = lax.broadcasted_iota(jnp.int32, (1, LANES), 1)
    odd = lax.rem(z, 2) == 1
    places = []
    for i in range(0, n, 2):
        pair = []
        for j in range(2):
            line = got[i + j, 0:1, :]
            swapped = pltpu.roll(line, LANES // 2, 1)
            pair.append(jnp.where(odd if j == 0 else jnp.logical_not(odd), swapped, line))
        places.append(jnp.where(lane < LANES // 2, pair[0], pair[1]))
    lines = mean_ref.shape[0] // 2
    for i in range(lines):
        line = mean_ref[pl.ds(which * lines + i, 1), :]
        mine = jnp.broadcast_to(line, (LANES, LANES)).T
        at = slice(i * LANES, (i + 1) * LANES)
        for g, place in enumerate(places):
            values = kern[at, g * LANES : (g + 1) * LANES]
            values = values - mine - place + grand
            aff[at, g * LANES : (g + 1) * LANES] = values.astype(BF16)
    partial[...] = jnp.dot(aff[...], hb[...], preferred_element_type=F32)
    if more:
        hh_ref, scales = more
        deep = (got.shape[1] - 8) // 2
        for i in range(n):
            hh_ref[i * deep : (i + 1) * deep, :LANES] = got[i, 8 : 8 + deep, :]
            hh_ref[i * deep : (i + 1) * deep, LANES:] = got[i, 8 + deep :, :]
        hh = hh_ref[...]
        line = lax.broadcasted_iota(jnp.int32, hh.shape, 0)
        place = lax.broadcasted_iota(jnp.int32, hh.shape, 1)
        norm = jnp.sum(jnp.where(line == place, hh, 0.0), axis=0, keepdims=True)
        norm = jnp.sqrt(jnp.maximum(norm, 1e-30))
        grown = norm * (1.05 + 1.05 * total * step_size(hh))
        summed = grown * jnp.max(grown, axis=1, keepdims=True)
        for i, (value, top) in enumerate(((norm, 512.0), (grown, 512.0), (summed, 32768.0))):
            scales[2 * i : 2 * i + 1, :] = top / value
            scales[2 * i + 1 : 2 * i + 2, :] = value / top


def step_size(hh):
    square = jnp.sum(jnp.sum(hh * hh, axis=0, keepdims=True), axis=1, keepdims=True)
    return 0.5 / jnp.sqrt(square + 1e-06)


def gram_kernel(hb, part_ref, gram_ref):
    gram_ref[...] = lax.dot_general(
        hb[...], hb[...], (((0,), (0,)), ((), ())), preferred_element_type=F32
    )
    part = part_ref.shape[0]
    at = pl.multiple_of(lax.axis_index(COL) * part, part)
    part_ref[...] = gram_ref[pl.ds(at, part), :]


def start_kernel(unit, points, factor, first, second, copies, wide, done):
    half, width = first.shape[0], points.shape[1]
    fetches = [
        pltpu.make_async_copy(points, copies.at[0], done.at[0]),
        pltpu.make_async_copy(factor, wide, done.at[1]),
    ]
    for fetch in fetches:
        fetch.start()
    for fetch in fetches:
        fetch.wait()
    value = copies[0]
    hb = (wide[...] * unit).astype(BF16)
    first[:, :width] = value[:half]
    first[:, width:] = hb[:half]
    second[:, :width] = value[half:]
    second[:, width:] = hb[half:]
    for i in range(1, copies.shape[0]):
        copies[i] = value


def step_kernel(before, after, ah_ref, hh_ref, h_ref, out, *copies):
    hh = hh_ref[...]
    h = h_ref[...] * before if before else h_ref[...]
    scale = step_size(hh)
    product = jnp.dot(h, hh, precision=lax.Precision.HIGHEST, preferred_element_type=F32)
    h = jnp.maximum(h - scale * (product - ah_ref[...]), 0.0)
    out[...] = h / after if after else h
    if copies:
        hb = h.astype(BF16)
        for i in range(copies[0].shape[0]):
            copies[0][i] = hb


def shards(points, factor):
    nz, ncore, ny, nx = (lax.axis_size(a) for a in ROW_COL)
    nrow, ncol = nz * ncore, ny * nx
    pts, rank = factor.shape
    total = pts * nrow * ncol
    unit = 2.0 / math.sqrt(total * rank)
    width = points.shape[1]
    half = pts // 2
    shape = jax.ShapeDtypeStruct

    first, second, copies = call(
        functools.partial(start_kernel, unit),
        [*[shape((half, width + rank), BF16)] * 2, shape((nz, pts, width), BF16)],
        [points, factor],
        1,
        [pltpu.VMEM((pts, rank), F32), pltpu.SemaphoreType.DMA((2,))],
        vmem=60,
        place=pl.ANY,
    )
    tie = lax.optimization_barrier
    along_z = lax.all_to_all(copies, Z, 0, 0, tiled=True)
    x1, x3 = from_ahead(first, X, 1), from_ahead(first, X, -1)
    y1, y3 = from_ahead(second, Y, 1), from_ahead(second, Y, -1)
    x2, y2 = from_ahead(first, X, 2), from_ahead(second, Y, 2)
    x1, x2, x3, y1, y2, y3 = tie((x1, x2, x3, y1, y2, y3))
    by_x = jnp.stack([first, x1, x2, x3])
    by_y = jnp.stack([second, y1, y2, y3])
    by_x, by_y = tie((by_x, by_y))
    y_three, x_three = from_ahead(by_x, Y, 3), from_ahead(by_y, X, 3)
    y_one, x_one = from_ahead(by_x, Y, 1), from_ahead(by_y, X, 1)
    y_two, x_two = from_ahead(by_x, Y, 2), from_ahead(by_y, X, 2)
    far = [x_three, y_three, x_one, y_one, x_two, y_two]
    far, along_z = tie((far, along_z.reshape(-1, width)))
    other = from_ahead(along_z, CORE, 1)
    cols = [*far, first, x1, x2, x3, second, y1, y2, y3]

    part = rank // ncol
    group = nrow * pts
    col_pts, hb_cols, col_sq, own_part = call(
        columns_kernel,
        [
            shape((group, width), BF16),
            shape((group, rank), BF16),
            shape((group // LANES, LANES), F32),
            shape((part, rank), F32),
        ],
        cols,
        2 * group * rank * rank,
        [pltpu.VMEM((rank, rank), F32)],
    )
    more_part = from_ahead(own_part, CORE, 1)
    lines = group // LANES
    own_kern, own_sums = call(
        rows_kernel,
        [shape((group // 2, group), F32), shape((lines // 2, LANES), F32)],
        [along_z, col_pts, col_sq],
        group * group * width,
    )
    other_kern, message = call(
        last_rows_kernel,
        [shape((group // 2, group), F32), shape((nrow, lines + part, LANES), F32)],
        [other, col_pts, col_sq, own_sums, own_part, more_part],
        group * group * width,
        [pltpu.VMEM((lines // 2, LANES), F32)],
    )
    mean_rows, message = call(
        means_kernel,
        [shape((lines, LANES), F32), shape((ncol, 8 + 2 * part, LANES), F32)],
        [lax.all_to_all(message, ROW, 0, 0, tiled=True)],
        1,
    )
    gathered = lax.all_to_all(message, COL, 0, 0, tiled=True)

    def centred(own):
        outs = [shape((group // 2, group), BF16), shape((group // 2, rank), F32)]
        if own:
            outs += [shape((rank, rank), F32), shape((8, rank), F32)]
        return call(
            functools.partial(centred_kernel, own),
            outs,
            [own_kern if own else other_kern, mean_rows, gathered, hb_cols],
            group * group * rank,
        )

    aff_other, partial_other = centred(False)
    got = from_ahead(partial_other, CORE, 1)
    aff_own, partial_own, hh, scales = centred(True)

    def over_z(mine):
        mine = lax.all_to_all(mine.astype(jnp.float16), Z, 0, 0, tiled=True)
        return jnp.sum(mine.astype(F32), axis=0)

    def stepped(before, after, ah, hh, h, copies):
        outs = [shape((pts, rank), F32)] + [shape((ncol, pts, rank), BF16)] * copies
        flops = 12 * pts * rank * rank
        return call(functools.partial(step_kernel, before, after), outs, [ah, hh, h], flops)

    mine = (partial_own + got) * scales[0]
    ah = over_z(mine.reshape(nz, pts, rank)) * scales[1]
    h, hb_cols = stepped(unit, None, ah, hh, factor, 1)

    hb_cols = lax.all_to_all(hb_cols, COL, 0, 0, tiled=True).reshape(group, rank)
    partial_other = jnp.dot(aff_other, hb_cols, preferred_element_type=F32)
    got = from_ahead(partial_other, CORE, 1)
    (own_part,) = call(
        gram_kernel,
        [shape((part, rank), F32)],
        [hb_cols],
        2 * group * rank * rank,
        [pltpu.VMEM((rank, rank), F32)],
    )
    more_part = from_ahead(own_part, CORE, 1)
    partial_own = jnp.dot(aff_own, hb_cols, preferred_element_type=F32)
    mine = ((partial_own + got) * scales[2]).reshape(nz, pts, rank)
    extra = jnp.broadcast_to((own_part + more_part) * scales[4], (nz, part, rank))
    own = over_z(jnp.concatenate([mine, extra], axis=1))
    hh = sent_to_all(own[pts:] * scales[5], COL).reshape(rank, rank)
    ah = own[:pts] * scales[3]
    return stepped(None, unit, ah, hh, h, 0)[0]


def solution(mesh):
    split = Mesh(mesh.devices.reshape(8, 2, 4, 4), ROW_COL)
    return jax.shard_map(
        shards,
        mesh=split,
        in_specs=(P(ROW_COL, None), P(ROW_COL, None)),
        out_specs=P(ROW_COL, None),
        check_vma=False,
    )
```

```python
import functools
import math

import jax
import jax.numpy as jnp
from jax import lax
from jax.experimental import pallas as pl
from jax.experimental.pallas import tpu as pltpu
from jax.sharding import Mesh
from jax.sharding import PartitionSpec as P

EMBED_WIDTH = 1024
Z, CORE, Y, X = "row_0", "row_1", "col_0", "col_1"
ROW = (Z, CORE)
COL = (Y, X)
ROW_COL = (Z, CORE, Y, X)


def from_ahead(value, axis, steps):
    length = lax.axis_size(axis)
    return lax.ppermute(value, axis, [((i + steps) % length, i) for i in range(length)])


def sent_to_all(value, axes):
    length = math.prod(lax.axis_size(a) for a in axes)
    copies = jnp.broadcast_to(value, (length, *value.shape))
    return lax.all_to_all(copies, axes, split_axis=0, concat_axis=0, tiled=True)


F32, BF16 = jnp.float32, jnp.bfloat16
VMEM = pl.BlockSpec(memory_space=pltpu.VMEM)
LANES = 128


def call(kernel, outs, args, flops, scratch=(), vmem=10, place=pltpu.VMEM):
    size = sum(math.prod(a.shape) * a.dtype.itemsize for a in (*outs, *args))
    return pl.pallas_call(
        kernel,
        out_shape=outs,
        in_specs=[pl.BlockSpec(memory_space=place)] * len(args),
        out_specs=[VMEM] * len(outs),
        scratch_shapes=list(scratch),
        compiler_params=pltpu.CompilerParams(vmem_limit_bytes=vmem << 20),
        cost_estimate=pl.CostEstimate(flops=flops, bytes_accessed=size, transcendentals=0),
    )(*args)


def rows_dot(a, b):
    return lax.dot_general(a, b, (((1,), (1,)), ((), ())), preferred_element_type=F32)


def squares(rows):
    wide = rows.astype(F32)
    groups = [wide[:, g : g + LANES] for g in range(0, rows.shape[1], LANES)]
    return sum(g * g for g in groups)


def columns_kernel(
    x3, y3, x1, y1, x2, y2, ax0, ax1, ax2, ax3, by0, by1, by2, by3, pts_ref, hb_ref, sq_ref, part_ref, gram_ref
):
    ny, nx = lax.axis_size(Y), lax.axis_size(X)
    y, x = lax.axis_index(Y), lax.axis_index(X)
    half = ax0.shape[0]
    width = pts_ref.shape[1]

    def put(far, near, lower, value):
        at = (lax.rem(y + far, ny) * nx + lax.rem(x + near, nx)) * 2 * half + lower
        at = pl.ds(pl.multiple_of(at, half), half)
        pts_ref[at, :] = value[:, :width]
        hb_ref[at, :] = value[:, width:]

    for near, ref in enumerate((ax0, ax1, ax2, ax3)):
        put(0, near, 0, ref[...])
    for far, ref in enumerate((by0, by1, by2, by3)):
        put(far, 0, half, ref[...])
    for far, ref in enumerate((y1, y2, y3)):
        for near in range(nx):
            put(far + 1, near, 0, ref[near])
    for near, ref in enumerate((x1, x2, x3)):
        for far in range(ny):
            put(far, near + 1, half, ref[far])
    for block in range(pts_ref.shape[0] // LANES):
        sums = squares(pts_ref[block * LANES : (block + 1) * LANES, :])
        sq_ref[block : block + 1, :] = jnp.sum(sums.T, axis=0, keepdims=True)
    gram_ref[...] = lax.dot_general(
        hb_ref[...], hb_ref[...], (((0,), (0,)), ((), ())), preferred_element_type=F32
    )
    part = part_ref.shape[0]
    at = pl.multiple_of((y * nx + x) * part, part)
    part_ref[...] = gram_ref[pl.ds(at, part), :]


def rows_kernel(rows_ref, cols, sq, kern, sums):
    col_sq = jnp.concatenate([sq[g : g + 1, :] for g in range(sq.shape[0])], axis=1)
    tall = 2 * LANES

    def block(i, _):
        at = pl.ds(pl.multiple_of(i * tall, tall), tall)
        rows = rows_ref[at, :]
        row_sq = jnp.sum(squares(rows), axis=1, keepdims=True)
        gram = rows_dot(rows, cols[...])
        values = jnp.exp((2.0 * gram - row_sq - col_sq) * (0.5 / EMBED_WIDTH))
        kern[at, :] = values
        total = sum(values[:, g : g + LANES] for g in range(0, values.shape[1], LANES))
        for j in range(2):
            line = jnp.sum(total[j * LANES : (j + 1) * LANES].T, axis=0, keepdims=True)
            sums[pl.ds(i * 2 + j, 1), :] = line
        return 0

    lax.fori_loop(0, rows_ref.shape[0] // tall, block, 0, unroll=True)


def last_rows_kernel(rows_ref, cols, sq, own_sums, part, more, kern, out, sums):
    rows_kernel(rows_ref, cols, sq, kern, sums)
    core = lax.axis_index(CORE)
    mine = own_sums[...]
    theirs = sums[...]
    lines = 2 * mine.shape[0]
    deep = part.shape[0] // 2
    at = pl.ds(pl.multiple_of(core * deep, deep), deep)
    gram = part[at, :] + more[at, :]
    swap = core == 1
    both = jnp.concatenate(
        [jnp.where(swap, theirs, mine), jnp.where(swap, mine, theirs)], axis=0
    )
    for i in range(out.shape[0]):
        out[i, :lines] = both
        out[i, lines : lines + deep] = gram[:, :LANES]
        out[i, lines + deep :] = gram[:, LANES:]


def means_kernel(got, mean_ref, out):
    z, core = lax.axis_index(Z), lax.axis_index(CORE)
    n = got.shape[0]
    lines = mean_ref.shape[0]
    total = lines * LANES * n
    even, odd = got[0], got[1]
    for i in range(2, n, 2):
        even, odd = even + got[i], odd + got[i + 1]
    sums = even + odd
    means = sums[:lines] / total
    mean_ref[...] = means
    own = mean_ref[pl.ds((core * lax.axis_size(Z) + z) // 2, 1), :]
    band = jnp.broadcast_to(jnp.sum(means, keepdims=True), (1, LANES))
    fill = jnp.zeros((lines - 2, LANES), F32)
    deep = (got.shape[1] - lines) // 2
    pieces = [own, band, fill]
    for at in (lines, lines + deep):
        pieces += [even[at : at + deep], odd[at : at + deep]]
    whole = jnp.concatenate(pieces, axis=0)
    for i in range(out.shape[0]):
        out[i] = whole


def centred_kernel(own, kern, mean_ref, got, hb, aff, partial, *more):
    z, core = lax.axis_index(Z), lax.axis_index(CORE)
    n = got.shape[0]
    total = mean_ref.shape[0] * LANES * n
    which = core if own else 1 - core
    grand = got[0, 1:2, :]
    for i in range(1, n):
        grand = grand + got[i, 1:2, :]
    grand = grand / total
    lane = lax.broadcasted_iota(jnp.int32, (1, LANES), 1)
    odd = lax.rem(z, 2) == 1
    places = []
    for i in range(0, n, 2):
        pair = []
        for j in range(2):
            line = got[i + j, 0:1, :]
            swapped = pltpu.roll(line, LANES // 2, 1)
            pair.append(jnp.where(odd if j == 0 else jnp.logical_not(odd), swapped, line))
        places.append(jnp.where(lane < LANES // 2, pair[0], pair[1]))
    lines = mean_ref.shape[0] // 2
    for i in range(lines):
        line = mean_ref[pl.ds(which * lines + i, 1), :]
        mine = jnp.broadcast_to(line, (LANES, LANES)).T
        at = slice(i * LANES, (i + 1) * LANES)
        for g, place in enumerate(places):
            values = kern[at, g * LANES : (g + 1) * LANES]
            values = values - mine - place + grand
            aff[at, g * LANES : (g + 1) * LANES] = values.astype(BF16)
    partial[...] = jnp.dot(aff[...], hb[...], preferred_element_type=F32)
    if more:
        hh_ref, scales = more
        deep = (got.shape[1] - 8) // 2
        for i in range(n):
            hh_ref[i * deep : (i + 1) * deep, :LANES] = got[i, 8 : 8 + deep, :]
            hh_ref[i * deep : (i + 1) * deep, LANES:] = got[i, 8 + deep :, :]
        hh = hh_ref[...]
        line = lax.broadcasted_iota(jnp.int32, hh.shape, 0)
        place = lax.broadcasted_iota(jnp.int32, hh.shape, 1)
        norm = jnp.sum(jnp.where(line == place, hh, 0.0), axis=0, keepdims=True)
        norm = jnp.sqrt(jnp.maximum(norm, 1e-30))
        grown = norm * (1.05 + 1.05 * total * step_size(hh))
        summed = grown * jnp.max(grown, axis=1, keepdims=True)
        for i, (value, top) in enumerate(((norm, 512.0), (grown, 512.0), (summed, 32768.0))):
            scales[2 * i : 2 * i + 1, :] = top / value
            scales[2 * i + 1 : 2 * i + 2, :] = value / top


def step_size(hh):
    square = jnp.sum(jnp.sum(hh * hh, axis=0, keepdims=True), axis=1, keepdims=True)
    return 0.5 / jnp.sqrt(square + 1e-06)


def gram_kernel(hb, part_ref, gram_ref):
    gram_ref[...] = lax.dot_general(
        hb[...], hb[...], (((0,), (0,)), ((), ())), preferred_element_type=F32
    )
    part = part_ref.shape[0]
    at = pl.multiple_of(lax.axis_index(COL) * part, part)
    part_ref[...] = gram_ref[pl.ds(at, part), :]


def start_kernel(unit, points, factor, first, second, copies, wide, done):
    half, width = first.shape[0], points.shape[1]
    fetches = [
        pltpu.make_async_copy(points, copies.at[0], done.at[0]),
        pltpu.make_async_copy(factor, wide, done.at[1]),
    ]
    for fetch in fetches:
        fetch.start()
    for fetch in fetches:
        fetch.wait()
    value = copies[0]
    hb = (wide[...] * unit).astype(BF16)
    first[:, :width] = value[:half]
    first[:, width:] = hb[:half]
    second[:, :width] = value[half:]
    second[:, width:] = hb[half:]
    for i in range(1, copies.shape[0]):
        copies[i] = value


def step_kernel(before, after, ah_ref, hh_ref, h_ref, out, *copies):
    hh = hh_ref[...]
    h = h_ref[...] * before if before else h_ref[...]
    scale = step_size(hh)
    product = jnp.dot(h, hh, precision=lax.Precision.HIGHEST, preferred_element_type=F32)
    h = jnp.maximum(h - scale * (product - ah_ref[...]), 0.0)
    out[...] = h / after if after else h
    if copies:
        hb = h.astype(BF16)
        for i in range(copies[0].shape[0]):
            copies[0][i] = hb


def shards(points, factor):
    nz, ncore, ny, nx = (lax.axis_size(a) for a in ROW_COL)
    nrow, ncol = nz * ncore, ny * nx
    pts, rank = factor.shape
    total = pts * nrow * ncol
    unit = 2.0 / math.sqrt(total * rank)
    width = points.shape[1]
    half = pts // 2
    shape = jax.ShapeDtypeStruct

    first, second, copies = call(
        functools.partial(start_kernel, unit),
        [*[shape((half, width + rank), BF16)] * 2, shape((nz, pts, width), BF16)],
        [points, factor],
        1,
        [pltpu.VMEM((pts, rank), F32), pltpu.SemaphoreType.DMA((2,))],
        vmem=60,
        place=pl.ANY,
    )
    tie = lax.optimization_barrier
    along_z = lax.all_to_all(copies, Z, 0, 0, tiled=True)
    x1, x3 = from_ahead(first, X, 1), from_ahead(first, X, -1)
    y1, y3 = from_ahead(second, Y, 1), from_ahead(second, Y, -1)
    x2, y2 = from_ahead(first, X, 2), from_ahead(second, Y, 2)
    x1, x2, x3, y1, y2, y3 = tie((x1, x2, x3, y1, y2, y3))
    by_x = jnp.stack([first, x1, x2, x3])
    by_y = jnp.stack([second, y1, y2, y3])
    by_x, by_y = tie((by_x, by_y))
    y_three, x_three = from_ahead(by_x, Y, 3), from_ahead(by_y, X, 3)
    y_one, x_one = from_ahead(by_x, Y, 1), from_ahead(by_y, X, 1)
    y_two, x_two = from_ahead(by_x, Y, 2), from_ahead(by_y, X, 2)
    far = [x_three, y_three, x_one, y_one, x_two, y_two]
    far, along_z = tie((far, along_z.reshape(-1, width)))
    other = from_ahead(along_z, CORE, 1)
    cols = [*far, first, x1, x2, x3, second, y1, y2, y3]

    part = rank // ncol
    group = nrow * pts
    col_pts, hb_cols, col_sq, own_part = call(
        columns_kernel,
        [
            shape((group, width), BF16),
            shape((group, rank), BF16),
            shape((group // LANES, LANES), F32),
            shape((part, rank), F32),
        ],
        cols,
        2 * group * rank * rank,
        [pltpu.VMEM((rank, rank), F32)],
    )
    more_part = from_ahead(own_part, CORE, 1)
    lines = group // LANES
    own_kern, own_sums = call(
        rows_kernel,
        [shape((group // 2, group), F32), shape((lines // 2, LANES), F32)],
        [along_z, col_pts, col_sq],
        group * group * width,
    )
    other_kern, message = call(
        last_rows_kernel,
        [shape((group // 2, group), F32), shape((nrow, lines + part, LANES), F32)],
        [other, col_pts, col_sq, own_sums, own_part, more_part],
        group * group * width,
        [pltpu.VMEM((lines // 2, LANES), F32)],
    )
    mean_rows, message = call(
        means_kernel,
        [shape((lines, LANES), F32), shape((ncol, 8 + 2 * part, LANES), F32)],
        [lax.all_to_all(message, ROW, 0, 0, tiled=True)],
        1,
    )
    gathered = lax.all_to_all(message, COL, 0, 0, tiled=True)

    def centred(own):
        outs = [shape((group // 2, group), BF16), shape((group // 2, rank), F32)]
        if own:
            outs += [shape((rank, rank), F32), shape((8, rank), F32)]
        return call(
            functools.partial(centred_kernel, own),
            outs,
            [own_kern if own else other_kern, mean_rows, gathered, hb_cols],
            group * group * rank,
        )

    aff_other, partial_other = centred(False)
    got = from_ahead(partial_other, CORE, 1)
    aff_own, partial_own, hh, scales = centred(True)

    def over_z(mine):
        mine = lax.all_to_all(mine.astype(jnp.float16), Z, 0, 0, tiled=True)
        return jnp.sum(mine.astype(F32), axis=0)

    def stepped(before, after, ah, hh, h, copies):
        outs = [shape((pts, rank), F32)] + [shape((ncol, pts, rank), BF16)] * copies
        flops = 12 * pts * rank * rank
        return call(functools.partial(step_kernel, before, after), outs, [ah, hh, h], flops)

    mine = (partial_own + got) * scales[0]
    ah = over_z(mine.reshape(nz, pts, rank)) * scales[1]
    h, hb_cols = stepped(unit, None, ah, hh, factor, 1)

    hb_cols = lax.all_to_all(hb_cols, COL, 0, 0, tiled=True).reshape(group, rank)
    partial_other = jnp.dot(aff_other, hb_cols, preferred_element_type=F32)
    got = from_ahead(partial_other, CORE, 1)
    (own_part,) = call(
        gram_kernel,
        [shape((part, rank), F32)],
        [hb_cols],
        2 * group * rank * rank,
        [pltpu.VMEM((rank, rank), F32)],
    )
    more_part = from_ahead(own_part, CORE, 1)
    partial_own = jnp.dot(aff_own, hb_cols, preferred_element_type=F32)
    mine = ((partial_own + got) * scales[2]).reshape(nz, pts, rank)
    extra = jnp.broadcast_to((own_part + more_part) * scales[4], (nz, part, rank))
    own = over_z(jnp.concatenate([mine, extra], axis=1))
    ah, own_part = tie((own[:pts] * scales[3], own[pts:] * scales[5]))
    hh = sent_to_all(own_part, COL).reshape(rank, rank)
    return stepped(None, unit, ah, hh, h, 0)[0]


def solution(mesh):
    split = Mesh(mesh.devices.reshape(8, 2, 4, 4), ROW_COL)
    return jax.shard_map(
        shards,
        mesh=split,
        in_specs=(P(ROW_COL, None), P(ROW_COL, None)),
        out_specs=P(ROW_COL, None),
        check_vma=False,
    )
```

```python
import functools
import math

import jax
import jax.numpy as jnp
from jax import lax
from jax.experimental import pallas as pl
from jax.experimental.pallas import tpu as pltpu
from jax.sharding import Mesh
from jax.sharding import PartitionSpec as P

EMBED_WIDTH = 1024
Z, CORE, Y, X = "row_0", "row_1", "col_0", "col_1"
ROW = (Z, CORE)
COL = (Y, X)
ROW_COL = (Z, CORE, Y, X)


def from_ahead(value, axis, steps):
    length = lax.axis_size(axis)
    return lax.ppermute(value, axis, [((i + steps) % length, i) for i in range(length)])


def sent_to_all(value, axes):
    length = math.prod(lax.axis_size(a) for a in axes)
    copies = jnp.broadcast_to(value, (length, *value.shape))
    return lax.all_to_all(copies, axes, split_axis=0, concat_axis=0, tiled=True)


F32, BF16 = jnp.float32, jnp.bfloat16
VMEM = pl.BlockSpec(memory_space=pltpu.VMEM)
LANES = 128


def call(kernel, outs, args, flops, scratch=(), vmem=10, place=pltpu.VMEM):
    size = sum(math.prod(a.shape) * a.dtype.itemsize for a in (*outs, *args))
    return pl.pallas_call(
        kernel,
        out_shape=outs,
        in_specs=[pl.BlockSpec(memory_space=place)] * len(args),
        out_specs=[VMEM] * len(outs),
        scratch_shapes=list(scratch),
        compiler_params=pltpu.CompilerParams(vmem_limit_bytes=vmem << 20),
        cost_estimate=pl.CostEstimate(flops=flops, bytes_accessed=size, transcendentals=0),
    )(*args)


def rows_dot(a, b):
    return lax.dot_general(a, b, (((1,), (1,)), ((), ())), preferred_element_type=F32)


def squares(rows):
    wide = rows.astype(F32)
    groups = [wide[:, g : g + LANES] for g in range(0, rows.shape[1], LANES)]
    return sum(g * g for g in groups)


def columns_kernel(
    x3, y3, x1, y1, x2, y2, ax0, ax1, ax2, ax3, by0, by1, by2, by3, pts_ref, hb_ref, sq_ref, part_ref, gram_ref
):
    ny, nx = lax.axis_size(Y), lax.axis_size(X)
    y, x = lax.axis_index(Y), lax.axis_index(X)
    half = ax0.shape[0]
    width = pts_ref.shape[1]

    def put(far, near, lower, value):
        at = (lax.rem(y + far, ny) * nx + lax.rem(x + near, nx)) * 2 * half + lower
        at = pl.ds(pl.multiple_of(at, half), half)
        pts_ref[at, :] = value[:, :width]
        hb_ref[at, :] = value[:, width:]

    for near, ref in enumerate((ax0, ax1, ax2, ax3)):
        put(0, near, 0, ref[...])
    for far, ref in enumerate((by0, by1, by2, by3)):
        put(far, 0, half, ref[...])
    for far, ref in enumerate((y1, y2, y3)):
        for near in range(nx):
            put(far + 1, near, 0, ref[near])
    for near, ref in enumerate((x1, x2, x3)):
        for far in range(ny):
            put(far, near + 1, half, ref[far])
    for block in range(pts_ref.shape[0] // LANES):
        sums = squares(pts_ref[block * LANES : (block + 1) * LANES, :])
        sq_ref[block : block + 1, :] = jnp.sum(sums.T, axis=0, keepdims=True)
    gram_ref[...] = lax.dot_general(
        hb_ref[...], hb_ref[...], (((0,), (0,)), ((), ())), preferred_element_type=F32
    )
    part = part_ref.shape[0]
    at = pl.multiple_of((y * nx + x) * part, part)
    part_ref[...] = gram_ref[pl.ds(at, part), :]


def rows_kernel(rows_ref, cols, sq, kern, sums):
    col_sq = jnp.concatenate([sq[g : g + 1, :] for g in range(sq.shape[0])], axis=1)
    tall = 2 * LANES

    def block(i, _):
        at = pl.ds(pl.multiple_of(i * tall, tall), tall)
        rows = rows_ref[at, :]
        row_sq = jnp.sum(squares(rows), axis=1, keepdims=True)
        gram = rows_dot(rows, cols[...])
        values = jnp.exp((2.0 * gram - row_sq - col_sq) * (0.5 / EMBED_WIDTH))
        kern[at, :] = values
        total = sum(values[:, g : g + LANES] for g in range(0, values.shape[1], LANES))
        for j in range(2):
            line = jnp.sum(total[j * LANES : (j + 1) * LANES].T, axis=0, keepdims=True)
            sums[pl.ds(i * 2 + j, 1), :] = line
        return 0

    lax.fori_loop(0, rows_ref.shape[0] // tall, block, 0, unroll=True)


def last_rows_kernel(rows_ref, cols, sq, own_sums, part, more, kern, out, sums):
    rows_kernel(rows_ref, cols, sq, kern, sums)
    core = lax.axis_index(CORE)
    mine = own_sums[...]
    theirs = sums[...]
    lines = 2 * mine.shape[0]
    deep = part.shape[0] // 2
    at = pl.ds(pl.multiple_of(core * deep, deep), deep)
    gram = part[at, :] + more[at, :]
    swap = core == 1
    both = jnp.concatenate(
        [jnp.where(swap, theirs, mine), jnp.where(swap, mine, theirs)], axis=0
    )
    for i in range(out.shape[0]):
        out[i, :lines] = both
        out[i, lines : lines + deep] = gram[:, :LANES]
        out[i, lines + deep :] = gram[:, LANES:]


def means_kernel(got, mean_ref, out):
    z, core = lax.axis_index(Z), lax.axis_index(CORE)
    n = got.shape[0]
    lines = mean_ref.shape[0]
    total = lines * LANES * n
    even, odd = got[0], got[1]
    for i in range(2, n, 2):
        even, odd = even + got[i], odd + got[i + 1]
    sums = even + odd
    means = sums[:lines] / total
    mean_ref[...] = means
    own = mean_ref[pl.ds((core * lax.axis_size(Z) + z) // 2, 1), :]
    band = jnp.broadcast_to(jnp.sum(means, keepdims=True), (1, LANES))
    fill = jnp.zeros((lines - 2, LANES), F32)
    deep = (got.shape[1] - lines) // 2
    pieces = [own, band, fill]
    for at in (lines, lines + deep):
        pieces += [even[at : at + deep], odd[at : at + deep]]
    whole = jnp.concatenate(pieces, axis=0)
    for i in range(out.shape[0]):
        out[i] = whole


def centred_kernel(own, kern, mean_ref, got, hb, aff, partial, *more):
    z, core = lax.axis_index(Z), lax.axis_index(CORE)
    n = got.shape[0]
    total = mean_ref.shape[0] * LANES * n
    which = core if own else 1 - core
    grand = got[0, 1:2, :]
    for i in range(1, n):
        grand = grand + got[i, 1:2, :]
    grand = grand / total
    lane = lax.broadcasted_iota(jnp.int32, (1, LANES), 1)
    odd = lax.rem(z, 2) == 1
    places = []
    for i in range(0, n, 2):
        pair = []
        for j in range(2):
            line = got[i + j, 0:1, :]
            swapped = pltpu.roll(line, LANES // 2, 1)
            pair.append(jnp.where(odd if j == 0 else jnp.logical_not(odd), swapped, line))
        places.append(jnp.where(lane < LANES // 2, pair[0], pair[1]))
    lines = mean_ref.shape[0] // 2
    for i in range(lines):
        line = mean_ref[pl.ds(which * lines + i, 1), :]
        mine = jnp.broadcast_to(line, (LANES, LANES)).T
        at = slice(i * LANES, (i + 1) * LANES)
        for g, place in enumerate(places):
            values = kern[at, g * LANES : (g + 1) * LANES]
            values = values - mine - place + grand
            aff[at, g * LANES : (g + 1) * LANES] = values.astype(BF16)
    partial[...] = jnp.dot(aff[...], hb[...], preferred_element_type=F32)
    if more:
        hh_ref, scales = more
        deep = (got.shape[1] - 8) // 2
        for i in range(n):
            hh_ref[i * deep : (i + 1) * deep, :LANES] = got[i, 8 : 8 + deep, :]
            hh_ref[i * deep : (i + 1) * deep, LANES:] = got[i, 8 + deep :, :]
        hh = hh_ref[...]
        line = lax.broadcasted_iota(jnp.int32, hh.shape, 0)
        place = lax.broadcasted_iota(jnp.int32, hh.shape, 1)
        norm = jnp.sum(jnp.where(line == place, hh, 0.0), axis=0, keepdims=True)
        norm = jnp.sqrt(jnp.maximum(norm, 1e-30))
        grown = norm * (1.05 + 1.05 * total * step_size(hh))
        summed = grown * jnp.max(grown, axis=1, keepdims=True)
        for i, (value, top) in enumerate(((norm, 512.0), (grown, 512.0), (summed, 32768.0))):
            scales[2 * i : 2 * i + 1, :] = top / value
            scales[2 * i + 1 : 2 * i + 2, :] = value / top


def step_size(hh):
    square = jnp.sum(jnp.sum(hh * hh, axis=0, keepdims=True), axis=1, keepdims=True)
    return 0.5 / jnp.sqrt(square + 1e-06)


def gram_kernel(hb, part_ref, gram_ref):
    gram_ref[...] = lax.dot_general(
        hb[...], hb[...], (((0,), (0,)), ((), ())), preferred_element_type=F32
    )
    part = part_ref.shape[0]
    at = pl.multiple_of(lax.axis_index(COL) * part, part)
    part_ref[...] = gram_ref[pl.ds(at, part), :]


def start_kernel(unit, points, factor, first, second, copies, wide, done):
    half, width = first.shape[0], points.shape[1]
    fetches = [
        pltpu.make_async_copy(points, copies.at[0], done.at[0]),
        pltpu.make_async_copy(factor, wide, done.at[1]),
    ]
    for fetch in fetches:
        fetch.start()
    for fetch in fetches:
        fetch.wait()
    value = copies[0]
    hb = (wide[...] * unit).astype(BF16)
    first[:, :width] = value[:half]
    first[:, width:] = hb[:half]
    second[:, :width] = value[half:]
    second[:, width:] = hb[half:]
    for i in range(1, copies.shape[0]):
        copies[i] = value


def step_kernel(before, after, ah_ref, hh_ref, h_ref, out, *copies):
    hh = hh_ref[...]
    h = h_ref[...] * before if before else h_ref[...]
    scale = step_size(hh)
    product = jnp.dot(h, hh, precision=lax.Precision.HIGHEST, preferred_element_type=F32)
    h = jnp.maximum(h - scale * (product - ah_ref[...]), 0.0)
    out[...] = h / after if after else h
    if copies:
        hb = h.astype(BF16)
        for i in range(copies[0].shape[0]):
            copies[0][i] = hb


def shards(points, factor):
    nz, ncore, ny, nx = (lax.axis_size(a) for a in ROW_COL)
    nrow, ncol = nz * ncore, ny * nx
    pts, rank = factor.shape
    total = pts * nrow * ncol
    unit = 2.0 / math.sqrt(total * rank)
    width = points.shape[1]
    half = pts // 2
    shape = jax.ShapeDtypeStruct

    first, second, copies = call(
        functools.partial(start_kernel, unit),
        [*[shape((half, width + rank), BF16)] * 2, shape((nz, pts, width), BF16)],
        [points, factor],
        1,
        [pltpu.VMEM((pts, rank), F32), pltpu.SemaphoreType.DMA((2,))],
        vmem=60,
        place=pl.ANY,
    )
    tie = lax.optimization_barrier
    along_z = lax.all_to_all(copies, Z, 0, 0, tiled=True)
    x1, x3 = from_ahead(first, X, 1), from_ahead(first, X, -1)
    y1, y3 = from_ahead(second, Y, 1), from_ahead(second, Y, -1)
    x2, y2 = from_ahead(first, X, 2), from_ahead(second, Y, 2)
    x1, x2, x3, y1, y2, y3 = tie((x1, x2, x3, y1, y2, y3))
    by_x = jnp.stack([first, x1, x2, x3])
    by_y = jnp.stack([second, y1, y2, y3])
    by_x, by_y = tie((by_x, by_y))
    y_one, x_one = from_ahead(by_x, Y, 1), from_ahead(by_y, X, 1)
    y_two, x_two = from_ahead(by_x, Y, 2), from_ahead(by_y, X, 2)
    by_x, by_y, x_two = tie((by_x, by_y, x_two))
    y_three, x_three = from_ahead(by_x, Y, 3), from_ahead(by_y, X, 3)
    far = [x_three, y_three, x_one, y_one, x_two, y_two]
    far, along_z = tie((far, along_z.reshape(-1, width)))
    other = from_ahead(along_z, CORE, 1)
    cols = [*far, first, x1, x2, x3, second, y1, y2, y3]

    part = rank // ncol
    group = nrow * pts
    col_pts, hb_cols, col_sq, own_part = call(
        columns_kernel,
        [
            shape((group, width), BF16),
            shape((group, rank), BF16),
            shape((group // LANES, LANES), F32),
            shape((part, rank), F32),
        ],
        cols,
        2 * group * rank * rank,
        [pltpu.VMEM((rank, rank), F32)],
    )
    more_part = from_ahead(own_part, CORE, 1)
    lines = group // LANES
    own_kern, own_sums = call(
        rows_kernel,
        [shape((group // 2, group), F32), shape((lines // 2, LANES), F32)],
        [along_z, col_pts, col_sq],
        group * group * width,
    )
    other_kern, message = call(
        last_rows_kernel,
        [shape((group // 2, group), F32), shape((nrow, lines + part, LANES), F32)],
        [other, col_pts, col_sq, own_sums, own_part, more_part],
        group * group * width,
        [pltpu.VMEM((lines // 2, LANES), F32)],
    )
    mean_rows, message = call(
        means_kernel,
        [shape((lines, LANES), F32), shape((ncol, 8 + 2 * part, LANES), F32)],
        [lax.all_to_all(message, ROW, 0, 0, tiled=True)],
        1,
    )
    gathered = lax.all_to_all(message, COL, 0, 0, tiled=True)

    def centred(own):
        outs = [shape((group // 2, group), BF16), shape((group // 2, rank), F32)]
        if own:
            outs += [shape((rank, rank), F32), shape((8, rank), F32)]
        return call(
            functools.partial(centred_kernel, own),
            outs,
            [own_kern if own else other_kern, mean_rows, gathered, hb_cols],
            group * group * rank,
        )

    aff_other, partial_other = centred(False)
    got = from_ahead(partial_other, CORE, 1)
    aff_own, partial_own, hh, scales = centred(True)

    def over_z(mine):
        mine = lax.all_to_all(mine.astype(jnp.float16), Z, 0, 0, tiled=True)
        return jnp.sum(mine.astype(F32), axis=0)

    def stepped(before, after, ah, hh, h, copies):
        outs = [shape((pts, rank), F32)] + [shape((ncol, pts, rank), BF16)] * copies
        flops = 12 * pts * rank * rank
        return call(functools.partial(step_kernel, before, after), outs, [ah, hh, h], flops)

    mine = (partial_own + got) * scales[0]
    ah = over_z(mine.reshape(nz, pts, rank)) * scales[1]
    h, hb_cols = stepped(unit, None, ah, hh, factor, 1)

    hb_cols = lax.all_to_all(hb_cols, COL, 0, 0, tiled=True).reshape(group, rank)
    partial_other = jnp.dot(aff_other, hb_cols, preferred_element_type=F32)
    got = from_ahead(partial_other, CORE, 1)
    (own_part,) = call(
        gram_kernel,
        [shape((part, rank), F32)],
        [hb_cols],
        2 * group * rank * rank,
        [pltpu.VMEM((rank, rank), F32)],
    )
    more_part = from_ahead(own_part, CORE, 1)
    partial_own = jnp.dot(aff_own, hb_cols, preferred_element_type=F32)
    mine = ((partial_own + got) * scales[2]).reshape(nz, pts, rank)
    extra = jnp.broadcast_to((own_part + more_part) * scales[4], (nz, part, rank))
    own = over_z(jnp.concatenate([mine, extra], axis=1))
    ah, own_part = tie((own[:pts] * scales[3], own[pts:] * scales[5]))
    hh = sent_to_all(own_part, COL).reshape(rank, rank)
    return stepped(None, unit, ah, hh, h, 0)[0]


def solution(mesh):
    split = Mesh(mesh.devices.reshape(8, 2, 4, 4), ROW_COL)
    return jax.shard_map(
        shards,
        mesh=split,
        in_specs=(P(ROW_COL, None), P(ROW_COL, None)),
        out_specs=P(ROW_COL, None),
        check_vma=False,
    )
```

```python
import functools
import math

import jax
import jax.numpy as jnp
from jax import lax
from jax.experimental import pallas as pl
from jax.experimental.pallas import tpu as pltpu
from jax.sharding import Mesh
from jax.sharding import PartitionSpec as P

EMBED_WIDTH = 1024
Z, CORE, Y, X = "row_0", "row_1", "col_0", "col_1"
ROW = (Z, CORE)
COL = (Y, X)
ROW_COL = (Z, CORE, Y, X)


def from_ahead(value, axis, steps):
    length = lax.axis_size(axis)
    return lax.ppermute(value, axis, [((i + steps) % length, i) for i in range(length)])


def sent_to_all(value, axes):
    length = math.prod(lax.axis_size(a) for a in axes)
    copies = jnp.broadcast_to(value, (length, *value.shape))
    return lax.all_to_all(copies, axes, split_axis=0, concat_axis=0, tiled=True)


F32, BF16 = jnp.float32, jnp.bfloat16
VMEM = pl.BlockSpec(memory_space=pltpu.VMEM)
LANES = 128


def call(kernel, outs, args, flops, scratch=(), vmem=10, place=pltpu.VMEM):
    size = sum(math.prod(a.shape) * a.dtype.itemsize for a in (*outs, *args))
    return pl.pallas_call(
        kernel,
        out_shape=outs,
        in_specs=[pl.BlockSpec(memory_space=place)] * len(args),
        out_specs=[VMEM] * len(outs),
        scratch_shapes=list(scratch),
        compiler_params=pltpu.CompilerParams(vmem_limit_bytes=vmem << 20),
        cost_estimate=pl.CostEstimate(flops=flops, bytes_accessed=size, transcendentals=0),
    )(*args)


def rows_dot(a, b):
    return lax.dot_general(a, b, (((1,), (1,)), ((), ())), preferred_element_type=F32)


def squares(rows):
    wide = rows.astype(F32)
    groups = [wide[:, g : g + LANES] for g in range(0, rows.shape[1], LANES)]
    return sum(g * g for g in groups)


def columns_kernel(
    x3, y3, x1, y1, x2, y2, ax0, ax1, ax2, ax3, by0, by1, by2, by3, pts_ref, hb_ref, sq_ref, part_ref, gram_ref
):
    ny, nx = lax.axis_size(Y), lax.axis_size(X)
    y, x = lax.axis_index(Y), lax.axis_index(X)
    half = ax0.shape[0]
    width = pts_ref.shape[1]

    def put(far, near, lower, value):
        at = (lax.rem(y + far, ny) * nx + lax.rem(x + near, nx)) * 2 * half + lower
        at = pl.ds(pl.multiple_of(at, half), half)
        pts_ref[at, :] = value[:, :width]
        hb_ref[at, :] = value[:, width:]

    for near, ref in enumerate((ax0, ax1, ax2, ax3)):
        put(0, near, 0, ref[...])
    for far, ref in enumerate((by0, by1, by2, by3)):
        put(far, 0, half, ref[...])
    for far, ref in enumerate((y1, y2, y3)):
        for near in range(nx):
            put(far + 1, near, 0, ref[near])
    for near, ref in enumerate((x1, x2, x3)):
        for far in range(ny):
            put(far, near + 1, half, ref[far])
    for block in range(pts_ref.shape[0] // LANES):
        sums = squares(pts_ref[block * LANES : (block + 1) * LANES, :])
        sq_ref[block : block + 1, :] = jnp.sum(sums.T, axis=0, keepdims=True)
    gram_ref[...] = lax.dot_general(
        hb_ref[...], hb_ref[...], (((0,), (0,)), ((), ())), preferred_element_type=F32
    )
    part = part_ref.shape[0]
    at = pl.multiple_of((y * nx + x) * part, part)
    part_ref[...] = gram_ref[pl.ds(at, part), :]


def rows_kernel(rows_ref, cols, sq, kern, sums):
    col_sq = jnp.concatenate([sq[g : g + 1, :] for g in range(sq.shape[0])], axis=1)
    tall = 2 * LANES

    def block(i, _):
        at = pl.ds(pl.multiple_of(i * tall, tall), tall)
        rows = rows_ref[at, :]
        row_sq = jnp.sum(squares(rows), axis=1, keepdims=True)
        gram = rows_dot(rows, cols[...])
        values = jnp.exp((2.0 * gram - row_sq - col_sq) * (0.5 / EMBED_WIDTH))
        kern[at, :] = values
        total = sum(values[:, g : g + LANES] for g in range(0, values.shape[1], LANES))
        for j in range(2):
            line = jnp.sum(total[j * LANES : (j + 1) * LANES].T, axis=0, keepdims=True)
            sums[pl.ds(i * 2 + j, 1), :] = line
        return 0

    lax.fori_loop(0, rows_ref.shape[0] // tall, block, 0, unroll=True)


def last_rows_kernel(rows_ref, cols, sq, own_sums, part, more, kern, out, sums):
    rows_kernel(rows_ref, cols, sq, kern, sums)
    core = lax.axis_index(CORE)
    mine = own_sums[...]
    theirs = sums[...]
    lines = 2 * mine.shape[0]
    deep = part.shape[0] // 2
    at = pl.ds(pl.multiple_of(core * deep, deep), deep)
    gram = part[at, :] + more[at, :]
    swap = core == 1
    both = jnp.concatenate(
        [jnp.where(swap, theirs, mine), jnp.where(swap, mine, theirs)], axis=0
    )
    for i in range(out.shape[0]):
        out[i, :lines] = both
        out[i, lines : lines + deep] = gram[:, :LANES]
        out[i, lines + deep :] = gram[:, LANES:]


def means_kernel(got, mean_ref, out):
    z, core = lax.axis_index(Z), lax.axis_index(CORE)
    n = got.shape[0]
    lines = mean_ref.shape[0]
    total = lines * LANES * n
    even, odd = got[0], got[1]
    for i in range(2, n, 2):
        even, odd = even + got[i], odd + got[i + 1]
    sums = even + odd
    means = sums[:lines] / total
    mean_ref[...] = means
    own = mean_ref[pl.ds((core * lax.axis_size(Z) + z) // 2, 1), :]
    band = jnp.broadcast_to(jnp.sum(means, keepdims=True), (1, LANES))
    fill = jnp.zeros((lines - 2, LANES), F32)
    deep = (got.shape[1] - lines) // 2
    pieces = [own, band, fill]
    for at in (lines, lines + deep):
        pieces += [even[at : at + deep], odd[at : at + deep]]
    whole = jnp.concatenate(pieces, axis=0)
    for i in range(out.shape[0]):
        out[i] = whole


def centred_kernel(own, kern, mean_ref, got, hb, aff, partial, *more):
    z, core = lax.axis_index(Z), lax.axis_index(CORE)
    n = got.shape[0]
    total = mean_ref.shape[0] * LANES * n
    which = core if own else 1 - core
    grand = got[0, 1:2, :]
    for i in range(1, n):
        grand = grand + got[i, 1:2, :]
    grand = grand / total
    lane = lax.broadcasted_iota(jnp.int32, (1, LANES), 1)
    odd = lax.rem(z, 2) == 1
    places = []
    for i in range(0, n, 2):
        pair = []
        for j in range(2):
            line = got[i + j, 0:1, :]
            swapped = pltpu.roll(line, LANES // 2, 1)
            pair.append(jnp.where(odd if j == 0 else jnp.logical_not(odd), swapped, line))
        places.append(jnp.where(lane < LANES // 2, pair[0], pair[1]))
    lines = mean_ref.shape[0] // 2
    for i in range(lines):
        line = mean_ref[pl.ds(which * lines + i, 1), :]
        mine = jnp.broadcast_to(line, (LANES, LANES)).T
        at = slice(i * LANES, (i + 1) * LANES)
        for g, place in enumerate(places):
            values = kern[at, g * LANES : (g + 1) * LANES]
            values = values - mine - place + grand
            aff[at, g * LANES : (g + 1) * LANES] = values.astype(BF16)
    partial[...] = jnp.dot(aff[...], hb[...], preferred_element_type=F32)
    if more:
        hh_ref, scales = more
        deep = (got.shape[1] - 8) // 2
        for i in range(n):
            hh_ref[i * deep : (i + 1) * deep, :LANES] = got[i, 8 : 8 + deep, :]
            hh_ref[i * deep : (i + 1) * deep, LANES:] = got[i, 8 + deep :, :]
        hh = hh_ref[...]
        line = lax.broadcasted_iota(jnp.int32, hh.shape, 0)
        place = lax.broadcasted_iota(jnp.int32, hh.shape, 1)
        norm = jnp.sum(jnp.where(line == place, hh, 0.0), axis=0, keepdims=True)
        norm = jnp.sqrt(jnp.maximum(norm, 1e-30))
        grown = norm * (1.05 + 1.05 * total * step_size(hh))
        summed = grown * jnp.max(grown, axis=1, keepdims=True)
        for i, (value, top) in enumerate(((norm, 512.0), (grown, 512.0), (summed, 32768.0))):
            scales[2 * i : 2 * i + 1, :] = top / value
            scales[2 * i + 1 : 2 * i + 2, :] = value / top


def step_size(hh):
    square = jnp.sum(jnp.sum(hh * hh, axis=0, keepdims=True), axis=1, keepdims=True)
    return 0.5 / jnp.sqrt(square + 1e-06)


def gram_kernel(hb, part_ref, gram_ref):
    gram_ref[...] = lax.dot_general(
        hb[...], hb[...], (((0,), (0,)), ((), ())), preferred_element_type=F32
    )
    part = part_ref.shape[0]
    at = pl.multiple_of(lax.axis_index(COL) * part, part)
    part_ref[...] = gram_ref[pl.ds(at, part), :]


def start_kernel(unit, points, factor, first, second, copies, wide, done):
    half, width = first.shape[0], points.shape[1]
    fetches = [
        pltpu.make_async_copy(points, copies.at[0], done.at[0]),
        pltpu.make_async_copy(factor, wide, done.at[1]),
    ]
    for fetch in fetches:
        fetch.start()
    for fetch in fetches:
        fetch.wait()
    value = copies[0]
    hb = (wide[...] * unit).astype(BF16)
    first[:, :width] = value[:half]
    first[:, width:] = hb[:half]
    second[:, :width] = value[half:]
    second[:, width:] = hb[half:]
    for i in range(1, copies.shape[0]):
        copies[i] = value


def step_kernel(before, after, ah_ref, hh_ref, h_ref, out, *copies):
    hh = hh_ref[...]
    h = h_ref[...] * before if before else h_ref[...]
    scale = step_size(hh)
    product = jnp.dot(h, hh, precision=lax.Precision.HIGHEST, preferred_element_type=F32)
    h = jnp.maximum(h - scale * (product - ah_ref[...]), 0.0)
    out[...] = h / after if after else h
    if copies:
        hb = h.astype(BF16)
        for i in range(copies[0].shape[0]):
            copies[0][i] = hb


def shards(points, factor):
    nz, ncore, ny, nx = (lax.axis_size(a) for a in ROW_COL)
    nrow, ncol = nz * ncore, ny * nx
    pts, rank = factor.shape
    total = pts * nrow * ncol
    unit = 2.0 / math.sqrt(total * rank)
    width = points.shape[1]
    half = pts // 2
    shape = jax.ShapeDtypeStruct

    first, second, copies = call(
        functools.partial(start_kernel, unit),
        [*[shape((half, width + rank), BF16)] * 2, shape((nz, pts, width), BF16)],
        [points, factor],
        1,
        [pltpu.VMEM((pts, rank), F32), pltpu.SemaphoreType.DMA((2,))],
        vmem=60,
        place=pl.ANY,
    )
    tie = lax.optimization_barrier
    along_z = lax.all_to_all(copies, Z, 0, 0, tiled=True)
    y1, x1 = from_ahead(second, Y, 1), from_ahead(first, X, 1)
    y2, x2 = from_ahead(second, Y, 2), from_ahead(first, X, 2)
    ahead, behind, x2 = tie((first, second, x2))
    y3, x3 = from_ahead(behind, Y, -1), from_ahead(ahead, X, -1)
    x1, x2, x3, y1, y2, y3 = tie((x1, x2, x3, y1, y2, y3))
    by_x = jnp.stack([first, x1, x2, x3])
    by_y = jnp.stack([second, y1, y2, y3])
    by_x, by_y = tie((by_x, by_y))
    y_one, x_one = from_ahead(by_x, Y, 1), from_ahead(by_y, X, 1)
    y_two, x_two = from_ahead(by_x, Y, 2), from_ahead(by_y, X, 2)
    by_x, by_y, x_two = tie((by_x, by_y, x_two))
    y_three, x_three = from_ahead(by_x, Y, 3), from_ahead(by_y, X, 3)
    far = [x_three, y_three, x_one, y_one, x_two, y_two]
    far, along_z = tie((far, along_z.reshape(-1, width)))
    other = from_ahead(along_z, CORE, 1)
    cols = [*far, first, x1, x2, x3, second, y1, y2, y3]

    part = rank // ncol
    group = nrow * pts
    col_pts, hb_cols, col_sq, own_part = call(
        columns_kernel,
        [
            shape((group, width), BF16),
            shape((group, rank), BF16),
            shape((group // LANES, LANES), F32),
            shape((part, rank), F32),
        ],
        cols,
        2 * group * rank * rank,
        [pltpu.VMEM((rank, rank), F32)],
    )
    more_part = from_ahead(own_part, CORE, 1)
    lines = group // LANES
    own_kern, own_sums = call(
        rows_kernel,
        [shape((group // 2, group), F32), shape((lines // 2, LANES), F32)],
        [along_z, col_pts, col_sq],
        group * group * width,
    )
    other_kern, message = call(
        last_rows_kernel,
        [shape((group // 2, group), F32), shape((nrow, lines + part, LANES), F32)],
        [other, col_pts, col_sq, own_sums, own_part, more_part],
        group * group * width,
        [pltpu.VMEM((lines // 2, LANES), F32)],
    )
    mean_rows, message = call(
        means_kernel,
        [shape((lines, LANES), F32), shape((ncol, 8 + 2 * part, LANES), F32)],
        [lax.all_to_all(message, ROW, 0, 0, tiled=True)],
        1,
    )
    gathered = lax.all_to_all(message, COL, 0, 0, tiled=True)

    def centred(own):
        outs = [shape((group // 2, group), BF16), shape((group // 2, rank), F32)]
        if own:
            outs += [shape((rank, rank), F32), shape((8, rank), F32)]
        return call(
            functools.partial(centred_kernel, own),
            outs,
            [own_kern if own else other_kern, mean_rows, gathered, hb_cols],
            group * group * rank,
        )

    aff_other, partial_other = centred(False)
    got = from_ahead(partial_other, CORE, 1)
    aff_own, partial_own, hh, scales = centred(True)

    def over_z(mine):
        mine = lax.all_to_all(mine.astype(jnp.float16), Z, 0, 0, tiled=True)
        return jnp.sum(mine.astype(F32), axis=0)

    def stepped(before, after, ah, hh, h, copies):
        outs = [shape((pts, rank), F32)] + [shape((ncol, pts, rank), BF16)] * copies
        flops = 12 * pts * rank * rank
        return call(functools.partial(step_kernel, before, after), outs, [ah, hh, h], flops)

    mine = (partial_own + got) * scales[0]
    ah = over_z(mine.reshape(nz, pts, rank)) * scales[1]
    h, hb_cols = stepped(unit, None, ah, hh, factor, 1)

    hb_cols = lax.all_to_all(hb_cols, COL, 0, 0, tiled=True).reshape(group, rank)
    partial_other = jnp.dot(aff_other, hb_cols, preferred_element_type=F32)
    got = from_ahead(partial_other, CORE, 1)
    (own_part,) = call(
        gram_kernel,
        [shape((part, rank), F32)],
        [hb_cols],
        2 * group * rank * rank,
        [pltpu.VMEM((rank, rank), F32)],
    )
    more_part = from_ahead(own_part, CORE, 1)
    partial_own = jnp.dot(aff_own, hb_cols, preferred_element_type=F32)
    mine = ((partial_own + got) * scales[2]).reshape(nz, pts, rank)
    extra = jnp.broadcast_to((own_part + more_part) * scales[4], (nz, part, rank))
    own = over_z(jnp.concatenate([mine, extra], axis=1))
    ah, own_part = tie((own[:pts] * scales[3], own[pts:] * scales[5]))
    hh = sent_to_all(own_part, COL).reshape(rank, rank)
    return stepped(None, unit, ah, hh, h, 0)[0]


def solution(mesh):
    split = Mesh(mesh.devices.reshape(8, 2, 4, 4), ROW_COL)
    return jax.shard_map(
        shards,
        mesh=split,
        in_specs=(P(ROW_COL, None), P(ROW_COL, None)),
        out_specs=P(ROW_COL, None),
        check_vma=False,
    )
```

```python
import functools
import math

import jax
import jax.numpy as jnp
from jax import lax
from jax.experimental import pallas as pl
from jax.experimental.pallas import tpu as pltpu
from jax.sharding import Mesh
from jax.sharding import PartitionSpec as P

EMBED_WIDTH = 1024
Z, CORE, Y, X = "row_0", "row_1", "col_0", "col_1"
ROW = (Z, CORE)
COL = (Y, X)
ROW_COL = (Z, CORE, Y, X)


def from_ahead(value, axis, steps):
    length = lax.axis_size(axis)
    return lax.ppermute(value, axis, [((i + steps) % length, i) for i in range(length)])


def sent_to_all(value, axes):
    length = math.prod(lax.axis_size(a) for a in axes)
    copies = jnp.broadcast_to(value, (length, *value.shape))
    return lax.all_to_all(copies, axes, split_axis=0, concat_axis=0, tiled=True)


F32, BF16 = jnp.float32, jnp.bfloat16
VMEM = pl.BlockSpec(memory_space=pltpu.VMEM)
LANES = 128


def call(kernel, outs, args, flops, scratch=(), vmem=10, place=pltpu.VMEM):
    size = sum(math.prod(a.shape) * a.dtype.itemsize for a in (*outs, *args))
    return pl.pallas_call(
        kernel,
        out_shape=outs,
        in_specs=[pl.BlockSpec(memory_space=place)] * len(args),
        out_specs=[VMEM] * len(outs),
        scratch_shapes=list(scratch),
        compiler_params=pltpu.CompilerParams(vmem_limit_bytes=vmem << 20),
        cost_estimate=pl.CostEstimate(flops=flops, bytes_accessed=size, transcendentals=0),
    )(*args)


def rows_dot(a, b):
    return lax.dot_general(a, b, (((1,), (1,)), ((), ())), preferred_element_type=F32)


def squares(rows):
    wide = rows.astype(F32)
    groups = [wide[:, g : g + LANES] for g in range(0, rows.shape[1], LANES)]
    return sum(g * g for g in groups)


def columns_kernel(
    x3, y3, x1, y1, x2, y2, ax0, ax1, ax2, ax3, by0, by1, by2, by3, pts_ref, hb_ref, sq_ref, part_ref, gram_ref
):
    ny, nx = lax.axis_size(Y), lax.axis_size(X)
    y, x = lax.axis_index(Y), lax.axis_index(X)
    half = ax0.shape[0]
    width = pts_ref.shape[1]

    def put(far, near, lower, value):
        at = (lax.rem(y + far, ny) * nx + lax.rem(x + near, nx)) * 2 * half + lower
        at = pl.ds(pl.multiple_of(at, half), half)
        pts_ref[at, :] = value[:, :width]
        hb_ref[at, :] = value[:, width:]

    for near, ref in enumerate((ax0, ax1, ax2, ax3)):
        put(0, near, 0, ref[...])
    for far, ref in enumerate((by0, by1, by2, by3)):
        put(far, 0, half, ref[...])
    for far, ref in enumerate((y1, y2, y3)):
        for near in range(nx):
            put(far + 1, near, 0, ref[near])
    for near, ref in enumerate((x1, x2, x3)):
        for far in range(ny):
            put(far, near + 1, half, ref[far])
    for block in range(pts_ref.shape[0] // LANES):
        sums = squares(pts_ref[block * LANES : (block + 1) * LANES, :])
        sq_ref[block : block + 1, :] = jnp.sum(sums.T, axis=0, keepdims=True)
    gram_ref[...] = lax.dot_general(
        hb_ref[...], hb_ref[...], (((0,), (0,)), ((), ())), preferred_element_type=F32
    )
    part = part_ref.shape[0]
    at = pl.multiple_of((y * nx + x) * part, part)
    part_ref[...] = gram_ref[pl.ds(at, part), :]


def rows_kernel(rows_ref, cols, sq, kern, sums):
    col_sq = jnp.concatenate([sq[g : g + 1, :] for g in range(sq.shape[0])], axis=1)
    tall = 2 * LANES

    def block(i, _):
        at = pl.ds(pl.multiple_of(i * tall, tall), tall)
        rows = rows_ref[at, :]
        row_sq = jnp.sum(squares(rows), axis=1, keepdims=True)
        gram = rows_dot(rows, cols[...])
        values = jnp.exp((2.0 * gram - row_sq - col_sq) * (0.5 / EMBED_WIDTH))
        kern[at, :] = values
        total = sum(values[:, g : g + LANES] for g in range(0, values.shape[1], LANES))
        for j in range(2):
            line = jnp.sum(total[j * LANES : (j + 1) * LANES].T, axis=0, keepdims=True)
            sums[pl.ds(i * 2 + j, 1), :] = line
        return 0

    lax.fori_loop(0, rows_ref.shape[0] // tall, block, 0, unroll=True)


def last_rows_kernel(rows_ref, cols, sq, own_sums, part, more, kern, out, sums):
    rows_kernel(rows_ref, cols, sq, kern, sums)
    core = lax.axis_index(CORE)
    mine = own_sums[...]
    theirs = sums[...]
    lines = 2 * mine.shape[0]
    deep = part.shape[0] // 2
    at = pl.ds(pl.multiple_of(core * deep, deep), deep)
    gram = part[at, :] + more[at, :]
    swap = core == 1
    both = jnp.concatenate(
        [jnp.where(swap, theirs, mine), jnp.where(swap, mine, theirs)], axis=0
    )
    for i in range(out.shape[0]):
        out[i, :lines] = both
        out[i, lines : lines + deep] = gram[:, :LANES]
        out[i, lines + deep :] = gram[:, LANES:]


def means_kernel(got, mean_ref, out):
    z, core = lax.axis_index(Z), lax.axis_index(CORE)
    n = got.shape[0]
    lines = mean_ref.shape[0]
    total = lines * LANES * n
    even, odd = got[0], got[1]
    for i in range(2, n, 2):
        even, odd = even + got[i], odd + got[i + 1]
    sums = even + odd
    means = sums[:lines] / total
    mean_ref[...] = means
    own = mean_ref[pl.ds((core * lax.axis_size(Z) + z) // 2, 1), :]
    band = jnp.broadcast_to(jnp.sum(means, keepdims=True), (1, LANES))
    fill = jnp.zeros((lines - 2, LANES), F32)
    deep = (got.shape[1] - lines) // 2
    pieces = [own, band, fill]
    for at in (lines, lines + deep):
        pieces += [even[at : at + deep], odd[at : at + deep]]
    whole = jnp.concatenate(pieces, axis=0)
    for i in range(out.shape[0]):
        out[i] = whole


def centred_kernel(own, kern, mean_ref, got, hb, aff, partial, *more):
    z, core = lax.axis_index(Z), lax.axis_index(CORE)
    n = got.shape[0]
    total = mean_ref.shape[0] * LANES * n
    which = core if own else 1 - core
    grand = got[0, 1:2, :]
    for i in range(1, n):
        grand = grand + got[i, 1:2, :]
    grand = grand / total
    lane = lax.broadcasted_iota(jnp.int32, (1, LANES), 1)
    odd = lax.rem(z, 2) == 1
    places = []
    for i in range(0, n, 2):
        pair = []
        for j in range(2):
            line = got[i + j, 0:1, :]
            swapped = pltpu.roll(line, LANES // 2, 1)
            pair.append(jnp.where(odd if j == 0 else jnp.logical_not(odd), swapped, line))
        places.append(jnp.where(lane < LANES // 2, pair[0], pair[1]))
    lines = mean_ref.shape[0] // 2
    for i in range(lines):
        line = mean_ref[pl.ds(which * lines + i, 1), :]
        mine = jnp.broadcast_to(line, (LANES, LANES)).T
        at = slice(i * LANES, (i + 1) * LANES)
        for g, place in enumerate(places):
            values = kern[at, g * LANES : (g + 1) * LANES]
            values = values - mine - place + grand
            aff[at, g * LANES : (g + 1) * LANES] = values.astype(BF16)
    partial[...] = jnp.dot(aff[...], hb[...], preferred_element_type=F32)
    if more:
        hh_ref, scales = more
        deep = (got.shape[1] - 8) // 2
        for i in range(n):
            hh_ref[i * deep : (i + 1) * deep, :LANES] = got[i, 8 : 8 + deep, :]
            hh_ref[i * deep : (i + 1) * deep, LANES:] = got[i, 8 + deep :, :]
        hh = hh_ref[...]
        line = lax.broadcasted_iota(jnp.int32, hh.shape, 0)
        place = lax.broadcasted_iota(jnp.int32, hh.shape, 1)
        norm = jnp.sum(jnp.where(line == place, hh, 0.0), axis=0, keepdims=True)
        norm = jnp.sqrt(jnp.maximum(norm, 1e-30))
        grown = norm * (1.05 + 1.05 * total * step_size(hh))
        summed = grown * jnp.max(grown, axis=1, keepdims=True)
        for i, (value, top) in enumerate(((norm, 512.0), (grown, 512.0), (summed, 32768.0))):
            scales[2 * i : 2 * i + 1, :] = top / value
            scales[2 * i + 1 : 2 * i + 2, :] = value / top


def step_size(hh):
    square = jnp.sum(jnp.sum(hh * hh, axis=0, keepdims=True), axis=1, keepdims=True)
    return 0.5 / jnp.sqrt(square + 1e-06)


def gram_kernel(hb, part_ref, gram_ref):
    gram_ref[...] = lax.dot_general(
        hb[...], hb[...], (((0,), (0,)), ((), ())), preferred_element_type=F32
    )
    part = part_ref.shape[0]
    at = pl.multiple_of(lax.axis_index(COL) * part, part)
    part_ref[...] = gram_ref[pl.ds(at, part), :]


def start_kernel(unit, points, factor, first, second, copies, wide, done):
    half, width = first.shape[0], points.shape[1]
    fetches = [
        pltpu.make_async_copy(points, copies.at[0], done.at[0]),
        pltpu.make_async_copy(factor, wide, done.at[1]),
    ]
    for fetch in fetches:
        fetch.start()
    for fetch in fetches:
        fetch.wait()
    value = copies[0]
    hb = (wide[...] * unit).astype(BF16)
    first[:, :width] = value[:half]
    first[:, width:] = hb[:half]
    second[:, :width] = value[half:]
    second[:, width:] = hb[half:]
    for i in range(1, copies.shape[0]):
        copies[i] = value


def step_kernel(before, after, ah_ref, hh_ref, h_ref, out, *copies):
    hh = hh_ref[...]
    h = h_ref[...] * before if before else h_ref[...]
    scale = step_size(hh)
    product = jnp.dot(h, hh, precision=lax.Precision.HIGHEST, preferred_element_type=F32)
    h = jnp.maximum(h - scale * (product - ah_ref[...]), 0.0)
    out[...] = h / after if after else h
    if copies:
        hb = h.astype(BF16)
        for i in range(copies[0].shape[0]):
            copies[0][i] = hb


def shards(points, factor):
    nz, ncore, ny, nx = (lax.axis_size(a) for a in ROW_COL)
    nrow, ncol = nz * ncore, ny * nx
    pts, rank = factor.shape
    total = pts * nrow * ncol
    unit = 2.0 / math.sqrt(total * rank)
    width = points.shape[1]
    half = pts // 2
    shape = jax.ShapeDtypeStruct

    first, second, copies = call(
        functools.partial(start_kernel, unit),
        [*[shape((half, width + rank), BF16)] * 2, shape((nz, pts, width), BF16)],
        [points, factor],
        1,
        [pltpu.VMEM((pts, rank), F32), pltpu.SemaphoreType.DMA((2,))],
        vmem=60,
        place=pl.ANY,
    )
    tie = lax.optimization_barrier
    along_z = lax.all_to_all(copies, Z, 0, 0, tiled=True)
    x1, x3 = from_ahead(first, X, 1), from_ahead(first, X, -1)
    y1, y3 = from_ahead(second, Y, 1), from_ahead(second, Y, -1)
    x2, y2 = from_ahead(first, X, 2), from_ahead(second, Y, 2)
    x1, x2, x3, y1, y2, y3 = tie((x1, x2, x3, y1, y2, y3))
    by_x = jnp.stack([first, x1, x2, x3])
    by_y = jnp.stack([second, y1, y2, y3])
    by_x, by_y = tie((by_x, by_y))
    y_one, x_one = from_ahead(by_x, Y, 1), from_ahead(by_y, X, 1)
    y_two, x_two = from_ahead(by_x, Y, 2), from_ahead(by_y, X, 2)
    y_three = from_ahead(by_x, Y, 3)
    by_y, x_two = tie((by_y, x_two))
    x_three = from_ahead(by_y, X, 3)
    far = [x_three, y_three, x_one, y_one, x_two, y_two]
    far, along_z = tie((far, along_z.reshape(-1, width)))
    other = from_ahead(along_z, CORE, 1)
    cols = [*far, first, x1, x2, x3, second, y1, y2, y3]

    part = rank // ncol
    group = nrow * pts
    col_pts, hb_cols, col_sq, own_part = call(
        columns_kernel,
        [
            shape((group, width), BF16),
            shape((group, rank), BF16),
            shape((group // LANES, LANES), F32),
            shape((part, rank), F32),
        ],
        cols,
        2 * group * rank * rank,
        [pltpu.VMEM((rank, rank), F32)],
    )
    more_part = from_ahead(own_part, CORE, 1)
    lines = group // LANES
    own_kern, own_sums = call(
        rows_kernel,
        [shape((group // 2, group), F32), shape((lines // 2, LANES), F32)],
        [along_z, col_pts, col_sq],
        group * group * width,
    )
    other_kern, message = call(
        last_rows_kernel,
        [shape((group // 2, group), F32), shape((nrow, lines + part, LANES), F32)],
        [other, col_pts, col_sq, own_sums, own_part, more_part],
        group * group * width,
        [pltpu.VMEM((lines // 2, LANES), F32)],
    )
    mean_rows, message = call(
        means_kernel,
        [shape((lines, LANES), F32), shape((ncol, 8 + 2 * part, LANES), F32)],
        [lax.all_to_all(message, ROW, 0, 0, tiled=True)],
        1,
    )
    gathered = lax.all_to_all(message, COL, 0, 0, tiled=True)

    def centred(own):
        outs = [shape((group // 2, group), BF16), shape((group // 2, rank), F32)]
        if own:
            outs += [shape((rank, rank), F32), shape((8, rank), F32)]
        return call(
            functools.partial(centred_kernel, own),
            outs,
            [own_kern if own else other_kern, mean_rows, gathered, hb_cols],
            group * group * rank,
        )

    aff_other, partial_other = centred(False)
    got = from_ahead(partial_other, CORE, 1)
    aff_own, partial_own, hh, scales = centred(True)

    def over_z(mine):
        mine = lax.all_to_all(mine.astype(jnp.float16), Z, 0, 0, tiled=True)
        return jnp.sum(mine.astype(F32), axis=0)

    def stepped(before, after, ah, hh, h, copies):
        outs = [shape((pts, rank), F32)] + [shape((ncol, pts, rank), BF16)] * copies
        flops = 12 * pts * rank * rank
        return call(functools.partial(step_kernel, before, after), outs, [ah, hh, h], flops)

    mine = (partial_own + got) * scales[0]
    ah = over_z(mine.reshape(nz, pts, rank)) * scales[1]
    h, hb_cols = stepped(unit, None, ah, hh, factor, 1)

    hb_cols = lax.all_to_all(hb_cols, COL, 0, 0, tiled=True).reshape(group, rank)
    partial_other = jnp.dot(aff_other, hb_cols, preferred_element_type=F32)
    got = from_ahead(partial_other, CORE, 1)
    (own_part,) = call(
        gram_kernel,
        [shape((part, rank), F32)],
        [hb_cols],
        2 * group * rank * rank,
        [pltpu.VMEM((rank, rank), F32)],
    )
    more_part = from_ahead(own_part, CORE, 1)
    partial_own = jnp.dot(aff_own, hb_cols, preferred_element_type=F32)
    mine = ((partial_own + got) * scales[2]).reshape(nz, pts, rank)
    extra = jnp.broadcast_to((own_part + more_part) * scales[4], (nz, part, rank))
    own = over_z(jnp.concatenate([mine, extra], axis=1))
    ah, own_part = tie((own[:pts] * scales[3], own[pts:] * scales[5]))
    hh = sent_to_all(own_part, COL).reshape(rank, rank)
    return stepped(None, unit, ah, hh, h, 0)[0]


def solution(mesh):
    split = Mesh(mesh.devices.reshape(8, 2, 4, 4), ROW_COL)
    return jax.shard_map(
        shards,
        mesh=split,
        in_specs=(P(ROW_COL, None), P(ROW_COL, None)),
        out_specs=P(ROW_COL, None),
        check_vma=False,
    )
```
